32 devices in a mesh: chan: 8 (over z, x), hour: 4 (over y, core).
Axes of the slice: x: 2, y: 2, z: 4, core: 2. Of those that a mesh axis runs over, the one named last changes fastest.
Arguments:
- traces: bfloat16 [1024, 16384], P('chan', 'hour'), may hold values from -6 to 6
- taps: bfloat16 [1024, 512], P('chan'), may hold values from -0.25 to 0.25
- bin_ids: int32 [4, 8], P(None, 'chan'), may hold values from 0 to 31
- owners: int32 [32], replicated, may hold values from 0 to 31, each once
Outputs:
- stacks: float32 [32, 8192], P(('chan', 'hour'))
The draws below stay inside these ranges and needn't reach their ends.
Inputs may be any that keep to these rules, and one draw needn't show every extreme that they name: bin_ids[r, i] is the distance bin of the pair of block i - r - 1 with block i; entries with i <= r name no pair and are not read. owners is a permutation: bin b is held in row owners[b] of stacks.
All inputs are finite; a program needn't handle non-finite values.
Results may differ from the reference program's by a relative error of at most 0.004.
Values may be sent and summed in bfloat16 or wider, within the bound.
A program may use at most 256 MiB of HBM per device.

```python
import math
import jax
import jax.numpy as jnp
from jax import lax

CB = 128
FR = 4096
TAPS = 512
FRAMES = 1
ROUNDS = 4
BLOCKS = 8
NCH = 1024
TIME = 16384
NBINS = 32
N_CHAN = 8
N_HOUR = 4


def with_ends(array, key, least, top_value):
    dims = array.shape
    place = [jax.random.randint(jax.random.fold_in(key, axis), (), 0, dims[axis]) for axis in range(len(dims))]
    array = array.at[tuple(place)].set(least)
    longest = dims.index(max(dims))
    place[longest] = (place[longest] + 1) % dims[longest]
    return array.at[tuple(place)].set(top_value)


def level_of(key, extent, shards, low, largest):
    loudness, own = 1.0, jax.random.fold_in(key, 6)
    for dim, shards_of in shards:
        steps = jnp.exp(jax.random.uniform(jax.random.fold_in(own, dim), (shards_of,), jnp.float32, low / len(shards), largest / len(shards)))
        loudness = loudness * jnp.repeat(steps, extent[dim] // shards_of).reshape([-1 if axis == dim else 1 for axis in range(len(extent))])
    return loudness


def bell_draw(key, extent, deviation, most, cuts=(), kind=jnp.bfloat16):
    entries = jax.random.normal(key, extent, jnp.float32) * deviation
    if len(cuts) > 0:
        entries = level_of(key, extent, cuts, -0.22, 0.18) * entries
    return jnp.clip(entries, min=-most, max=most).astype(kind)


def setup_inputs(seed: int = 0) -> dict:
    splits = jax.random.split(jax.random.key(seed), 5)
    return {
        "traces": bell_draw(splits[0], (NCH, TIME), 1.0, 6.0, ((0, 8), (1, 4))),
        "taps": bell_draw(splits[1], (NCH, TAPS), TAPS ** -0.5, 0.25, ((0, 8),)),
        "bin_ids": with_ends(jax.random.randint(splits[2], (ROUNDS, BLOCKS), 0, NBINS), jax.random.fold_in(splits[2], 1), 0, NBINS - 1).astype(jnp.int32),
        "owners": jax.random.permutation(splits[3], NBINS).astype(jnp.int32),
    }


def spectra(block, filters):
    signal = block.astype(jnp.float32).reshape(CB, N_HOUR * FRAMES, FR)
    freq = jnp.fft.rfft(signal, n=2 * FR, axis=-1)[..., :FR]
    response = jnp.fft.rfft(filters.astype(jnp.float32), n=2 * FR, axis=-1)[:, :FR]
    product = freq * response[:, None, :]
    return (jnp.real(product).astype(jnp.bfloat16), jnp.imag(product).astype(jnp.bfloat16))

def reference(traces, taps, bin_ids, owners):
    blocks = traces.reshape(N_CHAN, CB, N_HOUR * FRAMES * FR)
    filter_blocks = taps.reshape(N_CHAN, CB, TAPS)

    def pair_terms(block_index):
        own_re, own_im = spectra(blocks[block_index], filter_blocks[block_index])
        near_re = own_re.astype(jnp.float32)
        near_im = own_im.astype(jnp.float32)
        results = []
        for offset in range(ROUNDS):
            other = jnp.maximum(block_index - offset - 1, 0)
            far_re, far_im = spectra(blocks[other], filter_blocks[other])
            far_re = far_re.astype(jnp.float32)
            far_im = far_im.astype(jnp.float32)
            cross_re = lax.optimization_barrier(jnp.sum(far_re * near_re + far_im * near_im, axis=(0, 1)))
            cross_im = lax.optimization_barrier(jnp.sum(far_im * near_re - far_re * near_im, axis=(0, 1)))
            live = block_index >= offset + 1
            results.append(jnp.where(live, jnp.stack([cross_re, cross_im]), 0.0))
        return jnp.stack(results)
    cross = lax.map(pair_terms, jnp.arange(N_CHAN, dtype=jnp.int32))
    valid = jnp.arange(N_CHAN, dtype=jnp.int32)[:, None] >= jnp.arange(1, ROUNDS + 1, dtype=jnp.int32)[None, :]
    labels = jnp.where(valid, bin_ids.T, NBINS).reshape(-1).astype(jnp.int32)
    stack = jax.ops.segment_sum(cross.reshape(N_CHAN * ROUNDS, 2, FR), labels, num_segments=NBINS + 1)[:NBINS]
    placed = jnp.zeros_like(stack).at[owners].set(stack)
    spectrum = placed[:, 0] + 1j * placed[:, 1]
    padded = jnp.concatenate([spectrum, jnp.zeros((NBINS, 1), spectrum.dtype)], axis=1)
    scale = 1.0 / (FR * math.sqrt(FR * N_HOUR * FRAMES * CB))
    return (jnp.fft.irfft(padded, n=2 * FR, axis=-1) * (2 * FR * scale)).astype(jnp.float32)
```

```python
import functools
import math

import jax
import jax.numpy as jnp
import numpy as np
from jax import lax
from jax.experimental import pallas as pl
from jax.experimental.pallas import tpu as pltpu
from jax.sharding import PartitionSpec as P

FR = 4096
ROUNDS = 4
MESH = pl.DeviceIdType.MESH


exact = lax.Precision.HIGHEST

def passed_along(shard, axis, by):
    devices = lax.axis_size(axis)
    pairs = [(i, i + by) for i in range(devices) if 0 <= i + by < devices]
    return lax.ppermute(shard, axis, pairs)


def transform(real_part, imag_part, count):
    span = real_part.shape[-1]
    inner = 2 * span // 128
    lead = real_part.shape[:-1]
    first = jnp.arange(64, dtype=jnp.float32)[:, None]
    middle = jnp.arange(128, dtype=jnp.float32)[None, :]
    angle_one = 2.0 * math.pi / 128.0 * jnp.mod(first * middle, 128.0)
    cos_one = jnp.cos(angle_one)
    sin_one = -jnp.sin(angle_one)
    second = jnp.arange(inner, dtype=jnp.float32)[:, None]
    angle_turn = 2.0 * math.pi / (128.0 * inner) * jnp.mod(second * middle, 128.0 * inner)
    cos_turn = jnp.cos(angle_turn)
    sin_turn = -jnp.sin(angle_turn)
    outer = jnp.arange(count // 128, dtype=jnp.float32)[None, :]
    angle_two = 2.0 * math.pi / inner * jnp.mod(second * outer, float(inner))
    cos_two = jnp.cos(angle_two)
    sin_two = -jnp.sin(angle_two)
    grid = real_part.reshape(lead + (64, inner))
    section_re = jnp.einsum("...an,ak->...nk", grid, cos_one, precision=exact)
    section_im = jnp.einsum("...an,ak->...nk", grid, sin_one, precision=exact)
    if imag_part is not None:
        grid_im = imag_part.reshape(lead + (64, inner))
        section_re = section_re - jnp.einsum("...an,ak->...nk", grid_im, sin_one, precision=exact)
        section_im = section_im + jnp.einsum("...an,ak->...nk", grid_im, cos_one, precision=exact)
    turned_re = section_re * cos_turn - section_im * sin_turn
    turned_im = section_re * sin_turn + section_im * cos_turn
    out_re = jnp.einsum("...nk,nm->...mk", turned_re, cos_two, precision=exact) - jnp.einsum(
        "...nk,nm->...mk", turned_im, sin_two, precision=exact
    )
    out_im = jnp.einsum("...nk,nm->...mk", turned_re, sin_two, precision=exact) + jnp.einsum(
        "...nk,nm->...mk", turned_im, cos_two, precision=exact
    )
    return (out_re.reshape(lead + (count,)), out_im.reshape(lead + (count,)))


def filtered(samples, filters):
    channels = samples.shape[0]
    frames = samples.shape[1] // FR
    signal = samples.astype(jnp.float32).reshape(channels, frames, FR)
    freq_re, freq_im = transform(signal, None, FR)
    padded_taps = jnp.pad(filters.astype(jnp.float32), ((0, 0), (0, FR - filters.shape[1])))
    resp_re, resp_im = transform(padded_taps, None, FR)
    resp_re = resp_re[:, None, :]
    resp_im = resp_im[:, None, :]
    spec_re = (freq_re * resp_re - freq_im * resp_im).astype(jnp.bfloat16)
    spec_im = (freq_re * resp_im + freq_im * resp_re).astype(jnp.bfloat16)
    return (spec_re, spec_im)


def body(traces, taps, bin_ids, owners):
    channels = traces.shape[0]
    frames = traces.shape[1] // FR
    spec_re, spec_im = filtered(traces, taps)
    mine = lax.axis_index("chan")
    near_re = spec_re.astype(jnp.float32)
    near_im = spec_im.astype(jnp.float32)
    results = []
    for offset in range(ROUNDS):
        far_re, far_im = passed_along((spec_re, spec_im), "chan", offset + 1)
        far_re = far_re.astype(jnp.float32)
        far_im = far_im.astype(jnp.float32)
        cross_re = jnp.sum(far_re * near_re + far_im * near_im, axis=(0, 1))
        cross_im = jnp.sum(far_im * near_re - far_re * near_im, axis=(0, 1))
        results.append(jnp.stack([cross_re, cross_im]))
    contrib = jnp.stack(results)
    nbins = owners.shape[0]
    own_bins = bin_ids[:, 0]
    labels = jnp.arange(nbins, dtype=jnp.int32)
    places = jnp.sum(jnp.where(own_bins[:, None] == labels[None, :], owners[None, :], 0), axis=1)
    valid = jnp.arange(ROUNDS, dtype=jnp.int32) < mine
    places = jnp.where(valid, places, -1)
    width = contrib.shape[2]
    flat = contrib.reshape(ROUNDS, 2 * width)
    per_device = nbins // lax.axis_size("chan")
    rows = jnp.arange(lax.axis_size("chan") * per_device, dtype=jnp.int32)
    onehot = (places[None, :] == rows[:, None]).astype(jnp.float32)
    stacked = lax.psum_scatter(
        jnp.dot(onehot, flat, precision=exact, preferred_element_type=jnp.float32),
        "chan",
        scatter_dimension=0,
        tiled=True,
    )
    stacked = stacked.reshape(per_device, 2, width)
    final = lax.psum_scatter(stacked, "hour", scatter_dimension=0, tiled=True)
    weights = jnp.where(jnp.arange(FR) == 0, 1.0, 2.0).astype(jnp.float32)
    wave_re, wave_im = transform(final[:, 0] * weights, -final[:, 1] * weights, 2 * FR)
    norm = 1.0 / (FR * math.sqrt(FR * lax.axis_size("hour") * frames * channels))
    return wave_re * norm

SPLIT = 8
SUB = FR // SPLIT
LANES = 128
TILES = SUB // LANES


def sub_tables():
    a = np.arange(SUB)[:, None]
    k1 = np.arange(SUB)[None, :]
    turn = 2.0 * np.pi * ((a * k1) % (2 * SUB)) / (2 * SUB)
    cos, sin = np.cos(turn), -np.sin(turn)
    sin[:, 0] = 1.0 - 2.0 * (np.arange(SUB) % 2)
    table = np.stack([cos.reshape(SUB, TILES, LANES), sin.reshape(SUB, TILES, LANES)], axis=2)
    return table.reshape(SUB, 2 * SUB)


def two_parts(table):
    high = table.astype(jnp.bfloat16)
    low = (table - high.astype(np.float64)).astype(jnp.bfloat16)
    return high, low


def pick_table():
    span = SPLIT * LANES
    table = np.zeros((span, span), np.float32)
    for n in range(SPLIT):
        for b in range(LANES):
            table[SPLIT * b + n, n * LANES + b] = 1.0
    return table.astype(jnp.bfloat16)


def turn_table():
    n = np.arange(SPLIT)[:, None]
    k1 = np.arange(SUB)[None, :]
    turn = 2.0 * np.pi * n * k1 / (2 * FR)
    table = np.stack([np.cos(turn), -np.sin(turn)], axis=1).reshape(SPLIT, 2, TILES, 1, LANES)
    table = np.broadcast_to(table.transpose(2, 0, 1, 3, 4), (TILES, SPLIT, 2, 8, LANES))
    return np.ascontiguousarray(table).astype(np.float32)


def times(value, angle):
    re, im = value
    c, s = math.cos(angle), math.sin(angle)
    if abs(s) < 1e-12:
        return (re, im) if c > 0 else (-re, -im)
    if abs(c) < 1e-12:
        return (-im, re) if s > 0 else (im, -re)
    if abs(abs(c) - abs(s)) < 1e-12:
        root = abs(c)
        p, q = math.copysign(1.0, c), math.copysign(1.0, s)
        first = (re if p > 0 else -re) + (-im if q > 0 else im)
        second = (re if q > 0 else -re) + (im if p > 0 else -im)
        return first * root, second * root
    return re * c - im * s, re * s + im * c


def small_dft(values, sign, half=False):
    size = len(values)
    if size == 1:
        return values
    even = small_dft(values[0::2], sign)
    odd = small_dft(values[1::2], sign)
    low, high = [], []
    for k in range(size // 2):
        turned = times(odd[k], sign * 2.0 * math.pi * k / size)
        low.append((even[k][0] + turned[0], even[k][1] + turned[1]))
        if not half:
            high.append((even[k][0] - turned[0], even[k][1] - turned[1]))
    return low + high


LATE = 8
SLOTS = 32


def slot_of(step, before, chan):
    if isinstance(step, int) and step == chan - 1:
        return before
    return LATE + step * (step - 1) // 2 + before


def rows_of_pairs(ids, owners):
    depth = ids.shape[1]
    nbins = owners.shape[1]
    bins = lax.broadcasted_iota(jnp.int32, (nbins, depth), 0) + 1
    picked = (bins == ids[0:1, :]).astype(jnp.float32).astype(jnp.bfloat16)
    row = lax.broadcasted_iota(jnp.int32, (nbins, nbins), 0)
    moved = (row == owners[...]).astype(jnp.float32).astype(jnp.bfloat16)
    return jnp.dot(moved, picked, preferred_element_type=jnp.float32).astype(jnp.bfloat16)


def fold(values):
    sublane = lax.broadcasted_iota(jnp.int32, values[0].shape, 0)
    shift = 1
    while len(values) > 1:
        first = lax.rem(lax.div(sublane, shift), 2) == 0
        values = [
            jnp.where(first, a, b) + pltpu.roll(jnp.where(first, b, a), SPLIT - shift, 0)
            for a, b in zip(values[0::2], values[1::2])
        ]
        shift *= 2
    return values[0]


OUT_ROWS = 2 * FR // LANES
TERMS = 2 * SPLIT * (TILES + 1)


def column_table():
    v = np.arange(LANES)[:, None]
    t, k2 = np.arange(TILES)[None, :, None], np.arange(SPLIT)[None, None, :]
    main = 2.0 * np.pi * ((v[:, :, None] * (SPLIT * k2 + t)) % OUT_ROWS) / OUT_ROWS
    extra = 2.0 * np.pi * ((v * (SPLIT // 2 + SPLIT * (np.arange(SPLIT)[None, :] - SPLIT // 2))) % OUT_ROWS) / OUT_ROWS
    phase = np.concatenate([main, extra[:, None, :]], axis=1)
    top = np.stack([np.cos(phase), -np.sin(phase)], axis=2).reshape(LANES, TERMS)
    under = np.stack([np.sin(phase), np.cos(phase)], axis=2).reshape(LANES, TERMS)
    high, low = two_parts(np.concatenate([top, under], axis=0))
    rest = np.zeros((2 * LANES, 2 * LANES - 3 * TERMS), jnp.bfloat16)
    return np.concatenate([high, high, low, rest], axis=1)


def twist_table():
    turn = 2.0 * np.pi * np.arange(LANES)[:, None] * np.arange(LANES)[None, :] / (2 * FR)
    return np.stack([np.cos(turn), np.sin(turn)]).astype(np.float32)


def row_table():
    turn = 2.0 * np.pi * ((np.arange(OUT_ROWS)[:, None] * np.arange(LANES)[None, :]) % OUT_ROWS) / OUT_ROWS
    high, low = two_parts(np.concatenate([np.cos(turn), -np.sin(turn)], axis=1))
    return np.concatenate([high, high, low], axis=1)


def halves(value):
    top = value.astype(jnp.bfloat16)
    return top, (value - top.astype(jnp.float32)).astype(jnp.bfloat16)


def over_lanes(a, b):
    return lax.dot_general(a, b, (((1,), (1,)), ((), ())), preferred_element_type=jnp.float32)


def inverse(rows, column, twist, across, norm):
    lane = lax.broadcasted_iota(jnp.int32, rows.shape, 1)
    slot = lax.broadcasted_iota(jnp.int32, rows.shape, 0)
    rows = rows * jnp.where((lane == 0) & (slot == 0), norm, 2.0 * norm)
    apart = (lane == 0) & (slot < 2 * SPLIT) & (lax.rem(slot, SPLIT) >= SPLIT // 2)
    every = jnp.concatenate(
        [jnp.where(apart, 0.0, rows), jnp.where(apart, rows, 0.0)[: 2 * SPLIT]], axis=0
    )
    top, rest = halves(every)
    nothing = jnp.zeros((2 * LANES - 3 * TERMS, LANES), jnp.bfloat16)
    z = jnp.dot(
        column[...], jnp.concatenate([top, rest, top, nothing], axis=0), preferred_element_type=jnp.float32
    )
    z_re, z_im = z[:LANES], z[LANES:]
    c, s = twist[0], twist[1]
    y = jnp.concatenate([z_re * c - z_im * s, z_re * s + z_im * c], axis=1)
    top, rest = halves(y)
    return over_lanes(across[...], jnp.concatenate([top, rest, top], axis=1))


def kernel(chan, hour, norm, x, taps, bin_ids, owners, *refs):
    tables, out = refs[:7], refs[7]
    held = refs[8:15]
    pick, high, low, turns, column, twist = held[:6]
    across = held[6]
    xin, tin, ids, ids_in, xd, td, fx, fh, spec, kron, part, first, early, outbox, inbox = refs[15:30]
    table_sem, own_sem, ids_send, ids_recv, t_send, t_recv, x_send, x_recv = refs[30:38]
    f_send, f_recv, send, recv, send2, recv2 = refs[38:]
    me, my_hour = lax.axis_index("chan"), lax.axis_index("hour")
    per = xin.shape[1]
    span = SPLIT * LANES
    share = pl.ds(pl.multiple_of(my_hour * (tin.shape[2] // hour), LANES), tin.shape[2] // hour)

    def flipped(at, o, size):
        to, bit = at, 1
        while bit < size:
            to = to + lax.rem(lax.div(o, bit), 2) * bit * (1 - 2 * lax.rem(lax.div(at, bit), 2))
            bit *= 2
        return to

    def partner(o):
        return flipped(me, o, chan)

    def beside(o):
        return flipped(my_hour, o, hour)

    def sent(src, dst, sends, recvs, **device):
        return pltpu.make_async_remote_copy(
            src_ref=src, dst_ref=dst, send_sem=sends, recv_sem=recvs, device_id=device, device_id_type=MESH
        )

    loads = [pltpu.make_async_copy(src, dst, table_sem.at[z]) for z, (src, dst) in enumerate(zip(tables, held))]
    own = [
        pltpu.make_async_copy(x.at[me], xin.at[me], own_sem.at[0]),
        pltpu.make_async_copy(taps.at[me, :, share], tin.at[me, :, share], own_sem.at[1]),
    ]
    for copy in own + loads:
        copy.start()
    barrier = pltpu.get_barrier_semaphore()
    for o in range(1, hour):
        pl.semaphore_signal(
            barrier, inc=1, device_id={"hour": lax.rem(my_hour + o, hour)}, device_id_type=MESH
        )
    for o in range(1, chan):
        pl.semaphore_signal(barrier, inc=1, device_id={"chan": partner(o)}, device_id_type=MESH)
    place = lax.broadcasted_iota(jnp.int32, ids.shape, 1)
    labels = jnp.zeros(ids.shape, jnp.int32)
    for r in range(ROUNDS):
        live = (place == me * ROUNDS + r) & (me >= r + 1)
        labels = jnp.where(live, bin_ids[:, r : r + 1] + 1, labels)
    ids[...] = labels
    pl.semaphore_wait(barrier, chan + hour - 2)

    def x_copy(o):
        to = partner(o)
        return sent(x.at[to], xin.at[me], x_send.at[o], x_recv.at[o], chan=to)

    far_first = sorted(range(1, chan), key=lambda o: -(o.bit_length()))
    tap_copies, id_copies = [], []
    for o in far_first:
        to = partner(o)
        tap_copies.append(
            sent(taps.at[to, :, share], tin.at[me, :, share], t_send.at[o], t_recv.at[o], chan=to)
        )
        tap_copies[-1].start()
    for o in far_first:
        id_copies.append(sent(ids, ids_in.at[o], ids_send.at[o], ids_recv.at[o], chan=partner(o)))
        id_copies[-1].start()
    for o in range(1, chan):
        x_copy(o).start()
    own[1].wait()
    for copy in tap_copies:
        copy.wait_recv()
    forwards = []
    for o in range(1, hour):
        to = lax.rem(my_hour + o, hour)
        forwards.append(sent(tin.at[:, :, share], tin.at[:, :, share], f_send.at[o], f_recv.at[o], hour=to))
        forwards[-1].start()
    for copy in loads + own[:1]:
        copy.wait()

    lane0 = lax.broadcasted_iota(jnp.int32, (8, LANES), 1) == 0

    def spectra(block, t, edge):
        @pl.loop(0, per // 8)
        def _(g):
            piece = pl.ds(pl.multiple_of(8 * g, 8), 8)
            here = pl.ds(pl.multiple_of(block * per + 8 * g, 8), 8)

            def bins_of(f, rows):
                values, extra = [], []
                for n in range(SPLIT):
                    re = f[n, rows, pl.ds(pl.multiple_of(2 * t * LANES, LANES), LANES)]
                    im = f[n, rows, pl.ds(pl.multiple_of((2 * t + 1) * LANES, LANES), LANES)]
                    if edge:
                        angle = -math.pi * n / SPLIT
                        extra.append((im * math.cos(angle), im * math.sin(angle)))
                        im = jnp.where(lane0, 0.0, im)
                    if n == 0:
                        values.append((re, im))
                    else:
                        c, s = turns[t, n, 0], turns[t, n, 1]
                        values.append((re * c - im * s, re * s + im * c))
                found = small_dft(values, -1)
                if edge:
                    more = small_dft(extra, -1, half=True)
                    for k2 in range(SPLIT // 2):
                        old = found[SPLIT // 2 + k2]
                        found[SPLIT // 2 + k2] = tuple(
                            jnp.where(lane0, more[k2][z], old[z]) for z in range(2)
                        )
                return found

            freq = bins_of(fx, piece)
            resp = bins_of(fh, here)
            for k2 in range(SPLIT):
                (xr, xi), (hr, hi) = freq[k2], resp[k2]
                spec[t, k2, 0, here, :] = (xr * hr - xi * hi).astype(jnp.bfloat16).astype(jnp.float32)
                spec[t, k2, 1, here, :] = (xr * hi + xi * hr).astype(jnp.bfloat16).astype(jnp.float32)

    def take(block):
        flat = jnp.concatenate([xin[block, :, q * span : (q + 1) * span] for q in range(FR // span)], axis=0)
        got = jnp.dot(flat, pick[...], preferred_element_type=jnp.float32).astype(jnp.bfloat16)
        for q in range(FR // span):
            for n in range(SPLIT):
                xd[n * per : (n + 1) * per, q * LANES : (q + 1) * LANES] = got[
                    q * per : (q + 1) * per, n * LANES : (n + 1) * LANES
                ]
        found = jnp.dot(xd[...], high[...], preferred_element_type=jnp.float32) + jnp.dot(
            xd[...], low[...], preferred_element_type=jnp.float32
        )
        for n in range(SPLIT):
            fx[n] = found[n * per : (n + 1) * per]
        spectra(block, 0, True)

        @pl.loop(1, TILES)
        def _(t):
            spectra(block, t, False)

    for copy in forwards:
        copy.wait_recv()
    count = tin.shape[2]
    got = jnp.dot(
        tin[...].reshape(chan * per, count), pick[:count, :], preferred_element_type=jnp.float32
    ).astype(jnp.bfloat16)
    for n in range(SPLIT):
        td[n] = got[:, n * LANES : (n + 1) * LANES]

    @pl.loop(0, SPLIT)
    def _(n):
        fh[n] = jnp.dot(td[n], high[:LANES, :], preferred_element_type=jnp.float32) + jnp.dot(
            td[n], low[:LANES, :], preferred_element_type=jnp.float32
        )

    for copy in id_copies:
        copy.wait_recv()
    labels = ids[...]
    for o in range(1, chan):
        labels = labels + ids_in[o]
    by_pair = rows_of_pairs(labels, owners)
    nbins = chan * hour
    pair = lax.broadcasted_iota(jnp.int32, (ids.shape[1], SLOTS), 0)
    column_of = lax.broadcasted_iota(jnp.int32, (ids.shape[1], SLOTS), 1)
    places = jnp.zeros(pair.shape, jnp.float32)
    for s in range(1, chan):
        for j in range(s):
            near, far = jnp.maximum(partner(s), partner(j)), jnp.minimum(partner(s), partner(j))
            held_by = jnp.where(near - far <= ROUNDS, near * ROUNDS + near - far - 1, -1)
            hit = (column_of == slot_of(s, j, chan)) & (pair == held_by)
            places = jnp.where(hit, 1.0, places)
    by_slot = jnp.dot(by_pair, places.astype(jnp.bfloat16), preferred_element_type=jnp.float32).astype(jnp.bfloat16)
    deep = 2 * SPLIT
    spread = (
        lax.div(lax.broadcasted_iota(jnp.int32, (nbins * deep, nbins), 0), deep)
        == lax.broadcasted_iota(jnp.int32, (nbins * deep, nbins), 1)
    ).astype(jnp.float32).astype(jnp.bfloat16)
    widen = (
        lax.div(lax.broadcasted_iota(jnp.int32, (SLOTS, SLOTS * deep), 1), deep)
        == lax.broadcasted_iota(jnp.int32, (SLOTS, SLOTS * deep), 0)
    ).astype(jnp.float32).astype(jnp.bfloat16)
    tall = jnp.dot(spread, by_slot, preferred_element_type=jnp.float32).astype(jnp.bfloat16)
    both = jnp.dot(tall, widen, preferred_element_type=jnp.float32)
    same = lax.rem(lax.broadcasted_iota(jnp.int32, both.shape, 0), deep) == lax.rem(
        lax.broadcasted_iota(jnp.int32, both.shape, 1), deep
    )
    kron[...] = jnp.where(same, both, 0.0).astype(jnp.bfloat16)

    def cross(t, near, far, slot):
        res, ims = [], []
        for k2 in range(SPLIT):
            re = im = None
            for c in range(per // 8):
                at = pl.ds(pl.multiple_of(near * per + 8 * c, 8), 8)
                of = pl.ds(pl.multiple_of(far * per + 8 * c, 8), 8)
                nr, ni = spec[t, k2, 0, at, :], spec[t, k2, 1, at, :]
                fr, fi = spec[t, k2, 0, of, :], spec[t, k2, 1, of, :]
                one, two = fr * nr + fi * ni, fi * nr - fr * ni
                re, im = (one, two) if re is None else (re + one, im + two)
            res.append(re)
            ims.append(im)
        part[t, slot] = jnp.concatenate([fold(res), fold(ims)], axis=0).astype(jnp.bfloat16)

    def crosses(s, begin, t):
        @pl.loop(0, s)
        def _(j):
            a, b = partner(s), partner(j)
            cross(t, jnp.maximum(a, b), jnp.minimum(a, b), begin + j)

    def part_copy(z, o, begin, count):
        where = pl.ds(begin, count)
        return sent(part.at[beside(o), where], first.at[o, where], send.at[z, o], recv.at[z, o], hour=beside(o))

    groups = [(LATE, 6), (LATE + 6, 4), (LATE + 10, 5), (LATE + 15, 6), (0, 7)]
    order = [2, 3, 1, 0]
    take(me)

    @pl.loop(1, chan // 2)
    def _(s):
        x_copy(s).wait_recv()
        take(partner(s))

        @pl.loop(0, TILES)
        def _(t):
            crosses(s, LATE + lax.div(s * (s - 1), 2), t)

    for o in order[:3]:
        part_copy(0, o, *groups[0]).start()

    @pl.loop(chan // 2, chan)
    def _(s):
        x_copy(s).wait_recv()
        take(partner(s))
        last = lax.div(s, chan - 1)
        begin = (LATE + lax.div(s * (s - 1), 2)) * (1 - last)

        @pl.loop(0, TILES)
        def _(z):
            crosses(s, begin, beside(lax.rem(z + 1, hour)))

        for z in range(1, len(groups)):

            @pl.when(s == z + 3)
            def _():
                for o in order[:3]:
                    part_copy(z, o, *groups[z]).start()

    def mixed(begin, count, room):
        where = slice(begin, begin + count)
        total = part[my_hour, where].astype(jnp.float32)
        for o in range(1, hour):
            total = total + first[o, where].astype(jnp.float32)
        total = total.reshape(count * deep, LANES)
        if room > count:
            total = jnp.concatenate([total, jnp.zeros(((room - count) * deep, LANES), jnp.float32)], axis=0)
        got = jnp.dot(
            kron[:, begin * deep : (begin + room) * deep],
            jnp.concatenate(halves(total), axis=1),
            preferred_element_type=jnp.float32,
        )
        return got[:, :LANES] + got[:, LANES:]

    for z in range(len(groups) - 1):
        for o in range(1, hour):
            part_copy(z, o, *groups[z]).wait_recv()
    early[...] = mixed(LATE, 21, SLOTS - LATE)
    for o in range(1, hour):
        part_copy(4, o, *groups[4]).wait_recv()
    outbox[...] = (mixed(0, 7, LATE) + early[...]).astype(jnp.bfloat16).reshape(outbox.shape)
    for oc in far_first + [0]:
        for o in order:
            if oc or o:
                to, at = partner(oc), beside(o)
                sent(
                    outbox.at[to * hour + at],
                    inbox.at[oc * hour + my_hour],
                    send2.at[oc, o],
                    recv2.at[oc, o],
                    chan=to,
                    hour=at,
                ).start()
    inbox[my_hour] = outbox[me * hour + my_hour]
    for copy in tap_copies + id_copies + forwards:
        copy.wait_send()
    for o in range(1, chan):
        x_copy(o).wait_send()
    for z in range(len(groups)):
        for o in range(1, hour):
            part_copy(z, o, *groups[z]).wait_send()

    def out_copy(oc, o):
        return sent(
            outbox.at[0], inbox.at[oc * hour + beside(o)], send2.at[oc, o], recv2.at[oc, o],
            chan=partner(oc), hour=beside(o),
        )

    for oc in range(chan):
        for o in range(hour):
            if oc or o:
                out_copy(oc, o).wait_recv()
    rows = inbox[0:hour].astype(jnp.float32)
    for oc in range(1, chan):
        rows = rows + inbox[oc * hour : (oc + 1) * hour].astype(jnp.float32)
    out[...] = inverse(rows.reshape(TILES * deep, LANES), column, twist, across, norm)
    for oc in range(chan):
        for o in range(hour):
            if oc or o:
                out_copy(oc, o).wait_send()


def split_body(traces, taps, bin_ids, owners):
    chan, hour = lax.axis_size("chan"), lax.axis_size("hour")
    channels, count = taps.shape
    per = channels // chan
    norm = 1.0 / (FR * math.sqrt(FR * hour * channels))
    high, low = two_parts(sub_tables())
    tables = [pick_table(), high, low, turn_table(), column_table(), twist_table(), row_table()]
    depth = LANES
    part = (hour, SLOTS, 2 * SPLIT, LANES)
    rows = (chan * hour, 2 * SPLIT, LANES)
    vmem, hbm = pl.BlockSpec(memory_space=pltpu.VMEM), pl.BlockSpec(memory_space=pl.ANY)
    sems = pltpu.SemaphoreType.DMA
    wave = pl.pallas_call(
        functools.partial(kernel, chan, hour, norm),
        out_shape=jax.ShapeDtypeStruct((OUT_ROWS, LANES), jnp.float32),
        in_specs=[hbm, hbm, vmem, vmem] + [hbm] * len(tables),
        out_specs=vmem,
        scratch_shapes=[pltpu.VMEM(table.shape, table.dtype) for table in tables]
        + [
            pltpu.VMEM((chan, per, FR), jnp.bfloat16),
            pltpu.VMEM((chan, per, count), jnp.bfloat16),
            pltpu.VMEM((8, depth), jnp.int32),
            pltpu.VMEM((chan, 8, depth), jnp.int32),
            pltpu.VMEM((SPLIT * per, SUB), jnp.bfloat16),
            pltpu.VMEM((SPLIT, channels, LANES), jnp.bfloat16),
            pltpu.VMEM((SPLIT, per, 2 * SUB), jnp.float32),
            pltpu.VMEM((SPLIT, channels, 2 * SUB), jnp.float32),
            pltpu.VMEM((TILES, SPLIT, 2, channels, LANES), jnp.float32),
            pltpu.VMEM((rows[0] * rows[1], SLOTS * rows[1]), jnp.bfloat16),
            pltpu.VMEM(part, jnp.bfloat16),
            pltpu.VMEM(part, jnp.bfloat16),
            pltpu.VMEM((rows[0] * rows[1], LANES), jnp.float32),
            pltpu.VMEM(rows, jnp.bfloat16),
            pltpu.VMEM(rows, jnp.bfloat16),
            sems((len(tables),)),
            sems((2,)),
        ]
        + [sems((chan,))] * 6
        + [sems((hour,))] * 2
        + [sems((5, hour))] * 2
        + [sems((chan, hour))] * 2,
        compiler_params=pltpu.CompilerParams(
            collective_id=0, has_side_effects=True, vmem_limit_bytes=56 * 2**20
        ),
    )(
        traces.reshape(chan, per, FR),
        taps.reshape(chan, per, count),
        bin_ids.T,
        owners.reshape(1, -1),
        *[jnp.asarray(table) for table in tables],
    )
    return wave.reshape(1, 2 * FR)


def solution(mesh):
    placed = (P("chan", "hour"), P("chan", None), P(None, "chan"), P())

    def whole(traces, taps, bin_ids, owners):
        chan, hour = mesh.shape["chan"], mesh.shape["hour"]
        channels = traces.shape[0] // chan
        fits = (
            chan == 8
            and hour == TILES
            and channels % (16 * chan) == 0
            and traces.shape[1] == hour * FR
            and taps.shape[1] == SPLIT * LANES // 2
            and owners.shape[0] == chan * hour
        )
        return jax.shard_map(
            split_body if fits else body,
            mesh=mesh,
            in_specs=placed,
            out_specs=P(("chan", "hour"), None),
            check_vma=False,
        )(traces, taps, bin_ids, owners)

    return whole
```

```python
import functools
import math

import jax
import jax.numpy as jnp
import numpy as np
from jax import lax
from jax.experimental import pallas as pl
from jax.experimental.pallas import tpu as pltpu
from jax.sharding import PartitionSpec as P

FR = 4096
ROUNDS = 4
MESH = pl.DeviceIdType.MESH


exact = lax.Precision.HIGHEST

def passed_along(shard, axis, by):
    devices = lax.axis_size(axis)
    pairs = [(i, i + by) for i in range(devices) if 0 <= i + by < devices]
    return lax.ppermute(shard, axis, pairs)


def transform(real_part, imag_part, count):
    span = real_part.shape[-1]
    inner = 2 * span // 128
    lead = real_part.shape[:-1]
    first = jnp.arange(64, dtype=jnp.float32)[:, None]
    middle = jnp.arange(128, dtype=jnp.float32)[None, :]
    angle_one = 2.0 * math.pi / 128.0 * jnp.mod(first * middle, 128.0)
    cos_one = jnp.cos(angle_one)
    sin_one = -jnp.sin(angle_one)
    second = jnp.arange(inner, dtype=jnp.float32)[:, None]
    angle_turn = 2.0 * math.pi / (128.0 * inner) * jnp.mod(second * middle, 128.0 * inner)
    cos_turn = jnp.cos(angle_turn)
    sin_turn = -jnp.sin(angle_turn)
    outer = jnp.arange(count // 128, dtype=jnp.float32)[None, :]
    angle_two = 2.0 * math.pi / inner * jnp.mod(second * outer, float(inner))
    cos_two = jnp.cos(angle_two)
    sin_two = -jnp.sin(angle_two)
    grid = real_part.reshape(lead + (64, inner))
    section_re = jnp.einsum("...an,ak->...nk", grid, cos_one, precision=exact)
    section_im = jnp.einsum("...an,ak->...nk", grid, sin_one, precision=exact)
    if imag_part is not None:
        grid_im = imag_part.reshape(lead + (64, inner))
        section_re = section_re - jnp.einsum("...an,ak->...nk", grid_im, sin_one, precision=exact)
        section_im = section_im + jnp.einsum("...an,ak->...nk", grid_im, cos_one, precision=exact)
    turned_re = section_re * cos_turn - section_im * sin_turn
    turned_im = section_re * sin_turn + section_im * cos_turn
    out_re = jnp.einsum("...nk,nm->...mk", turned_re, cos_two, precision=exact) - jnp.einsum(
        "...nk,nm->...mk", turned_im, sin_two, precision=exact
    )
    out_im = jnp.einsum("...nk,nm->...mk", turned_re, sin_two, precision=exact) + jnp.einsum(
        "...nk,nm->...mk", turned_im, cos_two, precision=exact
    )
    return (out_re.reshape(lead + (count,)), out_im.reshape(lead + (count,)))


def filtered(samples, filters):
    channels = samples.shape[0]
    frames = samples.shape[1] // FR
    signal = samples.astype(jnp.float32).reshape(channels, frames, FR)
    freq_re, freq_im = transform(signal, None, FR)
    padded_taps = jnp.pad(filters.astype(jnp.float32), ((0, 0), (0, FR - filters.shape[1])))
    resp_re, resp_im = transform(padded_taps, None, FR)
    resp_re = resp_re[:, None, :]
    resp_im = resp_im[:, None, :]
    spec_re = (freq_re * resp_re - freq_im * resp_im).astype(jnp.bfloat16)
    spec_im = (freq_re * resp_im + freq_im * resp_re).astype(jnp.bfloat16)
    return (spec_re, spec_im)


def body(traces, taps, bin_ids, owners):
    channels = traces.shape[0]
    frames = traces.shape[1] // FR
    spec_re, spec_im = filtered(traces, taps)
    mine = lax.axis_index("chan")
    near_re = spec_re.astype(jnp.float32)
    near_im = spec_im.astype(jnp.float32)
    results = []
    for offset in range(ROUNDS):
        far_re, far_im = passed_along((spec_re, spec_im), "chan", offset + 1)
        far_re = far_re.astype(jnp.float32)
        far_im = far_im.astype(jnp.float32)
        cross_re = jnp.sum(far_re * near_re + far_im * near_im, axis=(0, 1))
        cross_im = jnp.sum(far_im * near_re - far_re * near_im, axis=(0, 1))
        results.append(jnp.stack([cross_re, cross_im]))
    contrib = jnp.stack(results)
    nbins = owners.shape[0]
    own_bins = bin_ids[:, 0]
    labels = jnp.arange(nbins, dtype=jnp.int32)
    places = jnp.sum(jnp.where(own_bins[:, None] == labels[None, :], owners[None, :], 0), axis=1)
    valid = jnp.arange(ROUNDS, dtype=jnp.int32) < mine
    places = jnp.where(valid, places, -1)
    width = contrib.shape[2]
    flat = contrib.reshape(ROUNDS, 2 * width)
    per_device = nbins // lax.axis_size("chan")
    rows = jnp.arange(lax.axis_size("chan") * per_device, dtype=jnp.int32)
    onehot = (places[None, :] == rows[:, None]).astype(jnp.float32)
    stacked = lax.psum_scatter(
        jnp.dot(onehot, flat, precision=exact, preferred_element_type=jnp.float32),
        "chan",
        scatter_dimension=0,
        tiled=True,
    )
    stacked = stacked.reshape(per_device, 2, width)
    final = lax.psum_scatter(stacked, "hour", scatter_dimension=0, tiled=True)
    weights = jnp.where(jnp.arange(FR) == 0, 1.0, 2.0).astype(jnp.float32)
    wave_re, wave_im = transform(final[:, 0] * weights, -final[:, 1] * weights, 2 * FR)
    norm = 1.0 / (FR * math.sqrt(FR * lax.axis_size("hour") * frames * channels))
    return wave_re * norm

SPLIT = 8
SUB = FR // SPLIT
LANES = 128
TILES = SUB // LANES


def sub_tables():
    a = np.arange(SUB)[:, None]
    k1 = np.arange(SUB)[None, :]
    turn = 2.0 * np.pi * ((a * k1) % (2 * SUB)) / (2 * SUB)
    cos, sin = np.cos(turn), -np.sin(turn)
    sin[:, 0] = 1.0 - 2.0 * (np.arange(SUB) % 2)
    table = np.stack([cos.reshape(SUB, TILES, LANES), sin.reshape(SUB, TILES, LANES)], axis=2)
    return table.reshape(SUB, 2 * SUB)


def two_parts(table):
    high = table.astype(jnp.bfloat16)
    low = (table - high.astype(np.float64)).astype(jnp.bfloat16)
    return high, low


PIECE = 512
SHARE = PIECE // SPLIT


def pick_tables():
    table = np.zeros((PIECE, SPLIT, 2, SHARE), np.float32)
    for n in range(SPLIT):
        for b in range(SHARE):
            table[SPLIT * b + n, n, :, b] = 1.0
    twice = table.reshape(PIECE, 2 * PIECE).astype(jnp.bfloat16)
    return np.ascontiguousarray(table[:, :, 0].reshape(PIECE, PIECE)).astype(jnp.bfloat16), twice


def turn_table():
    n = np.arange(SPLIT)[:, None]
    k1 = np.arange(SUB)[None, :]
    turn = 2.0 * np.pi * n * k1 / (2 * FR)
    table = np.stack([np.cos(turn), -np.sin(turn)], axis=1).reshape(SPLIT, 2, TILES, 1, LANES)
    table = np.broadcast_to(table.transpose(2, 0, 1, 3, 4), (TILES, SPLIT, 2, 8, LANES))
    return np.ascontiguousarray(table).astype(np.float32)


def times(value, angle):
    re, im = value
    c, s = math.cos(angle), math.sin(angle)
    if abs(s) < 1e-12:
        return (re, im) if c > 0 else (-re, -im)
    if abs(c) < 1e-12:
        return (-im, re) if s > 0 else (im, -re)
    if abs(abs(c) - abs(s)) < 1e-12:
        root = abs(c)
        p, q = math.copysign(1.0, c), math.copysign(1.0, s)
        first = (re if p > 0 else -re) + (-im if q > 0 else im)
        second = (re if q > 0 else -re) + (im if p > 0 else -im)
        return first * root, second * root
    return re * c - im * s, re * s + im * c


def small_dft(values, sign, half=False):
    size = len(values)
    if size == 1:
        return values
    even = small_dft(values[0::2], sign)
    odd = small_dft(values[1::2], sign)
    low, high = [], []
    for k in range(size // 2):
        turned = times(odd[k], sign * 2.0 * math.pi * k / size)
        low.append((even[k][0] + turned[0], even[k][1] + turned[1]))
        if not half:
            high.append((even[k][0] - turned[0], even[k][1] - turned[1]))
    return low + high


LATE = 8
SLOTS = 32


def slot_of(step, before, chan):
    if isinstance(step, int) and step == chan - 1:
        return before
    return LATE + step * (step - 1) // 2 + before


def rows_of_pairs(ids, owners):
    depth = ids.shape[1]
    nbins = owners.shape[1]
    bins = lax.broadcasted_iota(jnp.int32, (nbins, depth), 0) + 1
    picked = (bins == ids[0:1, :]).astype(jnp.float32).astype(jnp.bfloat16)
    row = lax.broadcasted_iota(jnp.int32, (nbins, nbins), 0)
    moved = (row == owners[...]).astype(jnp.float32).astype(jnp.bfloat16)
    return jnp.dot(moved, picked, preferred_element_type=jnp.float32).astype(jnp.bfloat16)


def fold(values):
    sublane = lax.broadcasted_iota(jnp.int32, values[0].shape, 0)
    shift = 1
    while len(values) > 1:
        first = lax.rem(lax.div(sublane, shift), 2) == 0
        values = [
            jnp.where(first, a, b) + pltpu.roll(jnp.where(first, b, a), SPLIT - shift, 0)
            for a, b in zip(values[0::2], values[1::2])
        ]
        shift *= 2
    return values[0]


OUT_ROWS = 2 * FR // LANES
TERMS = 2 * SPLIT * (TILES + 1)


def column_table():
    v = np.arange(LANES)[:, None]
    t, k2 = np.arange(TILES)[None, :, None], np.arange(SPLIT)[None, None, :]
    main = 2.0 * np.pi * ((v[:, :, None] * (SPLIT * k2 + t)) % OUT_ROWS) / OUT_ROWS
    extra = 2.0 * np.pi * ((v * (SPLIT // 2 + SPLIT * (np.arange(SPLIT)[None, :] - SPLIT // 2))) % OUT_ROWS) / OUT_ROWS
    phase = np.concatenate([main, extra[:, None, :]], axis=1)
    top = np.stack([np.cos(phase), -np.sin(phase)], axis=2).reshape(LANES, TERMS)
    under = np.stack([np.sin(phase), np.cos(phase)], axis=2).reshape(LANES, TERMS)
    high, low = two_parts(np.concatenate([top, under], axis=0))
    rest = np.zeros((2 * LANES, 2 * LANES - 3 * TERMS), jnp.bfloat16)
    return np.concatenate([high, high, low, rest], axis=1)


def twist_table():
    turn = 2.0 * np.pi * np.arange(LANES)[:, None] * np.arange(LANES)[None, :] / (2 * FR)
    return np.stack([np.cos(turn), np.sin(turn)]).astype(np.float32)


def row_table():
    turn = 2.0 * np.pi * ((np.arange(OUT_ROWS)[:, None] * np.arange(LANES)[None, :]) % OUT_ROWS) / OUT_ROWS
    high, low = two_parts(np.concatenate([np.cos(turn), -np.sin(turn)], axis=1))
    return np.concatenate([high, high, low], axis=1)


def halves(value):
    top = value.astype(jnp.bfloat16)
    return top, (value - top.astype(jnp.float32)).astype(jnp.bfloat16)


def over_lanes(a, b):
    return lax.dot_general(a, b, (((1,), (1,)), ((), ())), preferred_element_type=jnp.float32)


def inverse(rows, column, twist, across, norm):
    lane = lax.broadcasted_iota(jnp.int32, rows.shape, 1)
    slot = lax.broadcasted_iota(jnp.int32, rows.shape, 0)
    rows = rows * jnp.where((lane == 0) & (slot == 0), norm, 2.0 * norm)
    apart = (lane == 0) & (slot < 2 * SPLIT) & (lax.rem(slot, SPLIT) >= SPLIT // 2)
    every = jnp.concatenate(
        [jnp.where(apart, 0.0, rows), jnp.where(apart, rows, 0.0)[: 2 * SPLIT]], axis=0
    )
    top, rest = halves(every)
    nothing = jnp.zeros((2 * LANES - 3 * TERMS, LANES), jnp.bfloat16)
    z = jnp.dot(
        column[...], jnp.concatenate([top, rest, top, nothing], axis=0), preferred_element_type=jnp.float32
    )
    z_re, z_im = z[:LANES], z[LANES:]
    c, s = twist[0], twist[1]
    y = jnp.concatenate([z_re * c - z_im * s, z_re * s + z_im * c], axis=1)
    top, rest = halves(y)
    return over_lanes(across[...], jnp.concatenate([top, rest, top], axis=1))


def kernel(chan, hour, norm, x, taps, bin_ids, owners, *refs):
    tables, out = refs[:8], refs[8]
    held = refs[9:17]
    pick, high, low, turns, column, twist = held[:6]
    across, twice = held[6:]
    xin, tin, ids, ids_in, xd, td, fx, fh, spec, kron, part, first, early, outbox, inbox = refs[17:32]
    table_sem, own_sem, ids_send, ids_recv, t_send, t_recv, x_send, x_recv = refs[32:40]
    f_send, f_recv, send, recv, send2, recv2 = refs[40:]
    me, my_hour = lax.axis_index("chan"), lax.axis_index("hour")
    per = xin.shape[1]
    share = pl.ds(pl.multiple_of(my_hour * (tin.shape[2] // hour), LANES), tin.shape[2] // hour)

    def flipped(at, o, size):
        to, bit = at, 1
        while bit < size:
            to = to + lax.rem(lax.div(o, bit), 2) * bit * (1 - 2 * lax.rem(lax.div(at, bit), 2))
            bit *= 2
        return to

    def partner(o):
        return flipped(me, o, chan)

    def beside(o):
        return flipped(my_hour, o, hour)

    def sent(src, dst, sends, recvs, **device):
        return pltpu.make_async_remote_copy(
            src_ref=src, dst_ref=dst, send_sem=sends, recv_sem=recvs, device_id=device, device_id_type=MESH
        )

    loads = [pltpu.make_async_copy(src, dst, table_sem.at[z]) for z, (src, dst) in enumerate(zip(tables, held))]
    own = [
        pltpu.make_async_copy(x.at[me], xin.at[me], own_sem.at[0]),
        pltpu.make_async_copy(taps.at[me, :, share], tin.at[me, :, share], own_sem.at[1]),
    ]
    for copy in own + loads:
        copy.start()
    barrier = pltpu.get_barrier_semaphore()
    for o in range(1, hour):
        pl.semaphore_signal(
            barrier, inc=1, device_id={"hour": lax.rem(my_hour + o, hour)}, device_id_type=MESH
        )
    for o in range(1, chan):
        pl.semaphore_signal(barrier, inc=1, device_id={"chan": partner(o)}, device_id_type=MESH)
    place = lax.broadcasted_iota(jnp.int32, ids.shape, 1)
    labels = jnp.zeros(ids.shape, jnp.int32)
    for r in range(ROUNDS):
        live = (place == me * ROUNDS + r) & (me >= r + 1)
        labels = jnp.where(live, bin_ids[:, r : r + 1] + 1, labels)
    ids[...] = labels
    pl.semaphore_wait(barrier, chan + hour - 2)

    def x_copy(o):
        to = partner(o)
        return sent(x.at[to], xin.at[me], x_send.at[o], x_recv.at[o], chan=to)

    far_first = sorted(range(1, chan), key=lambda o: -(o.bit_length()))
    tap_copies, id_copies = [], []
    for o in far_first:
        to = partner(o)
        tap_copies.append(
            sent(taps.at[to, :, share], tin.at[me, :, share], t_send.at[o], t_recv.at[o], chan=to)
        )
        tap_copies[-1].start()
    for o in far_first:
        id_copies.append(sent(ids, ids_in.at[o], ids_send.at[o], ids_recv.at[o], chan=partner(o)))
        id_copies[-1].start()
    for o in range(1, chan):
        x_copy(o).start()
    lane0 = lax.broadcasted_iota(jnp.int32, (8, LANES), 1) == 0

    def spectra(block, t, edge):
        @pl.loop(0, per // 8)
        def _(g):
            piece = pl.ds(pl.multiple_of(8 * g, 8), 8)
            here = pl.ds(pl.multiple_of(block * per + 8 * g, 8), 8)

            def bins_of(f, rows):
                values, extra = [], []
                for n in range(SPLIT):
                    re = f[n, rows, pl.ds(pl.multiple_of(2 * t * LANES, LANES), LANES)]
                    im = f[n, rows, pl.ds(pl.multiple_of((2 * t + 1) * LANES, LANES), LANES)]
                    if edge:
                        angle = -math.pi * n / SPLIT
                        extra.append((im * math.cos(angle), im * math.sin(angle)))
                        im = jnp.where(lane0, 0.0, im)
                    if n == 0:
                        values.append((re, im))
                    else:
                        c, s = turns[t, n, 0], turns[t, n, 1]
                        values.append((re * c - im * s, re * s + im * c))
                found = small_dft(values, -1)
                if edge:
                    more = small_dft(extra, -1, half=True)
                    for k2 in range(SPLIT // 2):
                        old = found[SPLIT // 2 + k2]
                        found[SPLIT // 2 + k2] = tuple(
                            jnp.where(lane0, more[k2][z], old[z]) for z in range(2)
                        )
                return found

            freq = bins_of(fx, piece)
            resp = bins_of(fh, here)
            for k2 in range(SPLIT):
                (xr, xi), (hr, hi) = freq[k2], resp[k2]
                spec[t, k2, 0, here, :] = (xr * hr - xi * hi).astype(jnp.bfloat16).astype(jnp.float32)
                spec[t, k2, 1, here, :] = (xr * hi + xi * hr).astype(jnp.bfloat16).astype(jnp.float32)

    half = lax.broadcasted_iota(jnp.int32, (per, LANES), 1) < SHARE

    def transform_of(block):
        flat = jnp.concatenate([xin[block, :, q * PIECE : (q + 1) * PIECE] for q in range(FR // PIECE)], axis=0)
        got = jnp.dot(flat, pick[...], preferred_element_type=jnp.float32)
        for g in range(TILES):
            for n in range(SPLIT):
                a, b = (
                    got[q * per : (q + 1) * per, n // 2 * LANES : (n // 2 + 1) * LANES] for q in (2 * g, 2 * g + 1)
                )
                if n % 2:
                    a = pltpu.roll(a, SHARE, 1)
                else:
                    b = pltpu.roll(b, SHARE, 1)
                xd[n * per : (n + 1) * per, g * LANES : (g + 1) * LANES] = jnp.where(half, a, b).astype(jnp.bfloat16)
        found = jnp.dot(xd[...], high[...], preferred_element_type=jnp.float32) + jnp.dot(
            xd[...], low[...], preferred_element_type=jnp.float32
        )
        for n in range(SPLIT):
            fx[n] = found[n * per : (n + 1) * per]

    def spectra_of(block):
        spectra(block, 0, True)

        @pl.loop(1, TILES)
        def _(t):
            spectra(block, t, False)

    def take(block):
        transform_of(block)
        spectra_of(block)

    for copy in loads + own[:1]:
        copy.wait()
    transform_of(me)
    own[1].wait()
    for copy in tap_copies:
        copy.wait_recv()
    forwards = []
    for o in range(1, hour):
        to = lax.rem(my_hour + o, hour)
        forwards.append(sent(tin.at[:, :, share], tin.at[:, :, share], f_send.at[o], f_recv.at[o], hour=to))
        forwards[-1].start()
    for copy in id_copies:
        copy.wait_recv()
    labels = ids[...]
    for o in range(1, chan):
        labels = labels + ids_in[o]
    by_pair = rows_of_pairs(labels, owners)
    nbins = chan * hour
    pair = lax.broadcasted_iota(jnp.int32, (ids.shape[1], SLOTS), 0)
    column_of = lax.broadcasted_iota(jnp.int32, (ids.shape[1], SLOTS), 1)
    places = jnp.zeros(pair.shape, jnp.float32)
    for s in range(1, chan):
        for j in range(s):
            near, far = jnp.maximum(partner(s), partner(j)), jnp.minimum(partner(s), partner(j))
            held_by = jnp.where(near - far <= ROUNDS, near * ROUNDS + near - far - 1, -1)
            hit = (column_of == slot_of(s, j, chan)) & (pair == held_by)
            places = jnp.where(hit, 1.0, places)
    by_slot = jnp.dot(by_pair, places.astype(jnp.bfloat16), preferred_element_type=jnp.float32).astype(jnp.bfloat16)
    deep = 2 * SPLIT
    spread = (
        lax.div(lax.broadcasted_iota(jnp.int32, (nbins * deep, nbins), 0), deep)
        == lax.broadcasted_iota(jnp.int32, (nbins * deep, nbins), 1)
    ).astype(jnp.float32).astype(jnp.bfloat16)
    widen = (
        lax.div(lax.broadcasted_iota(jnp.int32, (SLOTS, SLOTS * deep), 1), deep)
        == lax.broadcasted_iota(jnp.int32, (SLOTS, SLOTS * deep), 0)
    ).astype(jnp.float32).astype(jnp.bfloat16)
    tall = jnp.dot(spread, by_slot, preferred_element_type=jnp.float32).astype(jnp.bfloat16)
    both = jnp.dot(tall, widen, preferred_element_type=jnp.float32)
    same = lax.rem(lax.broadcasted_iota(jnp.int32, both.shape, 0), deep) == lax.rem(
        lax.broadcasted_iota(jnp.int32, both.shape, 1), deep
    )
    kron[...] = jnp.where(same, both, 0.0).astype(jnp.bfloat16)

    def cross(t, near, far, slot):
        res, ims = [], []
        for k2 in range(SPLIT):
            re = im = None
            for c in range(per // 8):
                at = pl.ds(pl.multiple_of(near * per + 8 * c, 8), 8)
                of = pl.ds(pl.multiple_of(far * per + 8 * c, 8), 8)
                nr, ni = spec[t, k2, 0, at, :], spec[t, k2, 1, at, :]
                fr, fi = spec[t, k2, 0, of, :], spec[t, k2, 1, of, :]
                one, two = fr * nr + fi * ni, fi * nr - fr * ni
                re, im = (one, two) if re is None else (re + one, im + two)
            res.append(re)
            ims.append(im)
        part[t, slot] = jnp.concatenate([fold(res), fold(ims)], axis=0).astype(jnp.bfloat16)

    def crosses(s, begin):
        @pl.loop(0, s)
        def _(j):
            a, b = partner(s), partner(j)
            for t in range(TILES):
                cross(t, jnp.maximum(a, b), jnp.minimum(a, b), begin + j)

    def part_copy(z, o, begin, count):
        where = pl.ds(begin, count)
        return sent(part.at[beside(o), where], first.at[o, where], send.at[z, o], recv.at[z, o], hour=beside(o))

    groups = [(LATE, 6), (LATE + 6, 4), (LATE + 10, 5), (LATE + 15, 6), (0, 7)]
    order = [2, 3, 1, 0]
    for copy in forwards:
        copy.wait_recv()
    count = tin.shape[2]
    got = jnp.dot(tin[...].reshape(chan * per, count), twice[...], preferred_element_type=jnp.float32)
    for n in range(SPLIT):
        td[n] = got[:, n * LANES : (n + 1) * LANES].astype(jnp.bfloat16)
    found = jnp.dot(
        td[...].reshape(SPLIT * chan * per, LANES),
        jnp.concatenate([high[:SHARE, :], low[:SHARE, :]], axis=0),
        preferred_element_type=jnp.float32,
    )
    for n in range(SPLIT):
        fh[n] = found[n * chan * per : (n + 1) * chan * per]
    spectra_of(me)

    @pl.loop(1, chan // 2)
    def _(s):
        x_copy(s).wait_recv()
        take(partner(s))
        crosses(s, LATE + lax.div(s * (s - 1), 2))

    for o in order[:3]:
        part_copy(0, o, *groups[0]).start()

    @pl.loop(chan // 2, chan)
    def _(s):
        x_copy(s).wait_recv()
        take(partner(s))
        last = lax.div(s, chan - 1)
        begin = (LATE + lax.div(s * (s - 1), 2)) * (1 - last)

        crosses(s, begin)

        for z in range(1, len(groups)):

            @pl.when(s == z + 3)
            def _():
                for o in order[:3]:
                    part_copy(z, o, *groups[z]).start()

    def mixed(begin, count, room):
        where = slice(begin, begin + count)
        total = part[my_hour, where].astype(jnp.float32)
        for o in range(1, hour):
            total = total + first[o, where].astype(jnp.float32)
        total = total.reshape(count * deep, LANES)
        if room > count:
            total = jnp.concatenate([total, jnp.zeros(((room - count) * deep, LANES), jnp.float32)], axis=0)
        got = jnp.dot(
            kron[:, begin * deep : (begin + room) * deep],
            jnp.concatenate(halves(total), axis=1),
            preferred_element_type=jnp.float32,
        )
        return got[:, :LANES] + got[:, LANES:]

    for z in range(len(groups) - 1):
        for o in range(1, hour):
            part_copy(z, o, *groups[z]).wait_recv()
    early[...] = mixed(LATE, 21, SLOTS - LATE)
    for o in range(1, hour):
        part_copy(4, o, *groups[4]).wait_recv()
    outbox[...] = (mixed(0, 7, LATE) + early[...]).astype(jnp.bfloat16).reshape(outbox.shape)
    for oc in far_first + [0]:
        for o in order:
            if oc or o:
                to, at = partner(oc), beside(o)
                sent(
                    outbox.at[to * hour + at],
                    inbox.at[oc * hour + my_hour],
                    send2.at[oc, o],
                    recv2.at[oc, o],
                    chan=to,
                    hour=at,
                ).start()
    inbox[my_hour] = outbox[me * hour + my_hour]
    for copy in tap_copies + id_copies + forwards:
        copy.wait_send()
    for o in range(1, chan):
        x_copy(o).wait_send()
    for z in range(len(groups)):
        for o in range(1, hour):
            part_copy(z, o, *groups[z]).wait_send()

    def out_copy(oc, o):
        return sent(
            outbox.at[0], inbox.at[oc * hour + beside(o)], send2.at[oc, o], recv2.at[oc, o],
            chan=partner(oc), hour=beside(o),
        )

    for oc in range(chan):
        for o in range(hour):
            if oc or o:
                out_copy(oc, o).wait_recv()
    rows = inbox[0:hour].astype(jnp.float32)
    for oc in range(1, chan):
        rows = rows + inbox[oc * hour : (oc + 1) * hour].astype(jnp.float32)
    wave = inverse(rows.reshape(TILES * deep, LANES), column, twist, across, norm)
    for u in range(OUT_ROWS):
        out[:, u * LANES : (u + 1) * LANES] = wave[u : u + 1]
    for oc in range(chan):
        for o in range(hour):
            if oc or o:
                out_copy(oc, o).wait_send()


def split_body(traces, taps, bin_ids, owners):
    chan, hour = lax.axis_size("chan"), lax.axis_size("hour")
    channels, count = taps.shape
    per = channels // chan
    norm = 1.0 / (FR * math.sqrt(FR * hour * channels))
    high, low = two_parts(sub_tables())
    pick, twice = pick_tables()
    tables = [pick, high, low, turn_table(), column_table(), twist_table(), row_table(), twice]
    depth = LANES
    part = (hour, SLOTS, 2 * SPLIT, LANES)
    rows = (chan * hour, 2 * SPLIT, LANES)
    vmem, hbm = pl.BlockSpec(memory_space=pltpu.VMEM), pl.BlockSpec(memory_space=pl.ANY)
    sems = pltpu.SemaphoreType.DMA
    wave = pl.pallas_call(
        functools.partial(kernel, chan, hour, norm),
        out_shape=jax.ShapeDtypeStruct((1, 2 * FR), jnp.float32),
        in_specs=[hbm, hbm, vmem, vmem] + [hbm] * len(tables),
        out_specs=vmem,
        scratch_shapes=[pltpu.VMEM(table.shape, table.dtype) for table in tables]
        + [
            pltpu.VMEM((chan, per, FR), jnp.bfloat16),
            pltpu.VMEM((chan, per, count), jnp.bfloat16),
            pltpu.VMEM((8, depth), jnp.int32),
            pltpu.VMEM((chan, 8, depth), jnp.int32),
            pltpu.VMEM((SPLIT * per, SUB), jnp.bfloat16),
            pltpu.VMEM((SPLIT, channels, LANES), jnp.bfloat16),
            pltpu.VMEM((SPLIT, per, 2 * SUB), jnp.float32),
            pltpu.VMEM((SPLIT, channels, 2 * SUB), jnp.float32),
            pltpu.VMEM((TILES, SPLIT, 2, channels, LANES), jnp.float32),
            pltpu.VMEM((rows[0] * rows[1], SLOTS * rows[1]), jnp.bfloat16),
            pltpu.VMEM(part, jnp.bfloat16),
            pltpu.VMEM(part, jnp.bfloat16),
            pltpu.VMEM((rows[0] * rows[1], LANES), jnp.float32),
            pltpu.VMEM(rows, jnp.bfloat16),
            pltpu.VMEM(rows, jnp.bfloat16),
            sems((len(tables),)),
            sems((2,)),
        ]
        + [sems((chan,))] * 6
        + [sems((hour,))] * 2
        + [sems((5, hour))] * 2
        + [sems((chan, hour))] * 2,
        compiler_params=pltpu.CompilerParams(
            collective_id=0, has_side_effects=True, vmem_limit_bytes=56 * 2**20
        ),
    )(
        traces.reshape(chan, per, FR),
        taps.reshape(chan, per, count),
        bin_ids.T,
        owners.reshape(1, -1),
        *[jnp.asarray(table) for table in tables],
    )
    return wave


def solution(mesh):
    placed = (P("chan", "hour"), P("chan", None), P(None, "chan"), P())

    def whole(traces, taps, bin_ids, owners):
        chan, hour = mesh.shape["chan"], mesh.shape["hour"]
        channels = traces.shape[0] // chan
        fits = (
            chan == 8
            and hour == TILES
            and channels % (16 * chan) == 0
            and traces.shape[1] == hour * FR
            and taps.shape[1] == SPLIT * LANES // 2
            and owners.shape[0] == chan * hour
        )
        return jax.shard_map(
            split_body if fits else body,
            mesh=mesh,
            in_specs=placed,
            out_specs=P(("chan", "hour"), None),
            check_vma=False,
        )(traces, taps, bin_ids, owners)

    return whole
```

```python
import functools
import math

import jax
import jax.numpy as jnp
import numpy as np
from jax import lax
from jax.experimental import pallas as pl
from jax.experimental.pallas import tpu as pltpu
from jax.sharding import PartitionSpec as P

FR = 4096
ROUNDS = 4
MESH = pl.DeviceIdType.MESH


exact = lax.Precision.HIGHEST

def passed_along(shard, axis, by):
    devices = lax.axis_size(axis)
    pairs = [(i, i + by) for i in range(devices) if 0 <= i + by < devices]
    return lax.ppermute(shard, axis, pairs)


def transform(real_part, imag_part, count):
    span = real_part.shape[-1]
    inner = 2 * span // 128
    lead = real_part.shape[:-1]
    first = jnp.arange(64, dtype=jnp.float32)[:, None]
    middle = jnp.arange(128, dtype=jnp.float32)[None, :]
    angle_one = 2.0 * math.pi / 128.0 * jnp.mod(first * middle, 128.0)
    cos_one = jnp.cos(angle_one)
    sin_one = -jnp.sin(angle_one)
    second = jnp.arange(inner, dtype=jnp.float32)[:, None]
    angle_turn = 2.0 * math.pi / (128.0 * inner) * jnp.mod(second * middle, 128.0 * inner)
    cos_turn = jnp.cos(angle_turn)
    sin_turn = -jnp.sin(angle_turn)
    outer = jnp.arange(count // 128, dtype=jnp.float32)[None, :]
    angle_two = 2.0 * math.pi / inner * jnp.mod(second * outer, float(inner))
    cos_two = jnp.cos(angle_two)
    sin_two = -jnp.sin(angle_two)
    grid = real_part.reshape(lead + (64, inner))
    section_re = jnp.einsum("...an,ak->...nk", grid, cos_one, precision=exact)
    section_im = jnp.einsum("...an,ak->...nk", grid, sin_one, precision=exact)
    if imag_part is not None:
        grid_im = imag_part.reshape(lead + (64, inner))
        section_re = section_re - jnp.einsum("...an,ak->...nk", grid_im, sin_one, precision=exact)
        section_im = section_im + jnp.einsum("...an,ak->...nk", grid_im, cos_one, precision=exact)
    turned_re = section_re * cos_turn - section_im * sin_turn
    turned_im = section_re * sin_turn + section_im * cos_turn
    out_re = jnp.einsum("...nk,nm->...mk", turned_re, cos_two, precision=exact) - jnp.einsum(
        "...nk,nm->...mk", turned_im, sin_two, precision=exact
    )
    out_im = jnp.einsum("...nk,nm->...mk", turned_re, sin_two, precision=exact) + jnp.einsum(
        "...nk,nm->...mk", turned_im, cos_two, precision=exact
    )
    return (out_re.reshape(lead + (count,)), out_im.reshape(lead + (count,)))


def filtered(samples, filters):
    channels = samples.shape[0]
    frames = samples.shape[1] // FR
    signal = samples.astype(jnp.float32).reshape(channels, frames, FR)
    freq_re, freq_im = transform(signal, None, FR)
    padded_taps = jnp.pad(filters.astype(jnp.float32), ((0, 0), (0, FR - filters.shape[1])))
    resp_re, resp_im = transform(padded_taps, None, FR)
    resp_re = resp_re[:, None, :]
    resp_im = resp_im[:, None, :]
    spec_re = (freq_re * resp_re - freq_im * resp_im).astype(jnp.bfloat16)
    spec_im = (freq_re * resp_im + freq_im * resp_re).astype(jnp.bfloat16)
    return (spec_re, spec_im)


def body(traces, taps, bin_ids, owners):
    channels = traces.shape[0]
    frames = traces.shape[1] // FR
    spec_re, spec_im = filtered(traces, taps)
    mine = lax.axis_index("chan")
    near_re = spec_re.astype(jnp.float32)
    near_im = spec_im.astype(jnp.float32)
    results = []
    for offset in range(ROUNDS):
        far_re, far_im = passed_along((spec_re, spec_im), "chan", offset + 1)
        far_re = far_re.astype(jnp.float32)
        far_im = far_im.astype(jnp.float32)
        cross_re = jnp.sum(far_re * near_re + far_im * near_im, axis=(0, 1))
        cross_im = jnp.sum(far_im * near_re - far_re * near_im, axis=(0, 1))
        results.append(jnp.stack([cross_re, cross_im]))
    contrib = jnp.stack(results)
    nbins = owners.shape[0]
    own_bins = bin_ids[:, 0]
    labels = jnp.arange(nbins, dtype=jnp.int32)
    places = jnp.sum(jnp.where(own_bins[:, None] == labels[None, :], owners[None, :], 0), axis=1)
    valid = jnp.arange(ROUNDS, dtype=jnp.int32) < mine
    places = jnp.where(valid, places, -1)
    width = contrib.shape[2]
    flat = contrib.reshape(ROUNDS, 2 * width)
    per_device = nbins // lax.axis_size("chan")
    rows = jnp.arange(lax.axis_size("chan") * per_device, dtype=jnp.int32)
    onehot = (places[None, :] == rows[:, None]).astype(jnp.float32)
    stacked = lax.psum_scatter(
        jnp.dot(onehot, flat, precision=exact, preferred_element_type=jnp.float32),
        "chan",
        scatter_dimension=0,
        tiled=True,
    )
    stacked = stacked.reshape(per_device, 2, width)
    final = lax.psum_scatter(stacked, "hour", scatter_dimension=0, tiled=True)
    weights = jnp.where(jnp.arange(FR) == 0, 1.0, 2.0).astype(jnp.float32)
    wave_re, wave_im = transform(final[:, 0] * weights, -final[:, 1] * weights, 2 * FR)
    norm = 1.0 / (FR * math.sqrt(FR * lax.axis_size("hour") * frames * channels))
    return wave_re * norm

SPLIT = 8
SUB = FR // SPLIT
LANES = 128
TILES = SUB // LANES


def sub_tables():
    a = np.arange(SUB)[:, None]
    k1 = np.arange(SUB)[None, :]
    turn = 2.0 * np.pi * ((a * k1) % (2 * SUB)) / (2 * SUB)
    cos, sin = np.cos(turn), -np.sin(turn)
    sin[:, 0] = 1.0 - 2.0 * (np.arange(SUB) % 2)
    table = np.stack([cos.reshape(SUB, TILES, LANES), sin.reshape(SUB, TILES, LANES)], axis=2)
    return table.reshape(SUB, 2 * SUB)


def two_parts(table):
    high = table.astype(jnp.bfloat16)
    low = (table - high.astype(np.float64)).astype(jnp.bfloat16)
    return high, low


PIECE = 512
SHARE = PIECE // SPLIT


def pick_tables():
    table = np.zeros((PIECE, SPLIT, 2, SHARE), np.float32)
    for n in range(SPLIT):
        for b in range(SHARE):
            table[SPLIT * b + n, n, :, b] = 1.0
    twice = table.reshape(PIECE, 2 * PIECE).astype(jnp.bfloat16)
    return np.ascontiguousarray(table[:, :, 0].reshape(PIECE, PIECE)).astype(jnp.bfloat16), twice


def turn_table():
    n = np.arange(SPLIT)[:, None]
    k1 = np.arange(SUB)[None, :]
    turn = 2.0 * np.pi * n * k1 / (2 * FR)
    table = np.stack([np.cos(turn), -np.sin(turn)], axis=1).reshape(SPLIT, 2, TILES, 1, LANES)
    table = np.broadcast_to(table.transpose(2, 0, 1, 3, 4), (TILES, SPLIT, 2, 8, LANES))
    return np.ascontiguousarray(table).astype(np.float32)


def times(value, angle):
    re, im = value
    c, s = math.cos(angle), math.sin(angle)
    if abs(s) < 1e-12:
        return (re, im) if c > 0 else (-re, -im)
    if abs(c) < 1e-12:
        return (-im, re) if s > 0 else (im, -re)
    if abs(abs(c) - abs(s)) < 1e-12:
        root = abs(c)
        p, q = math.copysign(1.0, c), math.copysign(1.0, s)
        first = (re if p > 0 else -re) + (-im if q > 0 else im)
        second = (re if q > 0 else -re) + (im if p > 0 else -im)
        return first * root, second * root
    return re * c - im * s, re * s + im * c


def small_dft(values, sign, half=False):
    size = len(values)
    if size == 1:
        return values
    even = small_dft(values[0::2], sign)
    odd = small_dft(values[1::2], sign)
    low, high = [], []
    for k in range(size // 2):
        turned = times(odd[k], sign * 2.0 * math.pi * k / size)
        low.append((even[k][0] + turned[0], even[k][1] + turned[1]))
        if not half:
            high.append((even[k][0] - turned[0], even[k][1] - turned[1]))
    return low + high


LATE = 8
SLOTS = 32


def slot_of(step, before, chan):
    if isinstance(step, int) and step == chan - 1:
        return before
    return LATE + step * (step - 1) // 2 + before


def rows_of_pairs(ids, owners):
    depth = ids.shape[1]
    nbins = owners.shape[1]
    bins = lax.broadcasted_iota(jnp.int32, (nbins, depth), 0) + 1
    picked = (bins == ids[0:1, :]).astype(jnp.float32).astype(jnp.bfloat16)
    row = lax.broadcasted_iota(jnp.int32, (nbins, nbins), 0)
    moved = (row == owners[...]).astype(jnp.float32).astype(jnp.bfloat16)
    return jnp.dot(moved, picked, preferred_element_type=jnp.float32).astype(jnp.bfloat16)


def fold(values):
    sublane = lax.broadcasted_iota(jnp.int32, values[0].shape, 0)
    shift = 1
    while len(values) > 1:
        first = lax.rem(lax.div(sublane, shift), 2) == 0
        values = [
            jnp.where(first, a, b) + pltpu.roll(jnp.where(first, b, a), SPLIT - shift, 0)
            for a, b in zip(values[0::2], values[1::2])
        ]
        shift *= 2
    return values[0]


OUT_ROWS = 2 * FR // LANES
TERMS = 2 * SPLIT * (TILES + 1)


def column_table():
    v = np.arange(LANES)[:, None]
    t, k2 = np.arange(TILES)[None, :, None], np.arange(SPLIT)[None, None, :]
    main = 2.0 * np.pi * ((v[:, :, None] * (SPLIT * k2 + t)) % OUT_ROWS) / OUT_ROWS
    extra = 2.0 * np.pi * ((v * (SPLIT // 2 + SPLIT * (np.arange(SPLIT)[None, :] - SPLIT // 2))) % OUT_ROWS) / OUT_ROWS
    phase = np.concatenate([main, extra[:, None, :]], axis=1)
    top = np.stack([np.cos(phase), -np.sin(phase)], axis=2).reshape(LANES, TERMS)
    under = np.stack([np.sin(phase), np.cos(phase)], axis=2).reshape(LANES, TERMS)
    high, low = two_parts(np.concatenate([top, under], axis=0))
    rest = np.zeros((2 * LANES, 2 * LANES - 3 * TERMS), jnp.bfloat16)
    return np.concatenate([high, high, low, rest], axis=1)


def twist_table():
    turn = 2.0 * np.pi * np.arange(LANES)[:, None] * np.arange(LANES)[None, :] / (2 * FR)
    return np.stack([np.cos(turn), np.sin(turn)]).astype(np.float32)


def row_table():
    turn = 2.0 * np.pi * ((np.arange(OUT_ROWS)[:, None] * np.arange(LANES)[None, :]) % OUT_ROWS) / OUT_ROWS
    high, low = two_parts(np.concatenate([np.cos(turn), -np.sin(turn)], axis=1))
    return np.concatenate([high, high, low], axis=1)


def halves(value):
    top = value.astype(jnp.bfloat16)
    return top, (value - top.astype(jnp.float32)).astype(jnp.bfloat16)


def over_lanes(a, b):
    return lax.dot_general(a, b, (((1,), (1,)), ((), ())), preferred_element_type=jnp.float32)


def inverse(rows, column, twist, across):
    lane = lax.broadcasted_iota(jnp.int32, rows.shape, 1)
    slot = lax.broadcasted_iota(jnp.int32, rows.shape, 0)
    rows = rows * jnp.where((lane == 0) & (slot == 0), 1.0, 2.0)
    apart = (lane == 0) & (slot < 2 * SPLIT) & (lax.rem(slot, SPLIT) >= SPLIT // 2)
    every = jnp.concatenate(
        [jnp.where(apart, 0.0, rows), jnp.where(apart, rows, 0.0)[: 2 * SPLIT]], axis=0
    )
    top, rest = halves(every)
    nothing = jnp.zeros((2 * LANES - 3 * TERMS, LANES), jnp.bfloat16)
    z = jnp.dot(
        column[...], jnp.concatenate([top, rest, top, nothing], axis=0), preferred_element_type=jnp.float32
    )
    z_re, z_im = z[:LANES], z[LANES:]
    c, s = twist[0], twist[1]
    y = jnp.concatenate([z_re * c - z_im * s, z_re * s + z_im * c], axis=1)
    top, rest = halves(y)
    return over_lanes(across[...], jnp.concatenate([top, rest, top], axis=1))


def kernel(chan, hour, x, taps, bin_ids, owners, *refs):
    tables, out = refs[:8], refs[8]
    held = refs[9:17]
    pick, high, low, turns, column, twist = held[:6]
    across, twice = held[6:]
    xin, tin, ids, ids_in, xd, td, fx, fh, spec, kron, part, first, early, outbox, inbox = refs[17:32]
    table_sem, own_sem, ids_send, ids_recv, t_send, t_recv, x_send, x_recv = refs[32:40]
    f_send, f_recv, send, recv, send2, recv2 = refs[40:]
    me, my_hour = lax.axis_index("chan"), lax.axis_index("hour")
    per = xin.shape[1]
    share = pl.ds(pl.multiple_of(my_hour * (tin.shape[2] // hour), LANES), tin.shape[2] // hour)

    def flipped(at, o, size):
        to, bit = at, 1
        while bit < size:
            to = to + lax.rem(lax.div(o, bit), 2) * bit * (1 - 2 * lax.rem(lax.div(at, bit), 2))
            bit *= 2
        return to

    def partner(o):
        return flipped(me, o, chan)

    def beside(o):
        return flipped(my_hour, o, hour)

    def sent(src, dst, sends, recvs, **device):
        return pltpu.make_async_remote_copy(
            src_ref=src, dst_ref=dst, send_sem=sends, recv_sem=recvs, device_id=device, device_id_type=MESH
        )

    loads = [pltpu.make_async_copy(src, dst, table_sem.at[z]) for z, (src, dst) in enumerate(zip(tables, held))]
    own = [
        pltpu.make_async_copy(x.at[me], xin.at[me], own_sem.at[0]),
        pltpu.make_async_copy(taps.at[me, :, share], tin.at[me, :, share], own_sem.at[1]),
    ]
    for copy in own + loads:
        copy.start()
    barrier = pltpu.get_barrier_semaphore()
    for o in range(1, hour):
        pl.semaphore_signal(
            barrier, inc=1, device_id={"hour": lax.rem(my_hour + o, hour)}, device_id_type=MESH
        )
    for o in range(1, chan):
        pl.semaphore_signal(barrier, inc=1, device_id={"chan": partner(o)}, device_id_type=MESH)
    place = lax.broadcasted_iota(jnp.int32, ids.shape, 1)
    labels = jnp.zeros(ids.shape, jnp.int32)
    for r in range(ROUNDS):
        live = (place == me * ROUNDS + r) & (me >= r + 1)
        labels = jnp.where(live, bin_ids[:, r : r + 1] + 1, labels)
    ids[...] = labels
    pl.semaphore_wait(barrier, chan + hour - 2)

    def x_copy(o):
        to = partner(o)
        return sent(x.at[to], xin.at[me], x_send.at[o], x_recv.at[o], chan=to)

    far_first = sorted(range(1, chan), key=lambda o: -(o.bit_length()))
    tap_copies, id_copies = [], []
    for o in far_first:
        to = partner(o)
        tap_copies.append(
            sent(taps.at[to, :, share], tin.at[me, :, share], t_send.at[o], t_recv.at[o], chan=to)
        )
        tap_copies[-1].start()
    for o in far_first:
        id_copies.append(sent(ids, ids_in.at[o], ids_send.at[o], ids_recv.at[o], chan=partner(o)))
        id_copies[-1].start()
    for o in range(1, chan):
        x_copy(o).start()
    lane0 = lax.broadcasted_iota(jnp.int32, (8, LANES), 1) == 0

    def spectra(block, t, edge):
        @pl.loop(0, per // 8)
        def _(g):
            piece = pl.ds(pl.multiple_of(8 * g, 8), 8)
            here = pl.ds(pl.multiple_of(block * per + 8 * g, 8), 8)

            def bins_of(f, rows):
                values, extra = [], []
                for n in range(SPLIT):
                    re = f[n, rows, pl.ds(pl.multiple_of(2 * t * LANES, LANES), LANES)]
                    im = f[n, rows, pl.ds(pl.multiple_of((2 * t + 1) * LANES, LANES), LANES)]
                    if edge:
                        angle = -math.pi * n / SPLIT
                        extra.append((im * math.cos(angle), im * math.sin(angle)))
                        im = jnp.where(lane0, 0.0, im)
                    if n == 0:
                        values.append((re, im))
                    else:
                        c, s = turns[t, n, 0], turns[t, n, 1]
                        values.append((re * c - im * s, re * s + im * c))
                found = small_dft(values, -1)
                if edge:
                    more = small_dft(extra, -1, half=True)
                    for k2 in range(SPLIT // 2):
                        old = found[SPLIT // 2 + k2]
                        found[SPLIT // 2 + k2] = tuple(
                            jnp.where(lane0, more[k2][z], old[z]) for z in range(2)
                        )
                return found

            freq = bins_of(fx, piece)
            resp = bins_of(fh, here)
            for k2 in range(SPLIT):
                (xr, xi), (hr, hi) = freq[k2], resp[k2]
                spec[t, k2, 0, here, :] = (xr * hr - xi * hi).astype(jnp.bfloat16).astype(jnp.float32)
                spec[t, k2, 1, here, :] = (xr * hi + xi * hr).astype(jnp.bfloat16).astype(jnp.float32)

    half = lax.broadcasted_iota(jnp.int32, (per, LANES), 1) < SHARE

    def transform_of(block):
        flat = jnp.concatenate([xin[block, :, q * PIECE : (q + 1) * PIECE] for q in range(FR // PIECE)], axis=0)
        got = jnp.dot(flat, pick[...], preferred_element_type=jnp.float32)
        for g in range(TILES):
            for n in range(SPLIT):
                a, b = (
                    got[q * per : (q + 1) * per, n // 2 * LANES : (n // 2 + 1) * LANES] for q in (2 * g, 2 * g + 1)
                )
                if n % 2:
                    a = pltpu.roll(a, SHARE, 1)
                else:
                    b = pltpu.roll(b, SHARE, 1)
                xd[n * per : (n + 1) * per, g * LANES : (g + 1) * LANES] = jnp.where(half, a, b).astype(jnp.bfloat16)
        found = jnp.dot(xd[...], high[...], preferred_element_type=jnp.float32) + jnp.dot(
            xd[...], low[...], preferred_element_type=jnp.float32
        )
        for n in range(SPLIT):
            fx[n] = found[n * per : (n + 1) * per]

    def spectra_of(block):
        spectra(block, 0, True)

        @pl.loop(1, TILES)
        def _(t):
            spectra(block, t, False)

    def take(block):
        transform_of(block)
        spectra_of(block)

    for copy in loads + own[:1]:
        copy.wait()
    transform_of(me)
    own[1].wait()
    for copy in tap_copies:
        copy.wait_recv()
    forwards = []
    for o in range(1, hour):
        to = lax.rem(my_hour + o, hour)
        forwards.append(sent(tin.at[:, :, share], tin.at[:, :, share], f_send.at[o], f_recv.at[o], hour=to))
        forwards[-1].start()
    for copy in id_copies:
        copy.wait_recv()
    labels = ids[...]
    for o in range(1, chan):
        labels = labels + ids_in[o]
    by_pair = rows_of_pairs(labels, owners)
    nbins = chan * hour
    pair = lax.broadcasted_iota(jnp.int32, (ids.shape[1], SLOTS), 0)
    column_of = lax.broadcasted_iota(jnp.int32, (ids.shape[1], SLOTS), 1)
    places = jnp.zeros(pair.shape, jnp.float32)
    for s in range(1, chan):
        for j in range(s):
            near, far = jnp.maximum(partner(s), partner(j)), jnp.minimum(partner(s), partner(j))
            held_by = jnp.where(near - far <= ROUNDS, near * ROUNDS + near - far - 1, -1)
            hit = (column_of == slot_of(s, j, chan)) & (pair == held_by)
            places = jnp.where(hit, 1.0, places)
    by_slot = jnp.dot(by_pair, places.astype(jnp.bfloat16), preferred_element_type=jnp.float32).astype(jnp.bfloat16)
    deep = 2 * SPLIT
    spread = (
        lax.div(lax.broadcasted_iota(jnp.int32, (nbins * deep, nbins), 0), deep)
        == lax.broadcasted_iota(jnp.int32, (nbins * deep, nbins), 1)
    ).astype(jnp.float32).astype(jnp.bfloat16)
    widen = (
        lax.div(lax.broadcasted_iota(jnp.int32, (SLOTS, SLOTS * deep), 1), deep)
        == lax.broadcasted_iota(jnp.int32, (SLOTS, SLOTS * deep), 0)
    ).astype(jnp.float32).astype(jnp.bfloat16)
    tall = jnp.dot(spread, by_slot, preferred_element_type=jnp.float32).astype(jnp.bfloat16)
    both = jnp.dot(tall, widen, preferred_element_type=jnp.float32)
    same = lax.rem(lax.broadcasted_iota(jnp.int32, both.shape, 0), deep) == lax.rem(
        lax.broadcasted_iota(jnp.int32, both.shape, 1), deep
    )
    kron[...] = jnp.where(same, both, 0.0).astype(jnp.bfloat16)

    def cross(t, near, far, slot):
        res, ims = [], []
        for k2 in range(SPLIT):
            re = im = None
            for c in range(per // 8):
                at = pl.ds(pl.multiple_of(near * per + 8 * c, 8), 8)
                of = pl.ds(pl.multiple_of(far * per + 8 * c, 8), 8)
                nr, ni = spec[t, k2, 0, at, :], spec[t, k2, 1, at, :]
                fr, fi = spec[t, k2, 0, of, :], spec[t, k2, 1, of, :]
                one, two = fr * nr + fi * ni, fi * nr - fr * ni
                re, im = (one, two) if re is None else (re + one, im + two)
            res.append(re)
            ims.append(im)
        part[t, slot] = jnp.concatenate([fold(res), fold(ims)], axis=0).astype(jnp.bfloat16)

    def crosses(s, begin):
        @pl.loop(0, s)
        def _(j):
            a, b = partner(s), partner(j)
            for t in range(TILES):
                cross(t, jnp.maximum(a, b), jnp.minimum(a, b), begin + j)

    def part_copy(z, o, begin, count):
        where = pl.ds(begin, count)
        return sent(part.at[beside(o), where], first.at[o, where], send.at[z, o], recv.at[z, o], hour=beside(o))

    groups = [(LATE, 6), (LATE + 6, 4), (LATE + 10, 5), (LATE + 15, 6), (0, 7)]
    order = [2, 3, 1, 0]
    for copy in forwards:
        copy.wait_recv()
    count = tin.shape[2]
    got = jnp.dot(tin[...].reshape(chan * per, count), twice[...], preferred_element_type=jnp.float32)
    for n in range(SPLIT):
        td[n] = got[:, n * LANES : (n + 1) * LANES].astype(jnp.bfloat16)
    found = jnp.dot(
        td[...].reshape(SPLIT * chan * per, LANES),
        jnp.concatenate([high[:SHARE, :], low[:SHARE, :]], axis=0),
        preferred_element_type=jnp.float32,
    )
    for n in range(SPLIT):
        fh[n] = found[n * chan * per : (n + 1) * chan * per]
    spectra_of(me)

    @pl.loop(1, chan // 2)
    def _(s):
        x_copy(s).wait_recv()
        take(partner(s))
        crosses(s, LATE + lax.div(s * (s - 1), 2))

    for o in order[:3]:
        part_copy(0, o, *groups[0]).start()

    @pl.loop(chan // 2, chan - 1)
    def _(s):
        x_copy(s).wait_recv()
        take(partner(s))
        crosses(s, LATE + lax.div(s * (s - 1), 2))

        for z in range(1, len(groups) - 1):

            @pl.when(s == z + 3)
            def _():
                for o in order[:3]:
                    part_copy(z, o, *groups[z]).start()

    x_copy(chan - 1).wait_recv()
    block = partner(chan - 1)
    transform_of(block)

    @pl.loop(0, TILES)
    def _(z):
        late = lax.div(z, 2)
        o = (1 - late) * (2 + z) + late * (3 - z)
        t = beside(o)

        @pl.when(t == 0)
        def _():
            spectra(block, 0, True)

        @pl.when(t > 0)
        def _():
            spectra(block, t, False)

        for j in range(chan - 1):
            cross(t, jnp.maximum(block, partner(j)), jnp.minimum(block, partner(j)), j)

        @pl.when(o > 0)
        def _():
            part_copy(4, o, *groups[4]).start()

    def mixed(begin, count, room):
        where = slice(begin, begin + count)
        total = part[my_hour, where].astype(jnp.float32)
        for o in range(1, hour):
            total = total + first[o, where].astype(jnp.float32)
        total = total.reshape(count * deep, LANES)
        if room > count:
            total = jnp.concatenate([total, jnp.zeros(((room - count) * deep, LANES), jnp.float32)], axis=0)
        got = jnp.dot(
            kron[:, begin * deep : (begin + room) * deep],
            jnp.concatenate(halves(total), axis=1),
            preferred_element_type=jnp.float32,
        )
        return got[:, :LANES] + got[:, LANES:]

    for z in range(len(groups) - 1):
        for o in range(1, hour):
            part_copy(z, o, *groups[z]).wait_recv()
    early[...] = mixed(LATE, 21, SLOTS - LATE)
    for o in range(1, hour):
        part_copy(4, o, *groups[4]).wait_recv()
    outbox[...] = (mixed(0, 7, LATE) + early[...]).astype(jnp.bfloat16).reshape(outbox.shape)
    for oc in far_first + [0]:
        for o in order:
            if oc or o:
                to, at = partner(oc), beside(o)
                sent(
                    outbox.at[to * hour + at],
                    inbox.at[oc * hour + my_hour],
                    send2.at[0],
                    recv2.at[0],
                    chan=to,
                    hour=at,
                ).start()
    inbox[my_hour] = outbox[me * hour + my_hour]
    for copy in tap_copies + id_copies + forwards:
        copy.wait_send()
    for o in range(1, chan):
        x_copy(o).wait_send()
    for z in range(len(groups)):
        for o in range(1, hour):
            part_copy(z, o, *groups[z]).wait_send()

    others = pl.ds(0, chan * hour - 1)
    all_rows = sent(outbox.at[others], inbox.at[others], send2.at[0], recv2.at[0], chan=partner(1))
    all_rows.wait_recv()
    rows = inbox[0:hour].astype(jnp.float32)
    for oc in range(1, chan):
        rows = rows + inbox[oc * hour : (oc + 1) * hour].astype(jnp.float32)
    wave = inverse(rows.reshape(TILES * deep, LANES), column, twist, across)
    for u in range(OUT_ROWS):
        out[:, u * LANES : (u + 1) * LANES] = wave[u : u + 1]
    all_rows.wait_send()


def split_body(traces, taps, bin_ids, owners):
    chan, hour = lax.axis_size("chan"), lax.axis_size("hour")
    channels, count = taps.shape
    per = channels // chan
    norm = 1.0 / (FR * math.sqrt(FR * hour * channels))
    high, low = two_parts(sub_tables())
    pick, twice = pick_tables()
    tables = [pick, high, low, turn_table(), column_table(), twist_table(), row_table(), twice]
    depth = LANES
    part = (hour, SLOTS, 2 * SPLIT, LANES)
    rows = (chan * hour, 2 * SPLIT, LANES)
    vmem, hbm = pl.BlockSpec(memory_space=pltpu.VMEM), pl.BlockSpec(memory_space=pl.ANY)
    sems = pltpu.SemaphoreType.DMA
    wave = pl.pallas_call(
        functools.partial(kernel, chan, hour),
        out_shape=jax.ShapeDtypeStruct((1, 2 * FR), jnp.float32),
        in_specs=[hbm, hbm, vmem, vmem] + [hbm] * len(tables),
        out_specs=vmem,
        scratch_shapes=[pltpu.VMEM(table.shape, table.dtype) for table in tables]
        + [
            pltpu.VMEM((chan, per, FR), jnp.bfloat16),
            pltpu.VMEM((chan, per, count), jnp.bfloat16),
            pltpu.VMEM((8, depth), jnp.int32),
            pltpu.VMEM((chan, 8, depth), jnp.int32),
            pltpu.VMEM((SPLIT * per, SUB), jnp.bfloat16),
            pltpu.VMEM((SPLIT, channels, LANES), jnp.bfloat16),
            pltpu.VMEM((SPLIT, per, 2 * SUB), jnp.float32),
            pltpu.VMEM((SPLIT, channels, 2 * SUB), jnp.float32),
            pltpu.VMEM((TILES, SPLIT, 2, channels, LANES), jnp.float32),
            pltpu.VMEM((rows[0] * rows[1], SLOTS * rows[1]), jnp.bfloat16),
            pltpu.VMEM(part, jnp.bfloat16),
            pltpu.VMEM(part, jnp.bfloat16),
            pltpu.VMEM((rows[0] * rows[1], LANES), jnp.float32),
            pltpu.VMEM(rows, jnp.bfloat16),
            pltpu.VMEM(rows, jnp.bfloat16),
            sems((len(tables),)),
            sems((2,)),
        ]
        + [sems((chan,))] * 6
        + [sems((hour,))] * 2
        + [sems((5, hour))] * 2
        + [sems((1,))] * 2,
        compiler_params=pltpu.CompilerParams(
            collective_id=0, has_side_effects=True, vmem_limit_bytes=56 * 2**20
        ),
    )(
        traces.reshape(chan, per, FR),
        taps.reshape(chan, per, count),
        bin_ids.T,
        owners.reshape(1, -1),
        *[jnp.asarray(table) for table in tables],
    )
    return wave * norm


def solution(mesh):
    placed = (P("chan", "hour"), P("chan", None), P(None, "chan"), P())

    def whole(traces, taps, bin_ids, owners):
        chan, hour = mesh.shape["chan"], mesh.shape["hour"]
        channels = traces.shape[0] // chan
        fits = (
            chan == 8
            and hour == TILES
            and channels % (16 * chan) == 0
            and traces.shape[1] == hour * FR
            and taps.shape[1] == SPLIT * LANES // 2
            and owners.shape[0] == chan * hour
        )
        return jax.shard_map(
            split_body if fits else body,
            mesh=mesh,
            in_specs=placed,
            out_specs=P(("chan", "hour"), None),
            check_vma=False,
        )(traces, taps, bin_ids, owners)

    return whole
```

```python
import functools
import math

import jax
import jax.numpy as jnp
import numpy as np
from jax import lax
from jax.experimental import pallas as pl
from jax.experimental.pallas import tpu as pltpu
from jax.sharding import PartitionSpec as P

FR = 4096
ROUNDS = 4
MESH = pl.DeviceIdType.MESH


exact = lax.Precision.HIGHEST

def passed_along(shard, axis, by):
    devices = lax.axis_size(axis)
    pairs = [(i, i + by) for i in range(devices) if 0 <= i + by < devices]
    return lax.ppermute(shard, axis, pairs)


def transform(real_part, imag_part, count):
    span = real_part.shape[-1]
    inner = 2 * span // 128
    lead = real_part.shape[:-1]
    first = jnp.arange(64, dtype=jnp.float32)[:, None]
    middle = jnp.arange(128, dtype=jnp.float32)[None, :]
    angle_one = 2.0 * math.pi / 128.0 * jnp.mod(first * middle, 128.0)
    cos_one = jnp.cos(angle_one)
    sin_one = -jnp.sin(angle_one)
    second = jnp.arange(inner, dtype=jnp.float32)[:, None]
    angle_turn = 2.0 * math.pi / (128.0 * inner) * jnp.mod(second * middle, 128.0 * inner)
    cos_turn = jnp.cos(angle_turn)
    sin_turn = -jnp.sin(angle_turn)
    outer = jnp.arange(count // 128, dtype=jnp.float32)[None, :]
    angle_two = 2.0 * math.pi / inner * jnp.mod(second * outer, float(inner))
    cos_two = jnp.cos(angle_two)
    sin_two = -jnp.sin(angle_two)
    grid = real_part.reshape(lead + (64, inner))
    section_re = jnp.einsum("...an,ak->...nk", grid, cos_one, precision=exact)
    section_im = jnp.einsum("...an,ak->...nk", grid, sin_one, precision=exact)
    if imag_part is not None:
        grid_im = imag_part.reshape(lead + (64, inner))
        section_re = section_re - jnp.einsum("...an,ak->...nk", grid_im, sin_one, precision=exact)
        section_im = section_im + jnp.einsum("...an,ak->...nk", grid_im, cos_one, precision=exact)
    turned_re = section_re * cos_turn - section_im * sin_turn
    turned_im = section_re * sin_turn + section_im * cos_turn
    out_re = jnp.einsum("...nk,nm->...mk", turned_re, cos_two, precision=exact) - jnp.einsum(
        "...nk,nm->...mk", turned_im, sin_two, precision=exact
    )
    out_im = jnp.einsum("...nk,nm->...mk", turned_re, sin_two, precision=exact) + jnp.einsum(
        "...nk,nm->...mk", turned_im, cos_two, precision=exact
    )
    return (out_re.reshape(lead + (count,)), out_im.reshape(lead + (count,)))


def filtered(samples, filters):
    channels = samples.shape[0]
    frames = samples.shape[1] // FR
    signal = samples.astype(jnp.float32).reshape(channels, frames, FR)
    freq_re, freq_im = transform(signal, None, FR)
    padded_taps = jnp.pad(filters.astype(jnp.float32), ((0, 0), (0, FR - filters.shape[1])))
    resp_re, resp_im = transform(padded_taps, None, FR)
    resp_re = resp_re[:, None, :]
    resp_im = resp_im[:, None, :]
    spec_re = (freq_re * resp_re - freq_im * resp_im).astype(jnp.bfloat16)
    spec_im = (freq_re * resp_im + freq_im * resp_re).astype(jnp.bfloat16)
    return (spec_re, spec_im)


def body(traces, taps, bin_ids, owners):
    channels = traces.shape[0]
    frames = traces.shape[1] // FR
    spec_re, spec_im = filtered(traces, taps)
    mine = lax.axis_index("chan")
    near_re = spec_re.astype(jnp.float32)
    near_im = spec_im.astype(jnp.float32)
    results = []
    for offset in range(ROUNDS):
        far_re, far_im = passed_along((spec_re, spec_im), "chan", offset + 1)
        far_re = far_re.astype(jnp.float32)
        far_im = far_im.astype(jnp.float32)
        cross_re = jnp.sum(far_re * near_re + far_im * near_im, axis=(0, 1))
        cross_im = jnp.sum(far_im * near_re - far_re * near_im, axis=(0, 1))
        results.append(jnp.stack([cross_re, cross_im]))
    contrib = jnp.stack(results)
    nbins = owners.shape[0]
    own_bins = bin_ids[:, 0]
    labels = jnp.arange(nbins, dtype=jnp.int32)
    places = jnp.sum(jnp.where(own_bins[:, None] == labels[None, :], owners[None, :], 0), axis=1)
    valid = jnp.arange(ROUNDS, dtype=jnp.int32) < mine
    places = jnp.where(valid, places, -1)
    width = contrib.shape[2]
    flat = contrib.reshape(ROUNDS, 2 * width)
    per_device = nbins // lax.axis_size("chan")
    rows = jnp.arange(lax.axis_size("chan") * per_device, dtype=jnp.int32)
    onehot = (places[None, :] == rows[:, None]).astype(jnp.float32)
    stacked = lax.psum_scatter(
        jnp.dot(onehot, flat, precision=exact, preferred_element_type=jnp.float32),
        "chan",
        scatter_dimension=0,
        tiled=True,
    )
    stacked = stacked.reshape(per_device, 2, width)
    final = lax.psum_scatter(stacked, "hour", scatter_dimension=0, tiled=True)
    weights = jnp.where(jnp.arange(FR) == 0, 1.0, 2.0).astype(jnp.float32)
    wave_re, wave_im = transform(final[:, 0] * weights, -final[:, 1] * weights, 2 * FR)
    norm = 1.0 / (FR * math.sqrt(FR * lax.axis_size("hour") * frames * channels))
    return wave_re * norm

SPLIT = 8
SUB = FR // SPLIT
LANES = 128
TILES = SUB // LANES


def sub_tables():
    a = np.arange(SUB)[:, None]
    k1 = np.arange(SUB)[None, :]
    turn = 2.0 * np.pi * ((a * k1) % (2 * SUB)) / (2 * SUB)
    cos, sin = np.cos(turn), -np.sin(turn)
    sin[:, 0] = 1.0 - 2.0 * (np.arange(SUB) % 2)
    table = np.stack([cos.reshape(SUB, TILES, LANES), sin.reshape(SUB, TILES, LANES)], axis=2)
    return table.reshape(SUB, 2 * SUB)


def two_parts(table):
    high = table.astype(jnp.bfloat16)
    low = (table - high.astype(np.float64)).astype(jnp.bfloat16)
    return high, low


PIECE = 512
SHARE = PIECE // SPLIT


def pick_tables():
    table = np.zeros((PIECE, SPLIT, 2, SHARE), np.float32)
    for n in range(SPLIT):
        for b in range(SHARE):
            table[SPLIT * b + n, n, :, b] = 1.0
    twice = table.reshape(PIECE, 2 * PIECE).astype(jnp.bfloat16)
    return np.ascontiguousarray(table[:, :, 0].reshape(PIECE, PIECE)).astype(jnp.bfloat16), twice


def turn_table():
    n = np.arange(SPLIT)[:, None]
    k1 = np.arange(SUB)[None, :]
    turn = 2.0 * np.pi * n * k1 / (2 * FR)
    table = np.stack([np.cos(turn), -np.sin(turn)], axis=1).reshape(SPLIT, 2, TILES, 1, LANES)
    table = np.broadcast_to(table.transpose(2, 0, 1, 3, 4), (TILES, SPLIT, 2, 8, LANES))
    return np.ascontiguousarray(table).astype(np.float32)


def times(value, angle):
    re, im = value
    c, s = math.cos(angle), math.sin(angle)
    if abs(s) < 1e-12:
        return (re, im) if c > 0 else (-re, -im)
    if abs(c) < 1e-12:
        return (-im, re) if s > 0 else (im, -re)
    if abs(abs(c) - abs(s)) < 1e-12:
        root = abs(c)
        p, q = math.copysign(1.0, c), math.copysign(1.0, s)
        first = (re if p > 0 else -re) + (-im if q > 0 else im)
        second = (re if q > 0 else -re) + (im if p > 0 else -im)
        return first * root, second * root
    return re * c - im * s, re * s + im * c


def small_dft(values, sign, half=False):
    size = len(values)
    if size == 1:
        return values
    even = small_dft(values[0::2], sign)
    odd = small_dft(values[1::2], sign)
    low, high = [], []
    for k in range(size // 2):
        turned = times(odd[k], sign * 2.0 * math.pi * k / size)
        low.append((even[k][0] + turned[0], even[k][1] + turned[1]))
        if not half:
            high.append((even[k][0] - turned[0], even[k][1] - turned[1]))
    return low + high


LATE = 8
SLOTS = 32


def slot_of(step, before, chan):
    if isinstance(step, int) and step == chan - 1:
        return before
    return LATE + step * (step - 1) // 2 + before


def rows_of_pairs(ids, owners):
    depth = ids.shape[1]
    nbins = owners.shape[1]
    bins = lax.broadcasted_iota(jnp.int32, (nbins, depth), 0) + 1
    picked = (bins == ids[0:1, :]).astype(jnp.float32).astype(jnp.bfloat16)
    row = lax.broadcasted_iota(jnp.int32, (nbins, nbins), 0)
    moved = (row == owners[...]).astype(jnp.float32).astype(jnp.bfloat16)
    return jnp.dot(moved, picked, preferred_element_type=jnp.float32).astype(jnp.bfloat16)


def fold(values):
    sublane = lax.broadcasted_iota(jnp.int32, values[0].shape, 0)
    shift = 1
    while len(values) > 1:
        first = lax.rem(lax.div(sublane, shift), 2) == 0
        values = [
            jnp.where(first, a, b) + pltpu.roll(jnp.where(first, b, a), SPLIT - shift, 0)
            for a, b in zip(values[0::2], values[1::2])
        ]
        shift *= 2
    return values[0]


OUT_ROWS = 2 * FR // LANES
TERMS = 2 * SPLIT * (TILES + 1)


def column_table():
    v = np.arange(LANES)[:, None]
    t, k2 = np.arange(TILES)[None, :, None], np.arange(SPLIT)[None, None, :]
    main = 2.0 * np.pi * ((v[:, :, None] * (SPLIT * k2 + t)) % OUT_ROWS) / OUT_ROWS
    extra = 2.0 * np.pi * ((v * (SPLIT // 2 + SPLIT * (np.arange(SPLIT)[None, :] - SPLIT // 2))) % OUT_ROWS) / OUT_ROWS
    phase = np.concatenate([main, extra[:, None, :]], axis=1)
    top = np.stack([np.cos(phase), -np.sin(phase)], axis=2).reshape(LANES, TERMS)
    under = np.stack([np.sin(phase), np.cos(phase)], axis=2).reshape(LANES, TERMS)
    high, low = two_parts(np.concatenate([top, under], axis=0))
    rest = np.zeros((2 * LANES, 2 * LANES - 3 * TERMS), jnp.bfloat16)
    return np.concatenate([high, high, low, rest], axis=1)


def twist_table():
    turn = 2.0 * np.pi * np.arange(LANES)[:, None] * np.arange(LANES)[None, :] / (2 * FR)
    return np.stack([np.cos(turn), np.sin(turn)]).astype(np.float32)


def row_table():
    turn = 2.0 * np.pi * ((np.arange(OUT_ROWS)[:, None] * np.arange(LANES)[None, :]) % OUT_ROWS) / OUT_ROWS
    high, low = two_parts(np.concatenate([np.cos(turn), -np.sin(turn)], axis=1))
    return np.concatenate([high, high, low], axis=1)


def halves(value):
    top = value.astype(jnp.bfloat16)
    return top, (value - top.astype(jnp.float32)).astype(jnp.bfloat16)


def over_lanes(a, b):
    return lax.dot_general(a, b, (((1,), (1,)), ((), ())), preferred_element_type=jnp.float32)


def inverse(rows, column, twist, across):
    lane = lax.broadcasted_iota(jnp.int32, rows.shape, 1)
    slot = lax.broadcasted_iota(jnp.int32, rows.shape, 0)
    rows = rows * jnp.where((lane == 0) & (slot == 0), 1.0, 2.0)
    apart = (lane == 0) & (slot < 2 * SPLIT) & (lax.rem(slot, SPLIT) >= SPLIT // 2)
    every = jnp.concatenate(
        [jnp.where(apart, 0.0, rows), jnp.where(apart, rows, 0.0)[: 2 * SPLIT]], axis=0
    )
    top, rest = halves(every)
    nothing = jnp.zeros((2 * LANES - 3 * TERMS, LANES), jnp.bfloat16)
    z = jnp.dot(
        column[...], jnp.concatenate([top, rest, top, nothing], axis=0), preferred_element_type=jnp.float32
    )
    z_re, z_im = z[:LANES], z[LANES:]
    c, s = twist[0], twist[1]
    y = jnp.concatenate([z_re * c - z_im * s, z_re * s + z_im * c], axis=1)
    top, rest = halves(y)
    return over_lanes(across[...], jnp.concatenate([top, rest, top], axis=1))


def kernel(chan, hour, x, taps, bin_ids, owners, *refs):
    tables, out = refs[:8], refs[8]
    held = refs[9:17]
    pick, high, low, turns, column, twist = held[:6]
    across, twice = held[6:]
    xin, tin, ids, ids_in, xd, td, fx, fh, spec, kron, part, first, early, outbox, inbox = refs[17:32]
    table_sem, own_sem, ids_send, ids_recv, t_send, t_recv, x_send, x_recv = refs[32:40]
    f_send, f_recv, send, recv, send2, recv2 = refs[40:]
    me, my_hour = lax.axis_index("chan"), lax.axis_index("hour")
    per = xin.shape[1]
    share = pl.ds(pl.multiple_of(my_hour * (tin.shape[2] // hour), LANES), tin.shape[2] // hour)

    def flipped(at, o, size):
        to, bit = at, 1
        while bit < size:
            to = to + lax.rem(lax.div(o, bit), 2) * bit * (1 - 2 * lax.rem(lax.div(at, bit), 2))
            bit *= 2
        return to

    def partner(o):
        return flipped(me, o, chan)

    def beside(o):
        return flipped(my_hour, o, hour)

    def sent(src, dst, sends, recvs, **device):
        return pltpu.make_async_remote_copy(
            src_ref=src, dst_ref=dst, send_sem=sends, recv_sem=recvs, device_id=device, device_id_type=MESH
        )

    loads = [pltpu.make_async_copy(src, dst, table_sem.at[z]) for z, (src, dst) in enumerate(zip(tables, held))]
    own = [
        pltpu.make_async_copy(x.at[me], xin.at[me], own_sem.at[0]),
        pltpu.make_async_copy(taps.at[me, :, share], tin.at[me, :, share], own_sem.at[1]),
    ]
    barrier = pltpu.get_barrier_semaphore()
    for o in range(1, hour):
        pl.semaphore_signal(
            barrier, inc=1, device_id={"hour": lax.rem(my_hour + o, hour)}, device_id_type=MESH
        )
    for o in range(1, chan):
        pl.semaphore_signal(barrier, inc=1, device_id={"chan": partner(o)}, device_id_type=MESH)
    for copy in own + loads:
        copy.start()
    place = lax.broadcasted_iota(jnp.int32, ids.shape, 1)
    labels = jnp.zeros(ids.shape, jnp.int32)
    for r in range(ROUNDS):
        live = (place == me * ROUNDS + r) & (me >= r + 1)
        labels = jnp.where(live, bin_ids[:, r : r + 1] + 1, labels)
    ids[...] = labels
    pl.semaphore_wait(barrier, chan + hour - 2)

    def x_copy(o):
        to = partner(o)
        return sent(x.at[to], xin.at[me], x_send.at[o], x_recv.at[o], chan=to)

    far_first = sorted(range(1, chan), key=lambda o: -(o.bit_length()))
    tap_copies, id_copies = [], []
    for o in far_first:
        to = partner(o)
        tap_copies.append(
            sent(taps.at[to, :, share], tin.at[me, :, share], t_send.at[o], t_recv.at[o], chan=to)
        )
        tap_copies[-1].start()
    for o in far_first:
        id_copies.append(
            sent(ids.at[0:1], ids_in.at[o, 0:1], ids_send.at[o], ids_recv.at[o], chan=partner(o))
        )
        id_copies[-1].start()
    for o in range(1, chan):
        x_copy(o).start()
    lane0 = lax.broadcasted_iota(jnp.int32, (8, LANES), 1) == 0

    def spectra(block, t, edge):
        @pl.loop(0, per // 8)
        def _(g):
            piece = pl.ds(pl.multiple_of(8 * g, 8), 8)
            here = pl.ds(pl.multiple_of(block * per + 8 * g, 8), 8)

            def bins_of(f, rows):
                values, extra = [], []
                for n in range(SPLIT):
                    re = f[n, rows, pl.ds(pl.multiple_of(2 * t * LANES, LANES), LANES)]
                    im = f[n, rows, pl.ds(pl.multiple_of((2 * t + 1) * LANES, LANES), LANES)]
                    if edge:
                        angle = -math.pi * n / SPLIT
                        extra.append((im * math.cos(angle), im * math.sin(angle)))
                        im = jnp.where(lane0, 0.0, im)
                    if n == 0:
                        values.append((re, im))
                    else:
                        c, s = turns[t, n, 0], turns[t, n, 1]
                        values.append((re * c - im * s, re * s + im * c))
                found = small_dft(values, -1)
                if edge:
                    more = small_dft(extra, -1, half=True)
                    for k2 in range(SPLIT // 2):
                        old = found[SPLIT // 2 + k2]
                        found[SPLIT // 2 + k2] = tuple(
                            jnp.where(lane0, more[k2][z], old[z]) for z in range(2)
                        )
                return found

            freq = bins_of(fx, piece)
            resp = bins_of(fh, here)
            for k2 in range(SPLIT):
                (xr, xi), (hr, hi) = freq[k2], resp[k2]
                spec[t, k2, 0, here, :] = (xr * hr - xi * hi).astype(jnp.bfloat16).astype(jnp.float32)
                spec[t, k2, 1, here, :] = (xr * hi + xi * hr).astype(jnp.bfloat16).astype(jnp.float32)

    half = lax.broadcasted_iota(jnp.int32, (per, LANES), 1) < SHARE

    def transform_of(block):
        flat = jnp.concatenate([xin[block, :, q * PIECE : (q + 1) * PIECE] for q in range(FR // PIECE)], axis=0)
        got = jnp.dot(flat, pick[...], preferred_element_type=jnp.float32)
        for g in range(TILES):
            for n in range(SPLIT):
                a, b = (
                    got[q * per : (q + 1) * per, n // 2 * LANES : (n // 2 + 1) * LANES] for q in (2 * g, 2 * g + 1)
                )
                if n % 2:
                    a = pltpu.roll(a, SHARE, 1)
                else:
                    b = pltpu.roll(b, SHARE, 1)
                xd[n * per : (n + 1) * per, g * LANES : (g + 1) * LANES] = jnp.where(half, a, b).astype(jnp.bfloat16)
        found = jnp.dot(xd[...], high[...], preferred_element_type=jnp.float32) + jnp.dot(
            xd[...], low[...], preferred_element_type=jnp.float32
        )
        for n in range(SPLIT):
            fx[n] = found[n * per : (n + 1) * per]

    def spectra_of(block):
        spectra(block, 0, True)

        @pl.loop(1, TILES)
        def _(t):
            spectra(block, t, False)

    def take(block):
        transform_of(block)
        spectra_of(block)

    for copy in loads + own[:1]:
        copy.wait()
    transform_of(me)
    own[1].wait()
    for copy in tap_copies:
        copy.wait_recv()
    forwards = []
    for o in range(1, hour):
        to = lax.rem(my_hour + o, hour)
        forwards.append(sent(tin.at[:, :, share], tin.at[:, :, share], f_send.at[o], f_recv.at[o], hour=to))
        forwards[-1].start()
    for copy in id_copies:
        copy.wait_recv()
    labels = ids[0:1, :]
    for o in range(1, chan):
        labels = labels + ids_in[o, 0:1, :]
    by_pair = rows_of_pairs(labels, owners)
    nbins = chan * hour
    pair = lax.broadcasted_iota(jnp.int32, (ids.shape[1], SLOTS), 0)
    column_of = lax.broadcasted_iota(jnp.int32, (ids.shape[1], SLOTS), 1)
    places = jnp.zeros(pair.shape, jnp.float32)
    for s in range(1, chan):
        for j in range(s):
            near, far = jnp.maximum(partner(s), partner(j)), jnp.minimum(partner(s), partner(j))
            held_by = jnp.where(near - far <= ROUNDS, near * ROUNDS + near - far - 1, -1)
            hit = (column_of == slot_of(s, j, chan)) & (pair == held_by)
            places = jnp.where(hit, 1.0, places)
    by_slot = jnp.dot(by_pair, places.astype(jnp.bfloat16), preferred_element_type=jnp.float32).astype(jnp.bfloat16)
    deep = 2 * SPLIT
    spread = (
        lax.div(lax.broadcasted_iota(jnp.int32, (nbins * deep, nbins), 0), deep)
        == lax.broadcasted_iota(jnp.int32, (nbins * deep, nbins), 1)
    ).astype(jnp.float32).astype(jnp.bfloat16)
    widen = (
        lax.div(lax.broadcasted_iota(jnp.int32, (SLOTS, SLOTS * deep), 1), deep)
        == lax.broadcasted_iota(jnp.int32, (SLOTS, SLOTS * deep), 0)
    ).astype(jnp.float32).astype(jnp.bfloat16)
    tall = jnp.dot(spread, by_slot, preferred_element_type=jnp.float32).astype(jnp.bfloat16)
    both = jnp.dot(tall, widen, preferred_element_type=jnp.float32)
    same = lax.rem(lax.broadcasted_iota(jnp.int32, both.shape, 0), deep) == lax.rem(
        lax.broadcasted_iota(jnp.int32, both.shape, 1), deep
    )
    kron[...] = jnp.where(same, both, 0.0).astype(jnp.bfloat16)

    def cross(t, near, far, slot):
        res, ims = [], []
        for k2 in range(SPLIT):
            re = im = None
            for c in range(per // 8):
                at = pl.ds(pl.multiple_of(near * per + 8 * c, 8), 8)
                of = pl.ds(pl.multiple_of(far * per + 8 * c, 8), 8)
                nr, ni = spec[t, k2, 0, at, :], spec[t, k2, 1, at, :]
                fr, fi = spec[t, k2, 0, of, :], spec[t, k2, 1, of, :]
                one, two = fr * nr + fi * ni, fi * nr - fr * ni
                re, im = (one, two) if re is None else (re + one, im + two)
            res.append(re)
            ims.append(im)
        part[t, slot] = jnp.concatenate([fold(res), fold(ims)], axis=0).astype(jnp.bfloat16)

    def crosses(s, begin):
        @pl.loop(0, s)
        def _(j):
            a, b = partner(s), partner(j)
            for t in range(TILES):
                cross(t, jnp.maximum(a, b), jnp.minimum(a, b), begin + j)

    def part_copy(z, o, begin, count):
        where = pl.ds(begin, count)
        return sent(part.at[beside(o), where], first.at[o, where], send.at[z, o], recv.at[z, o], hour=beside(o))

    groups = [(LATE, 6), (LATE + 6, 4), (LATE + 10, 5), (LATE + 15, 6), (0, 7)]
    order = [2, 3, 1, 0]
    for copy in forwards:
        copy.wait_recv()
    count = tin.shape[2]
    got = jnp.dot(tin[...].reshape(chan * per, count), twice[...], preferred_element_type=jnp.float32)
    for n in range(SPLIT):
        td[n] = got[:, n * LANES : (n + 1) * LANES].astype(jnp.bfloat16)
    found = jnp.dot(
        td[...].reshape(SPLIT * chan * per, LANES),
        jnp.concatenate([high[:SHARE, :], low[:SHARE, :]], axis=0),
        preferred_element_type=jnp.float32,
    )
    for n in range(SPLIT):
        fh[n] = found[n * chan * per : (n + 1) * chan * per]
    spectra_of(me)

    @pl.loop(1, chan // 2)
    def _(s):
        x_copy(s).wait_recv()
        take(partner(s))
        crosses(s, LATE + lax.div(s * (s - 1), 2))

    for o in order[:3]:
        part_copy(0, o, *groups[0]).start()

    @pl.loop(chan // 2, chan - 1)
    def _(s):
        x_copy(s).wait_recv()
        take(partner(s))
        crosses(s, LATE + lax.div(s * (s - 1), 2))

        for z in range(1, len(groups) - 1):

            @pl.when(s == z + 3)
            def _():
                for o in order[:3]:
                    part_copy(z, o, *groups[z]).start()

    x_copy(chan - 1).wait_recv()
    block = partner(chan - 1)
    transform_of(block)

    @pl.loop(0, TILES)
    def _(z):
        late = lax.div(z, 2)
        o = (1 - late) * (2 + z) + late * (3 - z)
        t = beside(o)

        @pl.when(t == 0)
        def _():
            spectra(block, 0, True)

        @pl.when(t > 0)
        def _():
            spectra(block, t, False)

        for j in range(chan - 1):
            cross(t, jnp.maximum(block, partner(j)), jnp.minimum(block, partner(j)), j)

        @pl.when(o > 0)
        def _():
            part_copy(4, o, *groups[4]).start()

    def mixed(begin, count, room):
        where = slice(begin, begin + count)
        total = part[my_hour, where].astype(jnp.float32)
        for o in range(1, hour):
            total = total + first[o, where].astype(jnp.float32)
        total = total.reshape(count * deep, LANES)
        if room > count:
            total = jnp.concatenate([total, jnp.zeros(((room - count) * deep, LANES), jnp.float32)], axis=0)
        got = jnp.dot(
            kron[:, begin * deep : (begin + room) * deep],
            jnp.concatenate(halves(total), axis=1),
            preferred_element_type=jnp.float32,
        )
        return got[:, :LANES] + got[:, LANES:]

    for z in range(len(groups) - 1):
        for o in range(1, hour):
            part_copy(z, o, *groups[z]).wait_recv()
    early[...] = mixed(LATE, 21, SLOTS - LATE)
    for o in range(1, hour):
        part_copy(4, o, *groups[4]).wait_recv()
    outbox[...] = (mixed(0, 7, LATE) + early[...]).astype(jnp.bfloat16).reshape(outbox.shape)
    for oc in far_first + [0]:
        for o in order:
            if oc or o:
                to, at = partner(oc), beside(o)
                sent(
                    outbox.at[to * hour + at],
                    inbox.at[oc * hour + my_hour],
                    send2.at[0],
                    recv2.at[0],
                    chan=to,
                    hour=at,
                ).start()
    inbox[my_hour] = outbox[me * hour + my_hour]
    for copy in tap_copies + id_copies + forwards:
        copy.wait_send()
    for o in range(1, chan):
        x_copy(o).wait_send()
    for z in range(len(groups)):
        for o in range(1, hour):
            part_copy(z, o, *groups[z]).wait_send()

    others = pl.ds(0, chan * hour - 1)
    all_rows = sent(outbox.at[others], inbox.at[others], send2.at[0], recv2.at[0], chan=partner(1))
    all_rows.wait_recv()
    rows = inbox[0:hour].astype(jnp.float32)
    for oc in range(1, chan):
        rows = rows + inbox[oc * hour : (oc + 1) * hour].astype(jnp.float32)
    wave = inverse(rows.reshape(TILES * deep, LANES), column, twist, across)
    out[...] = wave
    all_rows.wait_send()


def split_body(traces, taps, bin_ids, owners):
    chan, hour = lax.axis_size("chan"), lax.axis_size("hour")
    channels, count = taps.shape
    per = channels // chan
    norm = 1.0 / (FR * math.sqrt(FR * hour * channels))
    high, low = two_parts(sub_tables())
    pick, twice = pick_tables()
    tables = [pick, high, low, turn_table(), column_table(), twist_table(), row_table(), twice]
    depth = LANES
    part = (hour, SLOTS, 2 * SPLIT, LANES)
    rows = (chan * hour, 2 * SPLIT, LANES)
    vmem, hbm = pl.BlockSpec(memory_space=pltpu.VMEM), pl.BlockSpec(memory_space=pl.ANY)
    sems = pltpu.SemaphoreType.DMA
    wave = pl.pallas_call(
        functools.partial(kernel, chan, hour),
        out_shape=pltpu.VMEM((OUT_ROWS, LANES), jnp.float32),
        in_specs=[hbm, hbm, vmem, vmem] + [hbm] * len(tables),
        out_specs=vmem,
        scratch_shapes=[pltpu.VMEM(table.shape, table.dtype) for table in tables]
        + [
            pltpu.VMEM((chan, per, FR), jnp.bfloat16),
            pltpu.VMEM((chan, per, count), jnp.bfloat16),
            pltpu.VMEM((8, depth), jnp.int32),
            pltpu.VMEM((chan, 8, depth), jnp.int32),
            pltpu.VMEM((SPLIT * per, SUB), jnp.bfloat16),
            pltpu.VMEM((SPLIT, channels, LANES), jnp.bfloat16),
            pltpu.VMEM((SPLIT, per, 2 * SUB), jnp.float32),
            pltpu.VMEM((SPLIT, channels, 2 * SUB), jnp.float32),
            pltpu.VMEM((TILES, SPLIT, 2, channels, LANES), jnp.float32),
            pltpu.VMEM((rows[0] * rows[1], SLOTS * rows[1]), jnp.bfloat16),
            pltpu.VMEM(part, jnp.bfloat16),
            pltpu.VMEM(part, jnp.bfloat16),
            pltpu.VMEM((rows[0] * rows[1], LANES), jnp.float32),
            pltpu.VMEM(rows, jnp.bfloat16),
            pltpu.VMEM(rows, jnp.bfloat16),
            sems((len(tables),)),
            sems((2,)),
        ]
        + [sems((chan,))] * 6
        + [sems((hour,))] * 2
        + [sems((5, hour))] * 2
        + [sems((1,))] * 2,
        compiler_params=pltpu.CompilerParams(
            collective_id=0, has_side_effects=True, vmem_limit_bytes=56 * 2**20
        ),
    )(
        traces.reshape(chan, per, FR),
        taps.reshape(chan, per, count),
        bin_ids.T,
        owners.reshape(1, -1),
        *[jnp.asarray(table) for table in tables],
    )
    return (wave * norm).reshape(1, 2 * FR)


def solution(mesh):
    placed = (P("chan", "hour"), P("chan", None), P(None, "chan"), P())

    def whole(traces, taps, bin_ids, owners):
        chan, hour = mesh.shape["chan"], mesh.shape["hour"]
        channels = traces.shape[0] // chan
        fits = (
            chan == 8
            and hour == TILES
            and channels % (16 * chan) == 0
            and traces.shape[1] == hour * FR
            and taps.shape[1] == SPLIT * LANES // 2
            and owners.shape[0] == chan * hour
        )
        return jax.shard_map(
            split_body if fits else body,
            mesh=mesh,
            in_specs=placed,
            out_specs=P(("chan", "hour"), None),
            check_vma=False,
        )(traces, taps, bin_ids, owners)

    return whole
```

```python
import functools
import math

import jax
import jax.numpy as jnp
import numpy as np
from jax import lax
from jax.experimental import pallas as pl
from jax.experimental.pallas import tpu as pltpu
from jax.sharding import PartitionSpec as P

FR = 4096
ROUNDS = 4
MESH = pl.DeviceIdType.MESH


exact = lax.Precision.HIGHEST

def passed_along(shard, axis, by):
    devices = lax.axis_size(axis)
    pairs = [(i, i + by) for i in range(devices) if 0 <= i + by < devices]
    return lax.ppermute(shard, axis, pairs)


def transform(real_part, imag_part, count):
    span = real_part.shape[-1]
    inner = 2 * span // 128
    lead = real_part.shape[:-1]
    first = jnp.arange(64, dtype=jnp.float32)[:, None]
    middle = jnp.arange(128, dtype=jnp.float32)[None, :]
    angle_one = 2.0 * math.pi / 128.0 * jnp.mod(first * middle, 128.0)
    cos_one = jnp.cos(angle_one)
    sin_one = -jnp.sin(angle_one)
    second = jnp.arange(inner, dtype=jnp.float32)[:, None]
    angle_turn = 2.0 * math.pi / (128.0 * inner) * jnp.mod(second * middle, 128.0 * inner)
    cos_turn = jnp.cos(angle_turn)
    sin_turn = -jnp.sin(angle_turn)
    outer = jnp.arange(count // 128, dtype=jnp.float32)[None, :]
    angle_two = 2.0 * math.pi / inner * jnp.mod(second * outer, float(inner))
    cos_two = jnp.cos(angle_two)
    sin_two = -jnp.sin(angle_two)
    grid = real_part.reshape(lead + (64, inner))
    section_re = jnp.einsum("...an,ak->...nk", grid, cos_one, precision=exact)
    section_im = jnp.einsum("...an,ak->...nk", grid, sin_one, precision=exact)
    if imag_part is not None:
        grid_im = imag_part.reshape(lead + (64, inner))
        section_re = section_re - jnp.einsum("...an,ak->...nk", grid_im, sin_one, precision=exact)
        section_im = section_im + jnp.einsum("...an,ak->...nk", grid_im, cos_one, precision=exact)
    turned_re = section_re * cos_turn - section_im * sin_turn
    turned_im = section_re * sin_turn + section_im * cos_turn
    out_re = jnp.einsum("...nk,nm->...mk", turned_re, cos_two, precision=exact) - jnp.einsum(
        "...nk,nm->...mk", turned_im, sin_two, precision=exact
    )
    out_im = jnp.einsum("...nk,nm->...mk", turned_re, sin_two, precision=exact) + jnp.einsum(
        "...nk,nm->...mk", turned_im, cos_two, precision=exact
    )
    return (out_re.reshape(lead + (count,)), out_im.reshape(lead + (count,)))


def filtered(samples, filters):
    channels = samples.shape[0]
    frames = samples.shape[1] // FR
    signal = samples.astype(jnp.float32).reshape(channels, frames, FR)
    freq_re, freq_im = transform(signal, None, FR)
    padded_taps = jnp.pad(filters.astype(jnp.float32), ((0, 0), (0, FR - filters.shape[1])))
    resp_re, resp_im = transform(padded_taps, None, FR)
    resp_re = resp_re[:, None, :]
    resp_im = resp_im[:, None, :]
    spec_re = (freq_re * resp_re - freq_im * resp_im).astype(jnp.bfloat16)
    spec_im = (freq_re * resp_im + freq_im * resp_re).astype(jnp.bfloat16)
    return (spec_re, spec_im)


def body(traces, taps, bin_ids, owners):
    channels = traces.shape[0]
    frames = traces.shape[1] // FR
    spec_re, spec_im = filtered(traces, taps)
    mine = lax.axis_index("chan")
    near_re = spec_re.astype(jnp.float32)
    near_im = spec_im.astype(jnp.float32)
    results = []
    for offset in range(ROUNDS):
        far_re, far_im = passed_along((spec_re, spec_im), "chan", offset + 1)
        far_re = far_re.astype(jnp.float32)
        far_im = far_im.astype(jnp.float32)
        cross_re = jnp.sum(far_re * near_re + far_im * near_im, axis=(0, 1))
        cross_im = jnp.sum(far_im * near_re - far_re * near_im, axis=(0, 1))
        results.append(jnp.stack([cross_re, cross_im]))
    contrib = jnp.stack(results)
    nbins = owners.shape[0]
    own_bins = bin_ids[:, 0]
    labels = jnp.arange(nbins, dtype=jnp.int32)
    places = jnp.sum(jnp.where(own_bins[:, None] == labels[None, :], owners[None, :], 0), axis=1)
    valid = jnp.arange(ROUNDS, dtype=jnp.int32) < mine
    places = jnp.where(valid, places, -1)
    width = contrib.shape[2]
    flat = contrib.reshape(ROUNDS, 2 * width)
    per_device = nbins // lax.axis_size("chan")
    rows = jnp.arange(lax.axis_size("chan") * per_device, dtype=jnp.int32)
    onehot = (places[None, :] == rows[:, None]).astype(jnp.float32)
    stacked = lax.psum_scatter(
        jnp.dot(onehot, flat, precision=exact, preferred_element_type=jnp.float32),
        "chan",
        scatter_dimension=0,
        tiled=True,
    )
    stacked = stacked.reshape(per_device, 2, width)
    final = lax.psum_scatter(stacked, "hour", scatter_dimension=0, tiled=True)
    weights = jnp.where(jnp.arange(FR) == 0, 1.0, 2.0).astype(jnp.float32)
    wave_re, wave_im = transform(final[:, 0] * weights, -final[:, 1] * weights, 2 * FR)
    norm = 1.0 / (FR * math.sqrt(FR * lax.axis_size("hour") * frames * channels))
    return wave_re * norm

SPLIT = 8
SUB = FR // SPLIT
LANES = 128
TILES = SUB // LANES


def sub_tables():
    a = np.arange(SUB)[:, None]
    k1 = np.arange(SUB)[None, :]
    turn = 2.0 * np.pi * ((a * k1) % (2 * SUB)) / (2 * SUB)
    cos, sin = np.cos(turn), -np.sin(turn)
    sin[:, 0] = 1.0 - 2.0 * (np.arange(SUB) % 2)
    table = np.stack([cos.reshape(SUB, TILES, LANES), sin.reshape(SUB, TILES, LANES)], axis=2)
    return table.reshape(SUB, 2 * SUB)


def two_parts(table):
    high = table.astype(jnp.bfloat16)
    low = (table - high.astype(np.float64)).astype(jnp.bfloat16)
    return high, low


PIECE = 512
SHARE = PIECE // SPLIT


def pick_tables():
    table = np.zeros((PIECE, SPLIT, 2, SHARE), np.float32)
    for n in range(SPLIT):
        for b in range(SHARE):
            table[SPLIT * b + n, n, :, b] = 1.0
    twice = table.reshape(PIECE, 2 * PIECE).astype(jnp.bfloat16)
    return np.ascontiguousarray(table[:, :, 0].reshape(PIECE, PIECE)).astype(jnp.bfloat16), twice


def turn_table():
    n = np.arange(SPLIT)[:, None]
    k1 = np.arange(SUB)[None, :]
    turn = 2.0 * np.pi * n * k1 / (2 * FR)
    table = np.stack([np.cos(turn), -np.sin(turn)], axis=1).reshape(SPLIT, 2, TILES, 1, LANES)
    table = np.broadcast_to(table.transpose(2, 0, 1, 3, 4), (TILES, SPLIT, 2, 8, LANES))
    return np.ascontiguousarray(table).astype(np.float32)


def times(value, angle):
    re, im = value
    c, s = math.cos(angle), math.sin(angle)
    if abs(s) < 1e-12:
        return (re, im) if c > 0 else (-re, -im)
    if abs(c) < 1e-12:
        return (-im, re) if s > 0 else (im, -re)
    if abs(abs(c) - abs(s)) < 1e-12:
        root = abs(c)
        p, q = math.copysign(1.0, c), math.copysign(1.0, s)
        first = (re if p > 0 else -re) + (-im if q > 0 else im)
        second = (re if q > 0 else -re) + (im if p > 0 else -im)
        return first * root, second * root
    return re * c - im * s, re * s + im * c


def small_dft(values, sign, half=False):
    size = len(values)
    if size == 1:
        return values
    even = small_dft(values[0::2], sign)
    odd = small_dft(values[1::2], sign)
    low, high = [], []
    for k in range(size // 2):
        turned = times(odd[k], sign * 2.0 * math.pi * k / size)
        low.append((even[k][0] + turned[0], even[k][1] + turned[1]))
        if not half:
            high.append((even[k][0] - turned[0], even[k][1] - turned[1]))
    return low + high


LATE = 8
SLOTS = 32


def slot_of(step, before, chan):
    if isinstance(step, int) and step == chan - 1:
        return before
    return LATE + step * (step - 1) // 2 + before


def rows_of_pairs(ids, owners):
    depth = ids.shape[1]
    nbins = owners.shape[1]
    bins = lax.broadcasted_iota(jnp.int32, (nbins, depth), 0) + 1
    picked = (bins == ids[0:1, :]).astype(jnp.float32).astype(jnp.bfloat16)
    row = lax.broadcasted_iota(jnp.int32, (nbins, nbins), 0)
    moved = (row == owners[...]).astype(jnp.float32).astype(jnp.bfloat16)
    return jnp.dot(moved, picked, preferred_element_type=jnp.float32).astype(jnp.bfloat16)


def fold(values):
    sublane = lax.broadcasted_iota(jnp.int32, values[0].shape, 0)
    shift = 1
    while len(values) > 1:
        first = lax.rem(lax.div(sublane, shift), 2) == 0
        values = [
            jnp.where(first, a, b) + pltpu.roll(jnp.where(first, b, a), SPLIT - shift, 0)
            for a, b in zip(values[0::2], values[1::2])
        ]
        shift *= 2
    return values[0]


OUT_ROWS = 2 * FR // LANES
TERMS = 2 * SPLIT * (TILES + 1)


def column_table():
    v = np.arange(LANES)[:, None]
    t, k2 = np.arange(TILES)[None, :, None], np.arange(SPLIT)[None, None, :]
    main = 2.0 * np.pi * ((v[:, :, None] * (SPLIT * k2 + t)) % OUT_ROWS) / OUT_ROWS
    extra = 2.0 * np.pi * ((v * (SPLIT // 2 + SPLIT * (np.arange(SPLIT)[None, :] - SPLIT // 2))) % OUT_ROWS) / OUT_ROWS
    phase = np.concatenate([main, extra[:, None, :]], axis=1)
    top = np.stack([np.cos(phase), -np.sin(phase)], axis=2).reshape(LANES, TERMS)
    under = np.stack([np.sin(phase), np.cos(phase)], axis=2).reshape(LANES, TERMS)
    high, low = two_parts(np.concatenate([top, under], axis=0))
    rest = np.zeros((2 * LANES, 2 * LANES - 3 * TERMS), jnp.bfloat16)
    return np.concatenate([high, high, low, rest], axis=1)


def twist_table():
    turn = 2.0 * np.pi * np.arange(LANES)[:, None] * np.arange(LANES)[None, :] / (2 * FR)
    return np.stack([np.cos(turn), np.sin(turn)]).astype(np.float32)


def row_table():
    turn = 2.0 * np.pi * ((np.arange(OUT_ROWS)[:, None] * np.arange(LANES)[None, :]) % OUT_ROWS) / OUT_ROWS
    high, low = two_parts(np.concatenate([np.cos(turn), -np.sin(turn)], axis=1))
    return np.concatenate([high, high, low], axis=1)


def halves(value):
    top = value.astype(jnp.bfloat16)
    return top, (value - top.astype(jnp.float32)).astype(jnp.bfloat16)


def over_lanes(a, b):
    return lax.dot_general(a, b, (((1,), (1,)), ((), ())), preferred_element_type=jnp.float32)


def inverse(rows, column, twist, across):
    lane = lax.broadcasted_iota(jnp.int32, rows.shape, 1)
    slot = lax.broadcasted_iota(jnp.int32, rows.shape, 0)
    rows = rows * jnp.where((lane == 0) & (slot == 0), 1.0, 2.0)
    apart = (lane == 0) & (slot < 2 * SPLIT) & (lax.rem(slot, SPLIT) >= SPLIT // 2)
    every = jnp.concatenate(
        [jnp.where(apart, 0.0, rows), jnp.where(apart, rows, 0.0)[: 2 * SPLIT]], axis=0
    )
    top, rest = halves(every)
    nothing = jnp.zeros((2 * LANES - 3 * TERMS, LANES), jnp.bfloat16)
    z = jnp.dot(
        column[...], jnp.concatenate([top, rest, top, nothing], axis=0), preferred_element_type=jnp.float32
    )
    z_re, z_im = z[:LANES], z[LANES:]
    c, s = twist[0], twist[1]
    y = jnp.concatenate([z_re * c - z_im * s, z_re * s + z_im * c], axis=1)
    top, rest = halves(y)
    return over_lanes(across[...], jnp.concatenate([top, rest, top], axis=1))


def kernel(chan, hour, x, taps, bin_ids, owners, *refs):
    tables, out = refs[:7], refs[7]
    held = refs[8:15]
    pick, high, turns, column, twist = held[:5]
    across, twice = held[5:]
    xin, tin, ids, ids_in, xd, td, fx, fh, spec, kron, part, first, early, outbox, inbox = refs[15:30]
    table_sem, own_sem, ids_send, ids_recv, t_send, t_recv, x_send, x_recv = refs[30:38]
    f_send, f_recv, send, recv, send2, recv2 = refs[38:]
    me, my_hour = lax.axis_index("chan"), lax.axis_index("hour")
    per = xin.shape[1]
    share = pl.ds(pl.multiple_of(my_hour * (tin.shape[2] // hour), LANES), tin.shape[2] // hour)

    def flipped(at, o, size):
        to, bit = at, 1
        while bit < size:
            to = to + lax.rem(lax.div(o, bit), 2) * bit * (1 - 2 * lax.rem(lax.div(at, bit), 2))
            bit *= 2
        return to

    def partner(o):
        return flipped(me, o, chan)

    def beside(o):
        return flipped(my_hour, o, hour)

    def sent(src, dst, sends, recvs, **device):
        return pltpu.make_async_remote_copy(
            src_ref=src, dst_ref=dst, send_sem=sends, recv_sem=recvs, device_id=device, device_id_type=MESH
        )

    loads = [pltpu.make_async_copy(src, dst, table_sem.at[z]) for z, (src, dst) in enumerate(zip(tables, held))]
    own = [
        pltpu.make_async_copy(x.at[me], xin.at[me], own_sem.at[0]),
        pltpu.make_async_copy(taps.at[me, :, share], tin.at[me, :, share], own_sem.at[1]),
    ]
    barrier = pltpu.get_barrier_semaphore()
    for o in range(1, hour):
        pl.semaphore_signal(
            barrier, inc=1, device_id={"hour": lax.rem(my_hour + o, hour)}, device_id_type=MESH
        )
    for o in range(1, chan):
        pl.semaphore_signal(barrier, inc=1, device_id={"chan": partner(o)}, device_id_type=MESH)
    for copy in own + loads:
        copy.start()
    place = lax.broadcasted_iota(jnp.int32, ids.shape, 1)
    labels = jnp.zeros(ids.shape, jnp.int32)
    for r in range(ROUNDS):
        live = (place == me * ROUNDS + r) & (me >= r + 1)
        labels = jnp.where(live, bin_ids[:, r : r + 1] + 1, labels)
    ids[...] = labels
    pl.semaphore_wait(barrier, chan + hour - 2)

    def x_copy(o):
        to = partner(o)
        return sent(x.at[to], xin.at[me], x_send.at[o], x_recv.at[o], chan=to)

    far_first = sorted(range(1, chan), key=lambda o: -(o.bit_length()))
    tap_copies, id_copies = [], []
    for o in far_first:
        to = partner(o)
        tap_copies.append(
            sent(taps.at[to, :, share], tin.at[me, :, share], t_send.at[o], t_recv.at[o], chan=to)
        )
        tap_copies[-1].start()
    for o in far_first:
        id_copies.append(
            sent(ids.at[0:1], ids_in.at[o, 0:1], ids_send.at[o], ids_recv.at[o], chan=partner(o))
        )
        id_copies[-1].start()
    for o in range(1, chan):
        x_copy(o).start()
    lane0 = lax.broadcasted_iota(jnp.int32, (8, LANES), 1) == 0

    def bins_of(f, rows, t, edge):
        values, extra = [], []
        for n in range(SPLIT):
            re = f[n, rows, pl.ds(pl.multiple_of(2 * t * LANES, LANES), LANES)]
            im = f[n, rows, pl.ds(pl.multiple_of((2 * t + 1) * LANES, LANES), LANES)]
            if edge:
                angle = -math.pi * n / SPLIT
                extra.append((im * math.cos(angle), im * math.sin(angle)))
                im = jnp.where(lane0, 0.0, im)
            if n == 0:
                values.append((re, im))
            else:
                c, s = turns[t, n, 0], turns[t, n, 1]
                values.append((re * c - im * s, re * s + im * c))
        found = small_dft(values, -1)
        if edge:
            more = small_dft(extra, -1, half=True)
            for k2 in range(SPLIT // 2):
                old = found[SPLIT // 2 + k2]
                found[SPLIT // 2 + k2] = tuple(jnp.where(lane0, more[k2][z], old[z]) for z in range(2))
        return found

    def responses(t, edge):
        @pl.loop(0, chan * per // 8)
        def _(g):
            here = pl.ds(pl.multiple_of(8 * g, 8), 8)
            for k2, (hr, hi) in enumerate(bins_of(fh, here, t, edge)):
                spec[t, k2, 0, here, :] = hr
                spec[t, k2, 1, here, :] = hi

    def spectra(block, t, edge):
        for g in range(per // 8):
            here = pl.ds(pl.multiple_of(block * per + 8 * g, 8), 8)
            for k2, (xr, xi) in enumerate(bins_of(fx, slice(8 * g, 8 * g + 8), t, edge)):
                hr, hi = spec[t, k2, 0, here, :], spec[t, k2, 1, here, :]
                spec[t, k2, 0, here, :] = (xr * hr - xi * hi).astype(jnp.bfloat16).astype(jnp.float32)
                spec[t, k2, 1, here, :] = (xr * hi + xi * hr).astype(jnp.bfloat16).astype(jnp.float32)

    half = lax.broadcasted_iota(jnp.int32, (per, LANES), 1) < SHARE

    def transform_of(block):
        flat = jnp.concatenate([xin[block, :, q * PIECE : (q + 1) * PIECE] for q in range(FR // PIECE)], axis=0)
        got = jnp.dot(flat, pick[...], preferred_element_type=jnp.float32)
        for g in range(TILES):
            for n in range(SPLIT):
                a, b = (
                    got[q * per : (q + 1) * per, n // 2 * LANES : (n // 2 + 1) * LANES] for q in (2 * g, 2 * g + 1)
                )
                if n % 2:
                    a = pltpu.roll(a, SHARE, 1)
                else:
                    b = pltpu.roll(b, SHARE, 1)
                xd[n * per : (n + 1) * per, g * LANES : (g + 1) * LANES] = jnp.where(half, a, b).astype(jnp.bfloat16)
        found = jnp.dot(jnp.concatenate([xd[...], xd[...]], axis=1), high[...], preferred_element_type=jnp.float32)
        for n in range(SPLIT):
            fx[n] = found[n * per : (n + 1) * per]

    def spectra_of(block):
        spectra(block, 0, True)

        @pl.loop(1, TILES)
        def _(t):
            spectra(block, t, False)

    def take(block):
        transform_of(block)
        spectra_of(block)

    for copy in loads + own[:1]:
        copy.wait()
    transform_of(me)
    own[1].wait()
    for copy in tap_copies:
        copy.wait_recv()
    forwards = []
    for o in range(1, hour):
        to = lax.rem(my_hour + o, hour)
        forwards.append(sent(tin.at[:, :, share], tin.at[:, :, share], f_send.at[o], f_recv.at[o], hour=to))
        forwards[-1].start()
    for copy in id_copies:
        copy.wait_recv()
    labels = ids[0:1, :]
    for o in range(1, chan):
        labels = labels + ids_in[o, 0:1, :]
    by_pair = rows_of_pairs(labels, owners)
    nbins = chan * hour
    pair = lax.broadcasted_iota(jnp.int32, (ids.shape[1], SLOTS), 0)
    column_of = lax.broadcasted_iota(jnp.int32, (ids.shape[1], SLOTS), 1)
    places = jnp.zeros(pair.shape, jnp.float32)
    for s in range(1, chan):
        for j in range(s):
            near, far = jnp.maximum(partner(s), partner(j)), jnp.minimum(partner(s), partner(j))
            held_by = jnp.where(near - far <= ROUNDS, near * ROUNDS + near - far - 1, -1)
            hit = (column_of == slot_of(s, j, chan)) & (pair == held_by)
            places = jnp.where(hit, 1.0, places)
    by_slot = jnp.dot(by_pair, places.astype(jnp.bfloat16), preferred_element_type=jnp.float32).astype(jnp.bfloat16)
    deep = 2 * SPLIT
    spread = (
        lax.div(lax.broadcasted_iota(jnp.int32, (nbins * deep, nbins), 0), deep)
        == lax.broadcasted_iota(jnp.int32, (nbins * deep, nbins), 1)
    ).astype(jnp.float32).astype(jnp.bfloat16)
    widen = (
        lax.div(lax.broadcasted_iota(jnp.int32, (SLOTS, SLOTS * deep), 1), deep)
        == lax.broadcasted_iota(jnp.int32, (SLOTS, SLOTS * deep), 0)
    ).astype(jnp.float32).astype(jnp.bfloat16)
    tall = jnp.dot(spread, by_slot, preferred_element_type=jnp.float32).astype(jnp.bfloat16)
    both = jnp.dot(tall, widen, preferred_element_type=jnp.float32)
    same = lax.rem(lax.broadcasted_iota(jnp.int32, both.shape, 0), deep) == lax.rem(
        lax.broadcasted_iota(jnp.int32, both.shape, 1), deep
    )
    kron[...] = jnp.where(same, both, 0.0).astype(jnp.bfloat16)

    def cross(t, near, far, slot):
        res, ims = [], []
        for k2 in range(SPLIT):
            re = im = None
            for c in range(per // 8):
                at = pl.ds(pl.multiple_of(near * per + 8 * c, 8), 8)
                of = pl.ds(pl.multiple_of(far * per + 8 * c, 8), 8)
                nr, ni = spec[t, k2, 0, at, :], spec[t, k2, 1, at, :]
                fr, fi = spec[t, k2, 0, of, :], spec[t, k2, 1, of, :]
                one, two = fr * nr + fi * ni, fi * nr - fr * ni
                re, im = (one, two) if re is None else (re + one, im + two)
            res.append(re)
            ims.append(im)
        part[t, slot] = jnp.concatenate([fold(res), fold(ims)], axis=0).astype(jnp.bfloat16)

    def crosses(s, begin):
        @pl.loop(0, s)
        def _(j):
            a, b = partner(s), partner(j)
            for t in range(TILES):
                cross(t, jnp.maximum(a, b), jnp.minimum(a, b), begin + j)

    def part_copy(z, o, begin, count):
        where = pl.ds(begin, count)
        return sent(part.at[beside(o), where], first.at[o, where], send.at[z, o], recv.at[z, o], hour=beside(o))

    groups = [(LATE, 6), (LATE + 6, 4), (LATE + 10, 5), (LATE + 15, 6), (0, 7)]
    order = [2, 3, 1, 0]
    for copy in forwards:
        copy.wait_recv()
    count = tin.shape[2]
    got = jnp.dot(tin[...].reshape(chan * per, count), twice[...], preferred_element_type=jnp.float32)
    for n in range(SPLIT):
        td[n] = got[:, n * LANES : (n + 1) * LANES].astype(jnp.bfloat16)
    found = jnp.dot(
        td[...].reshape(SPLIT * chan * per, LANES),
        jnp.concatenate([high[:SHARE, :], high[SUB : SUB + SHARE, :]], axis=0),
        preferred_element_type=jnp.float32,
    )
    for n in range(SPLIT):
        fh[n] = found[n * chan * per : (n + 1) * chan * per]
    responses(0, True)

    @pl.loop(1, TILES)
    def _(t):
        responses(t, False)

    spectra_of(me)

    @pl.loop(1, chan // 2)
    def _(s):
        x_copy(s).wait_recv()
        take(partner(s))
        crosses(s, LATE + lax.div(s * (s - 1), 2))

    for o in order[:3]:
        part_copy(0, o, *groups[0]).start()

    @pl.loop(chan // 2, chan - 1)
    def _(s):
        x_copy(s).wait_recv()
        take(partner(s))
        crosses(s, LATE + lax.div(s * (s - 1), 2))

        for z in range(1, len(groups) - 1):

            @pl.when(s == z + 3)
            def _():
                for o in order[:3]:
                    part_copy(z, o, *groups[z]).start()

    x_copy(chan - 1).wait_recv()
    block = partner(chan - 1)
    transform_of(block)

    @pl.loop(0, TILES)
    def _(z):
        late = lax.div(z, 2)
        o = (1 - late) * (2 + z) + late * (3 - z)
        t = beside(o)

        @pl.when(t == 0)
        def _():
            spectra(block, 0, True)

        @pl.when(t > 0)
        def _():
            spectra(block, t, False)

        for j in range(chan - 1):
            cross(t, jnp.maximum(block, partner(j)), jnp.minimum(block, partner(j)), j)

        @pl.when(o > 0)
        def _():
            part_copy(4, o, *groups[4]).start()

    def mixed(begin, count, room):
        where = slice(begin, begin + count)
        total = part[my_hour, where].astype(jnp.float32)
        for o in range(1, hour):
            total = total + first[o, where].astype(jnp.float32)
        total = total.reshape(count * deep, LANES)
        if room > count:
            total = jnp.concatenate([total, jnp.zeros(((room - count) * deep, LANES), jnp.float32)], axis=0)
        got = jnp.dot(
            kron[:, begin * deep : (begin + room) * deep],
            jnp.concatenate(halves(total), axis=1),
            preferred_element_type=jnp.float32,
        )
        return got[:, :LANES] + got[:, LANES:]

    for z in range(len(groups) - 1):
        for o in range(1, hour):
            part_copy(z, o, *groups[z]).wait_recv()
    early[...] = mixed(LATE, 21, SLOTS - LATE)
    for o in range(1, hour):
        part_copy(4, o, *groups[4]).wait_recv()
    outbox[...] = (mixed(0, 7, LATE) + early[...]).astype(jnp.bfloat16).reshape(outbox.shape)
    for oc in far_first + [0]:
        for o in order:
            if oc or o:
                to, at = partner(oc), beside(o)
                sent(
                    outbox.at[to * hour + at],
                    inbox.at[oc * hour + my_hour],
                    send2.at[0],
                    recv2.at[0],
                    chan=to,
                    hour=at,
                ).start()
    inbox[my_hour] = outbox[me * hour + my_hour]
    for copy in tap_copies + id_copies + forwards:
        copy.wait_send()
    for o in range(1, chan):
        x_copy(o).wait_send()
    for z in range(len(groups)):
        for o in range(1, hour):
            part_copy(z, o, *groups[z]).wait_send()

    others = pl.ds(0, chan * hour - 1)
    all_rows = sent(outbox.at[others], inbox.at[others], send2.at[0], recv2.at[0], chan=partner(1))
    all_rows.wait_recv()
    rows = inbox[0:hour].astype(jnp.float32)
    for oc in range(1, chan):
        rows = rows + inbox[oc * hour : (oc + 1) * hour].astype(jnp.float32)
    wave = inverse(rows.reshape(TILES * deep, LANES), column, twist, across)
    out[...] = wave
    all_rows.wait_send()


def split_body(traces, taps, bin_ids, owners):
    chan, hour = lax.axis_size("chan"), lax.axis_size("hour")
    channels, count = taps.shape
    per = channels // chan
    norm = 1.0 / (FR * math.sqrt(FR * hour * channels))
    high, low = two_parts(sub_tables())
    pick, twice = pick_tables()
    tables = [pick, np.concatenate([high, low], axis=0), turn_table(), column_table(), twist_table(), row_table(), twice]
    depth = LANES
    part = (hour, SLOTS, 2 * SPLIT, LANES)
    rows = (chan * hour, 2 * SPLIT, LANES)
    vmem, hbm = pl.BlockSpec(memory_space=pltpu.VMEM), pl.BlockSpec(memory_space=pl.ANY)
    sems = pltpu.SemaphoreType.DMA
    wave = pl.pallas_call(
        functools.partial(kernel, chan, hour),
        out_shape=pltpu.VMEM((OUT_ROWS, LANES), jnp.float32),
        in_specs=[hbm, hbm, vmem, vmem] + [hbm] * len(tables),
        out_specs=vmem,
        scratch_shapes=[pltpu.VMEM(table.shape, table.dtype) for table in tables]
        + [
            pltpu.VMEM((chan, per, FR), jnp.bfloat16),
            pltpu.VMEM((chan, per, count), jnp.bfloat16),
            pltpu.VMEM((8, depth), jnp.int32),
            pltpu.VMEM((chan, 8, depth), jnp.int32),
            pltpu.VMEM((SPLIT * per, SUB), jnp.bfloat16),
            pltpu.VMEM((SPLIT, channels, LANES), jnp.bfloat16),
            pltpu.VMEM((SPLIT, per, 2 * SUB), jnp.float32),
            pltpu.VMEM((SPLIT, channels, 2 * SUB), jnp.float32),
            pltpu.VMEM((TILES, SPLIT, 2, channels, LANES), jnp.float32),
            pltpu.VMEM((rows[0] * rows[1], SLOTS * rows[1]), jnp.bfloat16),
            pltpu.VMEM(part, jnp.bfloat16),
            pltpu.VMEM(part, jnp.bfloat16),
            pltpu.VMEM((rows[0] * rows[1], LANES), jnp.float32),
            pltpu.VMEM(rows, jnp.bfloat16),
            pltpu.VMEM(rows, jnp.bfloat16),
            sems((len(tables),)),
            sems((2,)),
        ]
        + [sems((chan,))] * 6
        + [sems((hour,))] * 2
        + [sems((5, hour))] * 2
        + [sems((1,))] * 2,
        compiler_params=pltpu.CompilerParams(
            collective_id=0, has_side_effects=True, vmem_limit_bytes=56 * 2**20
        ),
    )(
        traces.reshape(chan, per, FR),
        taps.reshape(chan, per, count),
        bin_ids.T,
        owners.reshape(1, -1),
        *[jnp.asarray(table) for table in tables],
    )
    return (wave * norm).reshape(1, 2 * FR)


def solution(mesh):
    placed = (P("chan", "hour"), P("chan", None), P(None, "chan"), P())

    def whole(traces, taps, bin_ids, owners):
        chan, hour = mesh.shape["chan"], mesh.shape["hour"]
        channels = traces.shape[0] // chan
        fits = (
            chan == 8
            and hour == TILES
            and channels % (16 * chan) == 0
            and traces.shape[1] == hour * FR
            and taps.shape[1] == SPLIT * LANES // 2
            and owners.shape[0] == chan * hour
        )
        return jax.shard_map(
            split_body if fits else body,
            mesh=mesh,
            in_specs=placed,
            out_specs=P(("chan", "hour"), None),
            check_vma=False,
        )(traces, taps, bin_ids, owners)

    return whole
```

```python
import functools
import math

import jax
import jax.numpy as jnp
import numpy as np
from jax import lax
from jax.experimental import pallas as pl
from jax.experimental.pallas import tpu as pltpu
from jax.sharding import PartitionSpec as P

FR = 4096
ROUNDS = 4
MESH = pl.DeviceIdType.MESH


exact = lax.Precision.HIGHEST

def passed_along(shard, axis, by):
    devices = lax.axis_size(axis)
    pairs = [(i, i + by) for i in range(devices) if 0 <= i + by < devices]
    return lax.ppermute(shard, axis, pairs)


def transform(real_part, imag_part, count):
    span = real_part.shape[-1]
    inner = 2 * span // 128
    lead = real_part.shape[:-1]
    first = jnp.arange(64, dtype=jnp.float32)[:, None]
    middle = jnp.arange(128, dtype=jnp.float32)[None, :]
    angle_one = 2.0 * math.pi / 128.0 * jnp.mod(first * middle, 128.0)
    cos_one = jnp.cos(angle_one)
    sin_one = -jnp.sin(angle_one)
    second = jnp.arange(inner, dtype=jnp.float32)[:, None]
    angle_turn = 2.0 * math.pi / (128.0 * inner) * jnp.mod(second * middle, 128.0 * inner)
    cos_turn = jnp.cos(angle_turn)
    sin_turn = -jnp.sin(angle_turn)
    outer = jnp.arange(count // 128, dtype=jnp.float32)[None, :]
    angle_two = 2.0 * math.pi / inner * jnp.mod(second * outer, float(inner))
    cos_two = jnp.cos(angle_two)
    sin_two = -jnp.sin(angle_two)
    grid = real_part.reshape(lead + (64, inner))
    section_re = jnp.einsum("...an,ak->...nk", grid, cos_one, precision=exact)
    section_im = jnp.einsum("...an,ak->...nk", grid, sin_one, precision=exact)
    if imag_part is not None:
        grid_im = imag_part.reshape(lead + (64, inner))
        section_re = section_re - jnp.einsum("...an,ak->...nk", grid_im, sin_one, precision=exact)
        section_im = section_im + jnp.einsum("...an,ak->...nk", grid_im, cos_one, precision=exact)
    turned_re = section_re * cos_turn - section_im * sin_turn
    turned_im = section_re * sin_turn + section_im * cos_turn
    out_re = jnp.einsum("...nk,nm->...mk", turned_re, cos_two, precision=exact) - jnp.einsum(
        "...nk,nm->...mk", turned_im, sin_two, precision=exact
    )
    out_im = jnp.einsum("...nk,nm->...mk", turned_re, sin_two, precision=exact) + jnp.einsum(
        "...nk,nm->...mk", turned_im, cos_two, precision=exact
    )
    return (out_re.reshape(lead + (count,)), out_im.reshape(lead + (count,)))


def filtered(samples, filters):
    channels = samples.shape[0]
    frames = samples.shape[1] // FR
    signal = samples.astype(jnp.float32).reshape(channels, frames, FR)
    freq_re, freq_im = transform(signal, None, FR)
    padded_taps = jnp.pad(filters.astype(jnp.float32), ((0, 0), (0, FR - filters.shape[1])))
    resp_re, resp_im = transform(padded_taps, None, FR)
    resp_re = resp_re[:, None, :]
    resp_im = resp_im[:, None, :]
    spec_re = (freq_re * resp_re - freq_im * resp_im).astype(jnp.bfloat16)
    spec_im = (freq_re * resp_im + freq_im * resp_re).astype(jnp.bfloat16)
    return (spec_re, spec_im)


def body(traces, taps, bin_ids, owners):
    channels = traces.shape[0]
    frames = traces.shape[1] // FR
    spec_re, spec_im = filtered(traces, taps)
    mine = lax.axis_index("chan")
    near_re = spec_re.astype(jnp.float32)
    near_im = spec_im.astype(jnp.float32)
    results = []
    for offset in range(ROUNDS):
        far_re, far_im = passed_along((spec_re, spec_im), "chan", offset + 1)
        far_re = far_re.astype(jnp.float32)
        far_im = far_im.astype(jnp.float32)
        cross_re = jnp.sum(far_re * near_re + far_im * near_im, axis=(0, 1))
        cross_im = jnp.sum(far_im * near_re - far_re * near_im, axis=(0, 1))
        results.append(jnp.stack([cross_re, cross_im]))
    contrib = jnp.stack(results)
    nbins = owners.shape[0]
    own_bins = bin_ids[:, 0]
    labels = jnp.arange(nbins, dtype=jnp.int32)
    places = jnp.sum(jnp.where(own_bins[:, None] == labels[None, :], owners[None, :], 0), axis=1)
    valid = jnp.arange(ROUNDS, dtype=jnp.int32) < mine
    places = jnp.where(valid, places, -1)
    width = contrib.shape[2]
    flat = contrib.reshape(ROUNDS, 2 * width)
    per_device = nbins // lax.axis_size("chan")
    rows = jnp.arange(lax.axis_size("chan") * per_device, dtype=jnp.int32)
    onehot = (places[None, :] == rows[:, None]).astype(jnp.float32)
    stacked = lax.psum_scatter(
        jnp.dot(onehot, flat, precision=exact, preferred_element_type=jnp.float32),
        "chan",
        scatter_dimension=0,
        tiled=True,
    )
    stacked = stacked.reshape(per_device, 2, width)
    final = lax.psum_scatter(stacked, "hour", scatter_dimension=0, tiled=True)
    weights = jnp.where(jnp.arange(FR) == 0, 1.0, 2.0).astype(jnp.float32)
    wave_re, wave_im = transform(final[:, 0] * weights, -final[:, 1] * weights, 2 * FR)
    norm = 1.0 / (FR * math.sqrt(FR * lax.axis_size("hour") * frames * channels))
    return wave_re * norm

SPLIT = 8
SUB = FR // SPLIT
LANES = 128
TILES = SUB // LANES


def sub_tables():
    a = np.arange(SUB)[:, None]
    k1 = np.arange(SUB)[None, :]
    turn = 2.0 * np.pi * ((a * k1) % (2 * SUB)) / (2 * SUB)
    cos, sin = np.cos(turn), -np.sin(turn)
    sin[:, 0] = 1.0 - 2.0 * (np.arange(SUB) % 2)
    table = np.stack([cos.reshape(SUB, TILES, LANES), sin.reshape(SUB, TILES, LANES)], axis=2)
    return table.reshape(SUB, 2 * SUB)


def two_parts(table):
    high = table.astype(jnp.bfloat16)
    low = (table - high.astype(np.float64)).astype(jnp.bfloat16)
    return high, low


PIECE = 512
SHARE = PIECE // SPLIT


def pick_tables():
    table = np.zeros((PIECE, SPLIT, 2, SHARE), np.float32)
    for n in range(SPLIT):
        for b in range(SHARE):
            table[SPLIT * b + n, n, :, b] = 1.0
    twice = table.reshape(PIECE, 2 * PIECE).astype(jnp.bfloat16)
    return np.ascontiguousarray(table[:, :, 0].reshape(PIECE, PIECE)).astype(jnp.bfloat16), twice


def turn_table():
    n = np.arange(SPLIT)[:, None]
    k1 = np.arange(SUB)[None, :]
    turn = 2.0 * np.pi * n * k1 / (2 * FR)
    table = np.stack([np.cos(turn), -np.sin(turn)], axis=1).reshape(SPLIT, 2, TILES, 1, LANES)
    table = np.broadcast_to(table.transpose(2, 0, 1, 3, 4), (TILES, SPLIT, 2, 8, LANES))
    return np.ascontiguousarray(table).astype(np.float32)


def times(value, angle):
    re, im = value
    c, s = math.cos(angle), math.sin(angle)
    if abs(s) < 1e-12:
        return (re, im) if c > 0 else (-re, -im)
    if abs(c) < 1e-12:
        return (-im, re) if s > 0 else (im, -re)
    if abs(abs(c) - abs(s)) < 1e-12:
        root = abs(c)
        p, q = math.copysign(1.0, c), math.copysign(1.0, s)
        first = (re if p > 0 else -re) + (-im if q > 0 else im)
        second = (re if q > 0 else -re) + (im if p > 0 else -im)
        return first * root, second * root
    return re * c - im * s, re * s + im * c


def small_dft(values, sign, half=False):
    size = len(values)
    if size == 1:
        return values
    even = small_dft(values[0::2], sign)
    odd = small_dft(values[1::2], sign)
    low, high = [], []
    for k in range(size // 2):
        turned = times(odd[k], sign * 2.0 * math.pi * k / size)
        low.append((even[k][0] + turned[0], even[k][1] + turned[1]))
        if not half:
            high.append((even[k][0] - turned[0], even[k][1] - turned[1]))
    return low + high


LATE = 8
SLOTS = 32


def slot_of(step, before, chan):
    if isinstance(step, int) and step == chan - 1:
        return before
    return LATE + step * (step - 1) // 2 + before


def rows_of_pairs(ids, owners):
    depth = ids.shape[1]
    nbins = owners.shape[1]
    bins = lax.broadcasted_iota(jnp.int32, (nbins, depth), 0) + 1
    picked = (bins == ids[0:1, :]).astype(jnp.float32).astype(jnp.bfloat16)
    row = lax.broadcasted_iota(jnp.int32, (nbins, nbins), 0)
    moved = (row == owners[...]).astype(jnp.float32).astype(jnp.bfloat16)
    return jnp.dot(moved, picked, preferred_element_type=jnp.float32).astype(jnp.bfloat16)


def fold(values):
    sublane = lax.broadcasted_iota(jnp.int32, values[0].shape, 0)
    shift = 1
    while len(values) > 1:
        first = lax.rem(lax.div(sublane, shift), 2) == 0
        values = [
            jnp.where(first, a, b) + pltpu.roll(jnp.where(first, b, a), SPLIT - shift, 0)
            for a, b in zip(values[0::2], values[1::2])
        ]
        shift *= 2
    return values[0]


OUT_ROWS = 2 * FR // LANES
TERMS = 2 * SPLIT * (TILES + 1)


def column_table():
    v = np.arange(LANES)[:, None]
    t, k2 = np.arange(TILES)[None, :, None], np.arange(SPLIT)[None, None, :]
    main = 2.0 * np.pi * ((v[:, :, None] * (SPLIT * k2 + t)) % OUT_ROWS) / OUT_ROWS
    extra = 2.0 * np.pi * ((v * (SPLIT // 2 + SPLIT * (np.arange(SPLIT)[None, :] - SPLIT // 2))) % OUT_ROWS) / OUT_ROWS
    phase = np.concatenate([main, extra[:, None, :]], axis=1)
    top = np.stack([np.cos(phase), -np.sin(phase)], axis=2).reshape(LANES, TERMS)
    under = np.stack([np.sin(phase), np.cos(phase)], axis=2).reshape(LANES, TERMS)
    high, low = two_parts(np.concatenate([top, under], axis=0))
    rest = np.zeros((2 * LANES, 2 * LANES - 3 * TERMS), jnp.bfloat16)
    return np.concatenate([high, high, low, rest], axis=1)


def twist_table():
    turn = 2.0 * np.pi * np.arange(LANES)[:, None] * np.arange(LANES)[None, :] / (2 * FR)
    return np.stack([np.cos(turn), np.sin(turn)]).astype(np.float32)


def row_table():
    turn = 2.0 * np.pi * ((np.arange(OUT_ROWS)[:, None] * np.arange(LANES)[None, :]) % OUT_ROWS) / OUT_ROWS
    high, low = two_parts(np.concatenate([np.cos(turn), -np.sin(turn)], axis=1))
    return np.concatenate([high, high, low], axis=1)


def halves(value):
    top = value.astype(jnp.bfloat16)
    return top, (value - top.astype(jnp.float32)).astype(jnp.bfloat16)


def over_lanes(a, b):
    return lax.dot_general(a, b, (((1,), (1,)), ((), ())), preferred_element_type=jnp.float32)


def inverse(rows, column, twist, across):
    lane = lax.broadcasted_iota(jnp.int32, rows.shape, 1)
    slot = lax.broadcasted_iota(jnp.int32, rows.shape, 0)
    rows = rows * jnp.where((lane == 0) & (slot == 0), 1.0, 2.0)
    apart = (lane == 0) & (slot < 2 * SPLIT) & (lax.rem(slot, SPLIT) >= SPLIT // 2)
    every = jnp.concatenate(
        [jnp.where(apart, 0.0, rows), jnp.where(apart, rows, 0.0)[: 2 * SPLIT]], axis=0
    )
    top, rest = halves(every)
    nothing = jnp.zeros((2 * LANES - 3 * TERMS, LANES), jnp.bfloat16)
    z = jnp.dot(
        column[...], jnp.concatenate([top, rest, top, nothing], axis=0), preferred_element_type=jnp.float32
    )
    z_re, z_im = z[:LANES], z[LANES:]
    c, s = twist[0], twist[1]
    y = jnp.concatenate([z_re * c - z_im * s, z_re * s + z_im * c], axis=1)
    top, rest = halves(y)
    return over_lanes(across[...], jnp.concatenate([top, rest, top], axis=1))


def kernel(chan, hour, x, taps, bin_ids, owners, *refs):
    tables, out = refs[:7], refs[7]
    held = refs[8:15]
    pick, high, turns, column, twist = held[:5]
    across, twice = held[5:]
    xin, tin, ids, ids_in, xd, td, fx, fh, spec, kron, part, first, early, outbox, inbox = refs[15:30]
    table_sem, own_sem, ids_send, ids_recv, t_send, t_recv, x_send, x_recv = refs[30:38]
    f_send, f_recv, send, recv, send2, recv2 = refs[38:]
    me, my_hour = lax.axis_index("chan"), lax.axis_index("hour")
    per = xin.shape[1]
    share = pl.ds(pl.multiple_of(my_hour * (tin.shape[2] // hour), LANES), tin.shape[2] // hour)

    def flipped(at, o, size):
        to, bit = at, 1
        while bit < size:
            to = to + lax.rem(lax.div(o, bit), 2) * bit * (1 - 2 * lax.rem(lax.div(at, bit), 2))
            bit *= 2
        return to

    def partner(o):
        return flipped(me, o, chan)

    def beside(o):
        return flipped(my_hour, o, hour)

    def sent(src, dst, sends, recvs, **device):
        return pltpu.make_async_remote_copy(
            src_ref=src, dst_ref=dst, send_sem=sends, recv_sem=recvs, device_id=device, device_id_type=MESH
        )

    loads = [pltpu.make_async_copy(src, dst, table_sem.at[z]) for z, (src, dst) in enumerate(zip(tables, held))]
    own = [
        pltpu.make_async_copy(x.at[me], xin.at[me], own_sem.at[0]),
        pltpu.make_async_copy(taps.at[me, :, share], tin.at[me, :, share], own_sem.at[1]),
    ]
    barrier = pltpu.get_barrier_semaphore()
    for o in range(1, hour):
        pl.semaphore_signal(
            barrier, inc=1, device_id={"hour": lax.rem(my_hour + o, hour)}, device_id_type=MESH
        )
    for o in range(1, chan):
        pl.semaphore_signal(barrier, inc=1, device_id={"chan": partner(o)}, device_id_type=MESH)
    for copy in own + loads:
        copy.start()
    place = lax.broadcasted_iota(jnp.int32, ids.shape, 1)
    labels = jnp.zeros(ids.shape, jnp.int32)
    for r in range(ROUNDS):
        live = (place == me * ROUNDS + r) & (me >= r + 1)
        labels = jnp.where(live, bin_ids[:, r : r + 1] + 1, labels)
    ids[...] = labels
    pl.semaphore_wait(barrier, chan + hour - 2)

    def x_copy(o):
        to = partner(o)
        return sent(x.at[to], xin.at[me], x_send.at[o], x_recv.at[o], chan=to)

    far_first = sorted(range(1, chan), key=lambda o: -(o.bit_length()))
    tap_copies, id_copies = [], []
    for o in far_first:
        to = partner(o)
        tap_copies.append(
            sent(taps.at[to, :, share], tin.at[me, :, share], t_send.at[o], t_recv.at[o], chan=to)
        )
        tap_copies[-1].start()
    for o in far_first:
        id_copies.append(
            sent(ids.at[0:1], ids_in.at[o, 0:1], ids_send.at[o], ids_recv.at[o], chan=partner(o))
        )
        id_copies[-1].start()
    for o in range(1, chan):
        x_copy(o).start()
    lane0 = lax.broadcasted_iota(jnp.int32, (8, LANES), 1) == 0

    def bins_of(f, rows, t, edge):
        values, extra = [], []
        for n in range(SPLIT):
            re = f[n, rows, pl.ds(pl.multiple_of(2 * t * LANES, LANES), LANES)]
            im = f[n, rows, pl.ds(pl.multiple_of((2 * t + 1) * LANES, LANES), LANES)]
            if edge:
                angle = -math.pi * n / SPLIT
                extra.append((im * math.cos(angle), im * math.sin(angle)))
                im = jnp.where(lane0, 0.0, im)
            if n == 0:
                values.append((re, im))
            else:
                c, s = turns[t, n, 0], turns[t, n, 1]
                values.append((re * c - im * s, re * s + im * c))
        found = small_dft(values, -1)
        if edge:
            more = small_dft(extra, -1, half=True)
            for k2 in range(SPLIT // 2):
                old = found[SPLIT // 2 + k2]
                found[SPLIT // 2 + k2] = tuple(jnp.where(lane0, more[k2][z], old[z]) for z in range(2))
        return found

    def responses(t, edge):
        @pl.loop(0, chan * per // 8)
        def _(g):
            here = pl.ds(pl.multiple_of(8 * g, 8), 8)
            for k2, (hr, hi) in enumerate(bins_of(fh, here, t, edge)):
                spec[t, k2, 0, here, :] = hr
                spec[t, k2, 1, here, :] = hi

    def spectra(block, t, edge):
        for g in range(per // 8):
            here = pl.ds(pl.multiple_of(block * per + 8 * g, 8), 8)
            for k2, (xr, xi) in enumerate(bins_of(fx, slice(8 * g, 8 * g + 8), t, edge)):
                hr, hi = spec[t, k2, 0, here, :], spec[t, k2, 1, here, :]
                spec[t, k2, 0, here, :] = (xr * hr - xi * hi).astype(jnp.bfloat16).astype(jnp.float32)
                spec[t, k2, 1, here, :] = (xr * hi + xi * hr).astype(jnp.bfloat16).astype(jnp.float32)

    half = lax.broadcasted_iota(jnp.int32, (per, LANES), 1) < SHARE

    def transform_of(block):
        flat = jnp.concatenate([xin[block, :, q * PIECE : (q + 1) * PIECE] for q in range(FR // PIECE)], axis=0)
        got = jnp.dot(flat, pick[...], preferred_element_type=jnp.float32)
        for g in range(TILES):
            for n in range(SPLIT):
                a, b = (
                    got[q * per : (q + 1) * per, n // 2 * LANES : (n // 2 + 1) * LANES] for q in (2 * g, 2 * g + 1)
                )
                if n % 2:
                    a = pltpu.roll(a, SHARE, 1)
                else:
                    b = pltpu.roll(b, SHARE, 1)
                xd[n * per : (n + 1) * per, g * LANES : (g + 1) * LANES] = jnp.where(half, a, b).astype(jnp.bfloat16)
        found = jnp.dot(jnp.concatenate([xd[...], xd[...]], axis=1), high[...], preferred_element_type=jnp.float32)
        for n in range(SPLIT):
            fx[n] = found[n * per : (n + 1) * per]

    def spectra_of(block):
        spectra(block, 0, True)

        @pl.loop(1, TILES)
        def _(t):
            spectra(block, t, False)

    def take(block):
        transform_of(block)
        spectra_of(block)

    for copy in loads + own[:1]:
        copy.wait()
    transform_of(me)
    own[1].wait()
    for copy in tap_copies:
        copy.wait_recv()
    forwards = []
    for o in range(1, hour):
        to = lax.rem(my_hour + o, hour)
        forwards.append(sent(tin.at[:, :, share], tin.at[:, :, share], f_send.at[o], f_recv.at[o], hour=to))
        forwards[-1].start()
    for copy in id_copies:
        copy.wait_recv()
    labels = ids[0:1, :]
    for o in range(1, chan):
        labels = labels + ids_in[o, 0:1, :]
    by_pair = rows_of_pairs(labels, owners)
    nbins = chan * hour
    pair = lax.broadcasted_iota(jnp.int32, (ids.shape[1], SLOTS), 0)
    column_of = lax.broadcasted_iota(jnp.int32, (ids.shape[1], SLOTS), 1)
    places = jnp.zeros(pair.shape, jnp.float32)
    for s in range(1, chan):
        for j in range(s):
            near, far = jnp.maximum(partner(s), partner(j)), jnp.minimum(partner(s), partner(j))
            held_by = jnp.where(near - far <= ROUNDS, near * ROUNDS + near - far - 1, -1)
            hit = (column_of == slot_of(s, j, chan)) & (pair == held_by)
            places = jnp.where(hit, 1.0, places)
    by_slot = jnp.dot(by_pair, places.astype(jnp.bfloat16), preferred_element_type=jnp.float32).astype(jnp.bfloat16)
    deep = 2 * SPLIT
    spread = (
        lax.div(lax.broadcasted_iota(jnp.int32, (nbins * deep, nbins), 0), deep)
        == lax.broadcasted_iota(jnp.int32, (nbins * deep, nbins), 1)
    ).astype(jnp.float32).astype(jnp.bfloat16)
    widen = (
        lax.div(lax.broadcasted_iota(jnp.int32, (SLOTS, SLOTS * deep), 1), deep)
        == lax.broadcasted_iota(jnp.int32, (SLOTS, SLOTS * deep), 0)
    ).astype(jnp.float32).astype(jnp.bfloat16)
    tall = jnp.dot(spread, by_slot, preferred_element_type=jnp.float32).astype(jnp.bfloat16)
    both = jnp.dot(tall, widen, preferred_element_type=jnp.float32)
    same = lax.rem(lax.broadcasted_iota(jnp.int32, both.shape, 0), deep) == lax.rem(
        lax.broadcasted_iota(jnp.int32, both.shape, 1), deep
    )
    kron[...] = jnp.where(same, both, 0.0).astype(jnp.bfloat16)

    def cross(t, near, far, slot):
        res, ims = [], []
        for k2 in range(SPLIT):
            re = im = None
            for c in range(per // 8):
                at = pl.ds(pl.multiple_of(near * per + 8 * c, 8), 8)
                of = pl.ds(pl.multiple_of(far * per + 8 * c, 8), 8)
                nr, ni = spec[t, k2, 0, at, :], spec[t, k2, 1, at, :]
                fr, fi = spec[t, k2, 0, of, :], spec[t, k2, 1, of, :]
                one, two = fr * nr + fi * ni, fi * nr - fr * ni
                re, im = (one, two) if re is None else (re + one, im + two)
            res.append(re)
            ims.append(im)
        part[t, slot] = jnp.concatenate([fold(res), fold(ims)], axis=0).astype(jnp.bfloat16)

    def crosses(s, begin):
        @pl.loop(0, s)
        def _(j):
            a, b = partner(s), partner(j)
            for t in range(TILES):
                cross(t, jnp.maximum(a, b), jnp.minimum(a, b), begin + j)

    def part_copy(z, o, begin, count):
        where = pl.ds(begin, count)
        return sent(part.at[beside(o), where], first.at[o, where], send.at[z, o], recv.at[z, o], hour=beside(o))

    groups = [(LATE, 6), (LATE + 6, 4), (LATE + 10, 5), (LATE + 15, 6), (0, 7)]
    order = [2, 3, 1, 0]
    for copy in forwards:
        copy.wait_recv()
    count = tin.shape[2]
    got = jnp.dot(tin[...].reshape(chan * per, count), twice[...], preferred_element_type=jnp.float32)
    for n in range(SPLIT):
        td[n] = got[:, n * LANES : (n + 1) * LANES].astype(jnp.bfloat16)
    found = jnp.dot(
        td[...].reshape(SPLIT * chan * per, LANES),
        jnp.concatenate([high[:SHARE, :], high[SUB : SUB + SHARE, :]], axis=0),
        preferred_element_type=jnp.float32,
    )
    for n in range(SPLIT):
        fh[n] = found[n * chan * per : (n + 1) * chan * per]
    responses(0, True)

    @pl.loop(1, TILES)
    def _(t):
        responses(t, False)

    spectra_of(me)

    @pl.loop(1, chan // 2)
    def _(s):
        x_copy(s).wait_recv()
        take(partner(s))
        crosses(s, LATE + lax.div(s * (s - 1), 2))

    for o in order[:3]:
        part_copy(0, o, *groups[0]).start()

    @pl.loop(chan // 2, chan - 1)
    def _(s):
        x_copy(s).wait_recv()
        take(partner(s))
        crosses(s, LATE + lax.div(s * (s - 1), 2))

        for z in range(1, len(groups) - 1):

            @pl.when(s == z + 3)
            def _():
                for o in order[:3]:
                    part_copy(z, o, *groups[z]).start()

    x_copy(chan - 1).wait_recv()
    block = partner(chan - 1)
    transform_of(block)

    @pl.loop(0, TILES)
    def _(z):
        late = lax.div(z, 2)
        o = (1 - late) * (2 + z) + late * (3 - z)
        t = beside(o)

        @pl.when(t == 0)
        def _():
            spectra(block, 0, True)

        @pl.when(t > 0)
        def _():
            spectra(block, t, False)

        for j in range(chan - 1):
            cross(t, jnp.maximum(block, partner(j)), jnp.minimum(block, partner(j)), j)

        @pl.when(o > 0)
        def _():
            part_copy(4, o, *groups[4]).start()

    def summed(begin, count, room):
        where = slice(begin, begin + count)
        total = part[my_hour, where].astype(jnp.float32)
        for o in range(1, hour):
            total = total + first[o, where].astype(jnp.float32)
        total = total.reshape(count * deep, LANES)
        if room > count:
            total = jnp.concatenate([total, jnp.zeros(((room - count) * deep, LANES), jnp.float32)], axis=0)
        return jnp.concatenate(halves(total), axis=1)

    def mixed(rows, begin, room, values):
        got = jnp.dot(
            kron[rows, begin * deep : (begin + room) * deep], values, preferred_element_type=jnp.float32
        )
        return got[:, :LANES] + got[:, LANES:]

    for z in range(len(groups) - 1):
        for o in range(1, hour):
            part_copy(z, o, *groups[z]).wait_recv()
    early[...] = mixed(slice(None), LATE, SLOTS - LATE, summed(LATE, 21, SLOTS - LATE))
    for o in range(1, hour):
        part_copy(4, o, *groups[4]).wait_recv()
    late = summed(0, 7, LATE)
    side = nbins // 2
    for z in range(2):
        half_of = 1 - lax.div(me, chan // 2) if z == 0 else lax.div(me, chan // 2)
        deep_rows = pl.ds(pl.multiple_of(half_of * side * deep, side * deep), side * deep)
        outbox[pl.ds(half_of * side, side)] = (
            (mixed(deep_rows, 0, LATE, late) + early[deep_rows, :]).astype(jnp.bfloat16).reshape(side, deep, LANES)
        )
        for oc in (5, 4, 7, 6) if z == 0 else (3, 2, 1, 0):
            for o in order:
                if oc or o:
                    to, at = partner(oc), beside(o)
                    sent(
                        outbox.at[to * hour + at],
                        inbox.at[oc * hour + my_hour],
                        send2.at[0],
                        recv2.at[0],
                        chan=to,
                        hour=at,
                    ).start()
    inbox[my_hour] = outbox[me * hour + my_hour]
    for copy in tap_copies + id_copies + forwards:
        copy.wait_send()
    for o in range(1, chan):
        x_copy(o).wait_send()
    for z in range(len(groups)):
        for o in range(1, hour):
            part_copy(z, o, *groups[z]).wait_send()

    others = pl.ds(0, chan * hour - 1)
    all_rows = sent(outbox.at[others], inbox.at[others], send2.at[0], recv2.at[0], chan=partner(1))
    all_rows.wait_recv()
    rows = inbox[0:hour].astype(jnp.float32)
    for oc in range(1, chan):
        rows = rows + inbox[oc * hour : (oc + 1) * hour].astype(jnp.float32)
    wave = inverse(rows.reshape(TILES * deep, LANES), column, twist, across)
    out[...] = wave
    all_rows.wait_send()


def split_body(traces, taps, bin_ids, owners):
    chan, hour = lax.axis_size("chan"), lax.axis_size("hour")
    channels, count = taps.shape
    per = channels // chan
    norm = 1.0 / (FR * math.sqrt(FR * hour * channels))
    high, low = two_parts(sub_tables())
    pick, twice = pick_tables()
    tables = [pick, np.concatenate([high, low], axis=0), turn_table(), column_table(), twist_table(), row_table(), twice]
    depth = LANES
    part = (hour, SLOTS, 2 * SPLIT, LANES)
    rows = (chan * hour, 2 * SPLIT, LANES)
    vmem, hbm = pl.BlockSpec(memory_space=pltpu.VMEM), pl.BlockSpec(memory_space=pl.ANY)
    sems = pltpu.SemaphoreType.DMA
    wave = pl.pallas_call(
        functools.partial(kernel, chan, hour),
        out_shape=pltpu.VMEM((OUT_ROWS, LANES), jnp.float32),
        in_specs=[hbm, hbm, vmem, vmem] + [hbm] * len(tables),
        out_specs=vmem,
        scratch_shapes=[pltpu.VMEM(table.shape, table.dtype) for table in tables]
        + [
            pltpu.VMEM((chan, per, FR), jnp.bfloat16),
            pltpu.VMEM((chan, per, count), jnp.bfloat16),
            pltpu.VMEM((8, depth), jnp.int32),
            pltpu.VMEM((chan, 8, depth), jnp.int32),
            pltpu.VMEM((SPLIT * per, SUB), jnp.bfloat16),
            pltpu.VMEM((SPLIT, channels, LANES), jnp.bfloat16),
            pltpu.VMEM((SPLIT, per, 2 * SUB), jnp.float32),
            pltpu.VMEM((SPLIT, channels, 2 * SUB), jnp.float32),
            pltpu.VMEM((TILES, SPLIT, 2, channels, LANES), jnp.float32),
            pltpu.VMEM((rows[0] * rows[1], SLOTS * rows[1]), jnp.bfloat16),
            pltpu.VMEM(part, jnp.bfloat16),
            pltpu.VMEM(part, jnp.bfloat16),
            pltpu.VMEM((rows[0] * rows[1], LANES), jnp.float32),
            pltpu.VMEM(rows, jnp.bfloat16),
            pltpu.VMEM(rows, jnp.bfloat16),
            sems((len(tables),)),
            sems((2,)),
        ]
        + [sems((chan,))] * 6
        + [sems((hour,))] * 2
        + [sems((5, hour))] * 2
        + [sems((1,))] * 2,
        compiler_params=pltpu.CompilerParams(
            collective_id=0, has_side_effects=True, vmem_limit_bytes=56 * 2**20
        ),
    )(
        traces.reshape(chan, per, FR),
        taps.reshape(chan, per, count),
        bin_ids.T,
        owners.reshape(1, -1),
        *[jnp.asarray(table) for table in tables],
    )
    return (wave * norm).reshape(1, 2 * FR)


def solution(mesh):
    placed = (P("chan", "hour"), P("chan", None), P(None, "chan"), P())

    def whole(traces, taps, bin_ids, owners):
        chan, hour = mesh.shape["chan"], mesh.shape["hour"]
        channels = traces.shape[0] // chan
        fits = (
            chan == 8
            and hour == TILES
            and channels % (16 * chan) == 0
            and traces.shape[1] == hour * FR
            and taps.shape[1] == SPLIT * LANES // 2
            and owners.shape[0] == chan * hour
        )
        return jax.shard_map(
            split_body if fits else body,
            mesh=mesh,
            in_specs=placed,
            out_specs=P(("chan", "hour"), None),
            check_vma=False,
        )(traces, taps, bin_ids, owners)

    return whole
```

```python
import functools
import math

import jax
import jax.numpy as jnp
import numpy as np
from jax import lax
from jax.experimental import pallas as pl
from jax.experimental.pallas import tpu as pltpu
from jax.sharding import PartitionSpec as P

FR = 4096
ROUNDS = 4
MESH = pl.DeviceIdType.MESH


exact = lax.Precision.HIGHEST

def passed_along(shard, axis, by):
    devices = lax.axis_size(axis)
    pairs = [(i, i + by) for i in range(devices) if 0 <= i + by < devices]
    return lax.ppermute(shard, axis, pairs)


def transform(real_part, imag_part, count):
    span = real_part.shape[-1]
    inner = 2 * span // 128
    lead = real_part.shape[:-1]
    first = jnp.arange(64, dtype=jnp.float32)[:, None]
    middle = jnp.arange(128, dtype=jnp.float32)[None, :]
    angle_one = 2.0 * math.pi / 128.0 * jnp.mod(first * middle, 128.0)
    cos_one = jnp.cos(angle_one)
    sin_one = -jnp.sin(angle_one)
    second = jnp.arange(inner, dtype=jnp.float32)[:, None]
    angle_turn = 2.0 * math.pi / (128.0 * inner) * jnp.mod(second * middle, 128.0 * inner)
    cos_turn = jnp.cos(angle_turn)
    sin_turn = -jnp.sin(angle_turn)
    outer = jnp.arange(count // 128, dtype=jnp.float32)[None, :]
    angle_two = 2.0 * math.pi / inner * jnp.mod(second * outer, float(inner))
    cos_two = jnp.cos(angle_two)
    sin_two = -jnp.sin(angle_two)
    grid = real_part.reshape(lead + (64, inner))
    section_re = jnp.einsum("...an,ak->...nk", grid, cos_one, precision=exact)
    section_im = jnp.einsum("...an,ak->...nk", grid, sin_one, precision=exact)
    if imag_part is not None:
        grid_im = imag_part.reshape(lead + (64, inner))
        section_re = section_re - jnp.einsum("...an,ak->...nk", grid_im, sin_one, precision=exact)
        section_im = section_im + jnp.einsum("...an,ak->...nk", grid_im, cos_one, precision=exact)
    turned_re = section_re * cos_turn - section_im * sin_turn
    turned_im = section_re * sin_turn + section_im * cos_turn
    out_re = jnp.einsum("...nk,nm->...mk", turned_re, cos_two, precision=exact) - jnp.einsum(
        "...nk,nm->...mk", turned_im, sin_two, precision=exact
    )
    out_im = jnp.einsum("...nk,nm->...mk", turned_re, sin_two, precision=exact) + jnp.einsum(
        "...nk,nm->...mk", turned_im, cos_two, precision=exact
    )
    return (out_re.reshape(lead + (count,)), out_im.reshape(lead + (count,)))


def filtered(samples, filters):
    channels = samples.shape[0]
    frames = samples.shape[1] // FR
    signal = samples.astype(jnp.float32).reshape(channels, frames, FR)
    freq_re, freq_im = transform(signal, None, FR)
    padded_taps = jnp.pad(filters.astype(jnp.float32), ((0, 0), (0, FR - filters.shape[1])))
    resp_re, resp_im = transform(padded_taps, None, FR)
    resp_re = resp_re[:, None, :]
    resp_im = resp_im[:, None, :]
    spec_re = (freq_re * resp_re - freq_im * resp_im).astype(jnp.bfloat16)
    spec_im = (freq_re * resp_im + freq_im * resp_re).astype(jnp.bfloat16)
    return (spec_re, spec_im)


def body(traces, taps, bin_ids, owners):
    channels = traces.shape[0]
    frames = traces.shape[1] // FR
    spec_re, spec_im = filtered(traces, taps)
    mine = lax.axis_index("chan")
    near_re = spec_re.astype(jnp.float32)
    near_im = spec_im.astype(jnp.float32)
    results = []
    for offset in range(ROUNDS):
        far_re, far_im = passed_along((spec_re, spec_im), "chan", offset + 1)
        far_re = far_re.astype(jnp.float32)
        far_im = far_im.astype(jnp.float32)
        cross_re = jnp.sum(far_re * near_re + far_im * near_im, axis=(0, 1))
        cross_im = jnp.sum(far_im * near_re - far_re * near_im, axis=(0, 1))
        results.append(jnp.stack([cross_re, cross_im]))
    contrib = jnp.stack(results)
    nbins = owners.shape[0]
    own_bins = bin_ids[:, 0]
    labels = jnp.arange(nbins, dtype=jnp.int32)
    places = jnp.sum(jnp.where(own_bins[:, None] == labels[None, :], owners[None, :], 0), axis=1)
    valid = jnp.arange(ROUNDS, dtype=jnp.int32) < mine
    places = jnp.where(valid, places, -1)
    width = contrib.shape[2]
    flat = contrib.reshape(ROUNDS, 2 * width)
    per_device = nbins // lax.axis_size("chan")
    rows = jnp.arange(lax.axis_size("chan") * per_device, dtype=jnp.int32)
    onehot = (places[None, :] == rows[:, None]).astype(jnp.float32)
    stacked = lax.psum_scatter(
        jnp.dot(onehot, flat, precision=exact, preferred_element_type=jnp.float32),
        "chan",
        scatter_dimension=0,
        tiled=True,
    )
    stacked = stacked.reshape(per_device, 2, width)
    final = lax.psum_scatter(stacked, "hour", scatter_dimension=0, tiled=True)
    weights = jnp.where(jnp.arange(FR) == 0, 1.0, 2.0).astype(jnp.float32)
    wave_re, wave_im = transform(final[:, 0] * weights, -final[:, 1] * weights, 2 * FR)
    norm = 1.0 / (FR * math.sqrt(FR * lax.axis_size("hour") * frames * channels))
    return wave_re * norm

SPLIT = 8
SUB = FR // SPLIT
LANES = 128
TILES = SUB // LANES


def sub_tables():
    a = np.arange(SUB)[:, None]
    k1 = np.arange(SUB)[None, :]
    turn = 2.0 * np.pi * ((a * k1) % (2 * SUB)) / (2 * SUB)
    cos, sin = np.cos(turn), -np.sin(turn)
    sin[:, 0] = 1.0 - 2.0 * (np.arange(SUB) % 2)
    table = np.stack([cos.reshape(SUB, TILES, LANES), sin.reshape(SUB, TILES, LANES)], axis=2)
    return table.reshape(SUB, 2 * SUB)


def two_parts(table):
    high = table.astype(jnp.bfloat16)
    low = (table - high.astype(np.float64)).astype(jnp.bfloat16)
    return high, low


PIECE = 512
SHARE = PIECE // SPLIT


def pick_tables():
    table = np.zeros((PIECE, SPLIT, 2, SHARE), np.float32)
    for n in range(SPLIT):
        for b in range(SHARE):
            table[SPLIT * b + n, n, :, b] = 1.0
    twice = table.reshape(PIECE, 2 * PIECE).astype(jnp.bfloat16)
    return np.ascontiguousarray(table[:, :, 0].reshape(PIECE, PIECE)).astype(jnp.bfloat16), twice


def turn_table():
    n = np.arange(SPLIT)[:, None]
    k1 = np.arange(SUB)[None, :]
    turn = 2.0 * np.pi * n * k1 / (2 * FR)
    table = np.stack([np.cos(turn), -np.sin(turn)], axis=1).reshape(SPLIT, 2, TILES, 1, LANES)
    table = np.broadcast_to(table.transpose(2, 0, 1, 3, 4), (TILES, SPLIT, 2, 8, LANES))
    return np.ascontiguousarray(table).astype(np.float32)


def times(value, angle):
    re, im = value
    c, s = math.cos(angle), math.sin(angle)
    if abs(s) < 1e-12:
        return (re, im) if c > 0 else (-re, -im)
    if abs(c) < 1e-12:
        return (-im, re) if s > 0 else (im, -re)
    if abs(abs(c) - abs(s)) < 1e-12:
        root = abs(c)
        p, q = math.copysign(1.0, c), math.copysign(1.0, s)
        first = (re if p > 0 else -re) + (-im if q > 0 else im)
        second = (re if q > 0 else -re) + (im if p > 0 else -im)
        return first * root, second * root
    return re * c - im * s, re * s + im * c


def small_dft(values, sign, half=False):
    size = len(values)
    if size == 1:
        return values
    even = small_dft(values[0::2], sign)
    odd = small_dft(values[1::2], sign)
    low, high = [], []
    for k in range(size // 2):
        turned = times(odd[k], sign * 2.0 * math.pi * k / size)
        low.append((even[k][0] + turned[0], even[k][1] + turned[1]))
        if not half:
            high.append((even[k][0] - turned[0], even[k][1] - turned[1]))
    return low + high


LATE = 8
SLOTS = 32


def slot_of(step, before, chan):
    if isinstance(step, int) and step == chan - 1:
        return before
    return LATE + step * (step - 1) // 2 + before


def rows_of_pairs(ids, owners):
    depth = ids.shape[1]
    nbins = owners.shape[1]
    bins = lax.broadcasted_iota(jnp.int32, (nbins, depth), 0) + 1
    picked = (bins == ids[0:1, :]).astype(jnp.float32).astype(jnp.bfloat16)
    row = lax.broadcasted_iota(jnp.int32, (nbins, nbins), 0)
    moved = (row == owners[...]).astype(jnp.float32).astype(jnp.bfloat16)
    return jnp.dot(moved, picked, preferred_element_type=jnp.float32).astype(jnp.bfloat16)


def fold(values):
    sublane = lax.broadcasted_iota(jnp.int32, values[0].shape, 0)
    shift = 1
    while len(values) > 1:
        first = lax.rem(lax.div(sublane, shift), 2) == 0
        values = [
            jnp.where(first, a, b) + pltpu.roll(jnp.where(first, b, a), SPLIT - shift, 0)
            for a, b in zip(values[0::2], values[1::2])
        ]
        shift *= 2
    return values[0]


OUT_ROWS = 2 * FR // LANES
TERMS = 2 * SPLIT * (TILES + 1)


def column_table():
    v = np.arange(LANES)[:, None]
    t, k2 = np.arange(TILES)[None, :, None], np.arange(SPLIT)[None, None, :]
    main = 2.0 * np.pi * ((v[:, :, None] * (SPLIT * k2 + t)) % OUT_ROWS) / OUT_ROWS
    extra = 2.0 * np.pi * ((v * (SPLIT // 2 + SPLIT * (np.arange(SPLIT)[None, :] - SPLIT // 2))) % OUT_ROWS) / OUT_ROWS
    phase = np.concatenate([main, extra[:, None, :]], axis=1)
    top = np.stack([np.cos(phase), -np.sin(phase)], axis=2).reshape(LANES, TERMS)
    under = np.stack([np.sin(phase), np.cos(phase)], axis=2).reshape(LANES, TERMS)
    high, low = two_parts(np.concatenate([top, under], axis=0))
    rest = np.zeros((2 * LANES, 2 * LANES - 3 * TERMS), jnp.bfloat16)
    return np.concatenate([high, high, low, rest], axis=1)


def twist_table():
    turn = 2.0 * np.pi * np.arange(LANES)[:, None] * np.arange(LANES)[None, :] / (2 * FR)
    return np.stack([np.cos(turn), np.sin(turn)]).astype(np.float32)


def row_table():
    turn = 2.0 * np.pi * ((np.arange(OUT_ROWS)[:, None] * np.arange(LANES)[None, :]) % OUT_ROWS) / OUT_ROWS
    high, low = two_parts(np.concatenate([np.cos(turn), -np.sin(turn)], axis=1))
    return np.concatenate([high, high, low], axis=1)


def halves(value):
    top = value.astype(jnp.bfloat16)
    return top, (value - top.astype(jnp.float32)).astype(jnp.bfloat16)


def over_lanes(a, b):
    return lax.dot_general(a, b, (((1,), (1,)), ((), ())), preferred_element_type=jnp.float32)


def inverse(rows, column, twist, across):
    lane = lax.broadcasted_iota(jnp.int32, rows.shape, 1)
    slot = lax.broadcasted_iota(jnp.int32, rows.shape, 0)
    rows = rows * jnp.where((lane == 0) & (slot == 0), 1.0, 2.0)
    apart = (lane == 0) & (slot < 2 * SPLIT) & (lax.rem(slot, SPLIT) >= SPLIT // 2)
    every = jnp.concatenate(
        [jnp.where(apart, 0.0, rows), jnp.where(apart, rows, 0.0)[: 2 * SPLIT]], axis=0
    )
    top, rest = halves(every)
    nothing = jnp.zeros((2 * LANES - 3 * TERMS, LANES), jnp.bfloat16)
    z = jnp.dot(
        column[...], jnp.concatenate([top, rest, top, nothing], axis=0), preferred_element_type=jnp.float32
    )
    z_re, z_im = z[:LANES], z[LANES:]
    c, s = twist[0], twist[1]
    y = jnp.concatenate([z_re * c - z_im * s, z_re * s + z_im * c], axis=1)
    top, rest = halves(y)
    return over_lanes(across[...], jnp.concatenate([top, rest, top], axis=1))


def kernel(chan, hour, x, taps, bin_ids, owners, *refs):
    tables, out = refs[:7], refs[7]
    held = refs[8:15]
    pick, high, turns, column, twist = held[:5]
    across, twice = held[5:]
    xin, tin, ids, ids_in, xd, td, fx, fh, spec, kron, part, first, early, outbox, inbox = refs[15:30]
    table_sem, own_sem, ids_send, ids_recv, t_send, t_recv, x_send, x_recv = refs[30:38]
    f_send, f_recv, send, recv, send2, recv2 = refs[38:]
    me, my_hour = lax.axis_index("chan"), lax.axis_index("hour")
    per = xin.shape[1]
    share = pl.ds(pl.multiple_of(my_hour * (tin.shape[2] // hour), LANES), tin.shape[2] // hour)

    def flipped(at, o, size):
        to, bit = at, 1
        while bit < size:
            to = to + lax.rem(lax.div(o, bit), 2) * bit * (1 - 2 * lax.rem(lax.div(at, bit), 2))
            bit *= 2
        return to

    def partner(o):
        return flipped(me, o, chan)

    def beside(o):
        return flipped(my_hour, o, hour)

    def sent(src, dst, sends, recvs, **device):
        return pltpu.make_async_remote_copy(
            src_ref=src, dst_ref=dst, send_sem=sends, recv_sem=recvs, device_id=device, device_id_type=MESH
        )

    loads = [pltpu.make_async_copy(src, dst, table_sem.at[z]) for z, (src, dst) in enumerate(zip(tables, held))]
    own = [
        pltpu.make_async_copy(x.at[me], xin.at[me], own_sem.at[0]),
        pltpu.make_async_copy(taps.at[me, :, share], tin.at[me, :, share], own_sem.at[1]),
    ]
    barrier = pltpu.get_barrier_semaphore()
    for o in range(1, hour):
        pl.semaphore_signal(
            barrier, inc=1, device_id={"hour": lax.rem(my_hour + o, hour)}, device_id_type=MESH
        )
    for o in range(1, chan):
        pl.semaphore_signal(barrier, inc=1, device_id={"chan": partner(o)}, device_id_type=MESH)
    for copy in own + loads:
        copy.start()
    place = lax.broadcasted_iota(jnp.int32, ids.shape, 1)
    labels = jnp.zeros(ids.shape, jnp.int32)
    for r in range(ROUNDS):
        live = (place == me * ROUNDS + r) & (me >= r + 1)
        labels = jnp.where(live, bin_ids[:, r : r + 1] + 1, labels)
    ids[...] = labels
    pl.semaphore_wait(barrier, chan + hour - 2)

    def x_copy(o):
        to = partner(o)
        return sent(x.at[to], xin.at[me], x_send.at[o], x_recv.at[o], chan=to)

    far_first = sorted(range(1, chan), key=lambda o: -(o.bit_length()))
    tap_copies, id_copies = [], []
    for o in far_first:
        to = partner(o)
        tap_copies.append(
            sent(taps.at[to, :, share], tin.at[me, :, share], t_send.at[o], t_recv.at[o], chan=to)
        )
        tap_copies[-1].start()
    for o in far_first:
        id_copies.append(
            sent(ids.at[0:1], ids_in.at[o, 0:1], ids_send.at[o], ids_recv.at[o], chan=partner(o))
        )
        id_copies[-1].start()
    for o in range(1, chan):
        x_copy(o).start()
    lane0 = lax.broadcasted_iota(jnp.int32, (8, LANES), 1) == 0

    def bins_of(f, rows, t, edge):
        values, extra = [], []
        for n in range(SPLIT):
            re = f[n, rows, pl.ds(pl.multiple_of(2 * t * LANES, LANES), LANES)]
            im = f[n, rows, pl.ds(pl.multiple_of((2 * t + 1) * LANES, LANES), LANES)]
            if edge:
                angle = -math.pi * n / SPLIT
                extra.append((im * math.cos(angle), im * math.sin(angle)))
                im = jnp.where(lane0, 0.0, im)
            if n == 0:
                values.append((re, im))
            else:
                c, s = turns[t, n, 0], turns[t, n, 1]
                values.append((re * c - im * s, re * s + im * c))
        found = small_dft(values, -1)
        if edge:
            more = small_dft(extra, -1, half=True)
            for k2 in range(SPLIT // 2):
                old = found[SPLIT // 2 + k2]
                found[SPLIT // 2 + k2] = tuple(jnp.where(lane0, more[k2][z], old[z]) for z in range(2))
        return found

    def responses(t, edge):
        @pl.loop(0, chan * per // 8)
        def _(g):
            here = pl.ds(pl.multiple_of(8 * g, 8), 8)
            for k2, (hr, hi) in enumerate(bins_of(fh, here, t, edge)):
                spec[t, k2, 0, here, :] = hr
                spec[t, k2, 1, here, :] = hi

    def spectra(block, t, edge):
        for g in range(per // 8):
            here = pl.ds(pl.multiple_of(block * per + 8 * g, 8), 8)
            for k2, (xr, xi) in enumerate(bins_of(fx, slice(8 * g, 8 * g + 8), t, edge)):
                hr, hi = spec[t, k2, 0, here, :], spec[t, k2, 1, here, :]
                spec[t, k2, 0, here, :] = (xr * hr - xi * hi).astype(jnp.bfloat16).astype(jnp.float32)
                spec[t, k2, 1, here, :] = (xr * hi + xi * hr).astype(jnp.bfloat16).astype(jnp.float32)

    half = lax.broadcasted_iota(jnp.int32, (per, LANES), 1) < SHARE

    def transform_of(block):
        flat = jnp.concatenate([xin[block, :, q * PIECE : (q + 1) * PIECE] for q in range(FR // PIECE)], axis=0)
        got = jnp.dot(flat, pick[...], preferred_element_type=jnp.float32)
        for g in range(TILES):
            for n in range(SPLIT):
                a, b = (
                    got[q * per : (q + 1) * per, n // 2 * LANES : (n // 2 + 1) * LANES] for q in (2 * g, 2 * g + 1)
                )
                if n % 2:
                    a = pltpu.roll(a, SHARE, 1)
                else:
                    b = pltpu.roll(b, SHARE, 1)
                xd[n * per : (n + 1) * per, g * LANES : (g + 1) * LANES] = jnp.where(half, a, b).astype(jnp.bfloat16)
        found = jnp.dot(jnp.concatenate([xd[...], xd[...]], axis=1), high[...], preferred_element_type=jnp.float32)
        for n in range(SPLIT):
            fx[n] = found[n * per : (n + 1) * per]

    def spectra_of(block):
        spectra(block, 0, True)

        @pl.loop(1, TILES)
        def _(t):
            spectra(block, t, False)

    def take(block):
        transform_of(block)
        spectra_of(block)

    for copy in loads + own[:1]:
        copy.wait()
    transform_of(me)
    own[1].wait()
    for copy in tap_copies:
        copy.wait_recv()
    forwards = []
    for o in range(1, hour):
        to = lax.rem(my_hour + o, hour)
        forwards.append(sent(tin.at[:, :, share], tin.at[:, :, share], f_send.at[o], f_recv.at[o], hour=to))
        forwards[-1].start()
    for copy in id_copies:
        copy.wait_recv()
    labels = ids[0:1, :]
    for o in range(1, chan):
        labels = labels + ids_in[o, 0:1, :]
    by_pair = rows_of_pairs(labels, owners)
    nbins = chan * hour
    pair = lax.broadcasted_iota(jnp.int32, (ids.shape[1], SLOTS), 0)
    column_of = lax.broadcasted_iota(jnp.int32, (ids.shape[1], SLOTS), 1)
    places = jnp.zeros(pair.shape, jnp.float32)
    for s in range(1, chan):
        for j in range(s):
            near, far = jnp.maximum(partner(s), partner(j)), jnp.minimum(partner(s), partner(j))
            held_by = jnp.where(near - far <= ROUNDS, near * ROUNDS + near - far - 1, -1)
            hit = (column_of == slot_of(s, j, chan)) & (pair == held_by)
            places = jnp.where(hit, 1.0, places)
    by_slot = jnp.dot(by_pair, places.astype(jnp.bfloat16), preferred_element_type=jnp.float32).astype(jnp.bfloat16)
    deep = 2 * SPLIT
    spread = (
        lax.div(lax.broadcasted_iota(jnp.int32, (nbins * deep, nbins), 0), deep)
        == lax.broadcasted_iota(jnp.int32, (nbins * deep, nbins), 1)
    ).astype(jnp.float32).astype(jnp.bfloat16)
    widen = (
        lax.div(lax.broadcasted_iota(jnp.int32, (SLOTS, SLOTS * deep), 1), deep)
        == lax.broadcasted_iota(jnp.int32, (SLOTS, SLOTS * deep), 0)
    ).astype(jnp.float32).astype(jnp.bfloat16)
    tall = jnp.dot(spread, by_slot, preferred_element_type=jnp.float32).astype(jnp.bfloat16)
    both = jnp.dot(tall, widen, preferred_element_type=jnp.float32)
    same = lax.rem(lax.broadcasted_iota(jnp.int32, both.shape, 0), deep) == lax.rem(
        lax.broadcasted_iota(jnp.int32, both.shape, 1), deep
    )
    kron[...] = jnp.where(same, both, 0.0).astype(jnp.bfloat16)

    def cross(t, near, far, slot):
        res, ims = [], []
        for k2 in range(SPLIT):
            re = im = None
            for c in range(per // 8):
                at = pl.ds(pl.multiple_of(near * per + 8 * c, 8), 8)
                of = pl.ds(pl.multiple_of(far * per + 8 * c, 8), 8)
                nr, ni = spec[t, k2, 0, at, :], spec[t, k2, 1, at, :]
                fr, fi = spec[t, k2, 0, of, :], spec[t, k2, 1, of, :]
                one, two = fr * nr + fi * ni, fi * nr - fr * ni
                re, im = (one, two) if re is None else (re + one, im + two)
            res.append(re)
            ims.append(im)
        part[t, slot] = jnp.concatenate([fold(res), fold(ims)], axis=0).astype(jnp.bfloat16)

    def crosses(s, begin):
        @pl.loop(0, s)
        def _(j):
            a, b = partner(s), partner(j)
            for t in range(TILES):
                cross(t, jnp.maximum(a, b), jnp.minimum(a, b), begin + j)

    def part_copy(z, o, begin, count):
        where = pl.ds(begin, count)
        return sent(part.at[beside(o), where], first.at[o, where], send.at[z, o], recv.at[z, o], hour=beside(o))

    groups = [(LATE, 6), (LATE + 6, 4), (LATE + 10, 5), (LATE + 15, 6), (0, 7)]
    order = [2, 3, 1, 0]
    for copy in forwards:
        copy.wait_recv()
    count = tin.shape[2]
    got = jnp.dot(tin[...].reshape(chan * per, count), twice[...], preferred_element_type=jnp.float32)
    for n in range(SPLIT):
        td[n] = got[:, n * LANES : (n + 1) * LANES].astype(jnp.bfloat16)
    found = jnp.dot(
        td[...].reshape(SPLIT * chan * per, LANES),
        jnp.concatenate([high[:SHARE, :], high[SUB : SUB + SHARE, :]], axis=0),
        preferred_element_type=jnp.float32,
    )
    for n in range(SPLIT):
        fh[n] = found[n * chan * per : (n + 1) * chan * per]
    responses(0, True)

    @pl.loop(1, TILES)
    def _(t):
        responses(t, False)

    spectra_of(me)

    @pl.loop(1, chan // 2)
    def _(s):
        x_copy(s).wait_recv()
        take(partner(s))
        crosses(s, LATE + lax.div(s * (s - 1), 2))

    for o in order[:3]:
        part_copy(0, o, *groups[0]).start()

    @pl.loop(chan // 2, chan - 1)
    def _(s):
        x_copy(s).wait_recv()
        take(partner(s))
        crosses(s, LATE + lax.div(s * (s - 1), 2))

        for z in range(1, len(groups) - 1):

            @pl.when(s == z + 3)
            def _():
                for o in order[:3]:
                    part_copy(z, o, *groups[z]).start()

    x_copy(chan - 1).wait_recv()
    block = partner(chan - 1)
    transform_of(block)

    @pl.loop(0, TILES)
    def _(z):
        late = lax.div(z, 2)
        o = (1 - late) * (2 + z) + late * (3 - z)
        t = beside(o)

        @pl.when(t == 0)
        def _():
            spectra(block, 0, True)

        @pl.when(t > 0)
        def _():
            spectra(block, t, False)

        for j in range(chan - 1):
            cross(t, jnp.maximum(block, partner(j)), jnp.minimum(block, partner(j)), j)

        @pl.when(o > 0)
        def _():
            part_copy(4, o, *groups[4]).start()

    def summed(begin, count, room):
        where = slice(begin, begin + count)
        total = part[my_hour, where].astype(jnp.float32)
        for o in range(1, hour):
            total = total + first[o, where].astype(jnp.float32)
        total = total.reshape(count * deep, LANES)
        if room > count:
            total = jnp.concatenate([total, jnp.zeros(((room - count) * deep, LANES), jnp.float32)], axis=0)
        return jnp.concatenate(halves(total), axis=1)

    def mixed(rows, begin, room, values):
        got = jnp.dot(
            kron[rows, begin * deep : (begin + room) * deep], values, preferred_element_type=jnp.float32
        )
        return got[:, :LANES] + got[:, LANES:]

    for z in range(len(groups) - 1):
        for o in range(1, hour):
            part_copy(z, o, *groups[z]).wait_recv()
    early[...] = mixed(slice(None), LATE, SLOTS - LATE, summed(LATE, 21, SLOTS - LATE))
    for o in range(1, hour):
        part_copy(4, o, *groups[4]).wait_recv()
    late = summed(0, 7, LATE)
    side = nbins // 2
    for z in range(2):
        half_of = 1 - lax.div(me, chan // 2) if z == 0 else lax.div(me, chan // 2)
        deep_rows = pl.ds(pl.multiple_of(half_of * side * deep, side * deep), side * deep)
        outbox[pl.ds(half_of * side, side)] = (
            (mixed(deep_rows, 0, LATE, late) + early[deep_rows, :]).astype(jnp.bfloat16).reshape(side, deep, LANES)
        )
        for oc in (5, 4, 7, 6) if z == 0 else (3, 2, 1, 0):
            for o in (0, 1, 2, 3):
                if oc or o:
                    to, at = partner(oc), beside(o)
                    sent(
                        outbox.at[to * hour + at],
                        inbox.at[oc * hour + my_hour],
                        send2.at[0],
                        recv2.at[0],
                        chan=to,
                        hour=at,
                    ).start()
    inbox[my_hour] = outbox[me * hour + my_hour]
    for copy in tap_copies + id_copies + forwards:
        copy.wait_send()
    for o in range(1, chan):
        x_copy(o).wait_send()
    for z in range(len(groups)):
        for o in range(1, hour):
            part_copy(z, o, *groups[z]).wait_send()

    others = pl.ds(0, chan * hour - 1)
    all_rows = sent(outbox.at[others], inbox.at[others], send2.at[0], recv2.at[0], chan=partner(1))
    all_rows.wait_recv()
    rows = inbox[0:hour].astype(jnp.float32)
    for oc in range(1, chan):
        rows = rows + inbox[oc * hour : (oc + 1) * hour].astype(jnp.float32)
    wave = inverse(rows.reshape(TILES * deep, LANES), column, twist, across)
    out[...] = wave
    all_rows.wait_send()


def split_body(traces, taps, bin_ids, owners):
    chan, hour = lax.axis_size("chan"), lax.axis_size("hour")
    channels, count = taps.shape
    per = channels // chan
    norm = 1.0 / (FR * math.sqrt(FR * hour * channels))
    high, low = two_parts(sub_tables())
    pick, twice = pick_tables()
    tables = [pick, np.concatenate([high, low], axis=0), turn_table(), column_table(), twist_table(), row_table(), twice]
    depth = LANES
    part = (hour, SLOTS, 2 * SPLIT, LANES)
    rows = (chan * hour, 2 * SPLIT, LANES)
    vmem, hbm = pl.BlockSpec(memory_space=pltpu.VMEM), pl.BlockSpec(memory_space=pl.ANY)
    sems = pltpu.SemaphoreType.DMA
    wave = pl.pallas_call(
        functools.partial(kernel, chan, hour),
        out_shape=pltpu.VMEM((OUT_ROWS, LANES), jnp.float32),
        in_specs=[hbm, hbm, vmem, vmem] + [hbm] * len(tables),
        out_specs=vmem,
        scratch_shapes=[pltpu.VMEM(table.shape, table.dtype) for table in tables]
        + [
            pltpu.VMEM((chan, per, FR), jnp.bfloat16),
            pltpu.VMEM((chan, per, count), jnp.bfloat16),
            pltpu.VMEM((8, depth), jnp.int32),
            pltpu.VMEM((chan, 8, depth), jnp.int32),
            pltpu.VMEM((SPLIT * per, SUB), jnp.bfloat16),
            pltpu.VMEM((SPLIT, channels, LANES), jnp.bfloat16),
            pltpu.VMEM((SPLIT, per, 2 * SUB), jnp.float32),
            pltpu.VMEM((SPLIT, channels, 2 * SUB), jnp.float32),
            pltpu.VMEM((TILES, SPLIT, 2, channels, LANES), jnp.float32),
            pltpu.VMEM((rows[0] * rows[1], SLOTS * rows[1]), jnp.bfloat16),
            pltpu.VMEM(part, jnp.bfloat16),
            pltpu.VMEM(part, jnp.bfloat16),
            pltpu.VMEM((rows[0] * rows[1], LANES), jnp.float32),
            pltpu.VMEM(rows, jnp.bfloat16),
            pltpu.VMEM(rows, jnp.bfloat16),
            sems((len(tables),)),
            sems((2,)),
        ]
        + [sems((chan,))] * 6
        + [sems((hour,))] * 2
        + [sems((5, hour))] * 2
        + [sems((1,))] * 2,
        compiler_params=pltpu.CompilerParams(
            collective_id=0, has_side_effects=True, vmem_limit_bytes=56 * 2**20
        ),
    )(
        traces.reshape(chan, per, FR),
        taps.reshape(chan, per, count),
        bin_ids.T,
        owners.reshape(1, -1),
        *[jnp.asarray(table) for table in tables],
    )
    return (wave * norm).reshape(1, 2 * FR)


def solution(mesh):
    placed = (P("chan", "hour"), P("chan", None), P(None, "chan"), P())

    def whole(traces, taps, bin_ids, owners):
        chan, hour = mesh.shape["chan"], mesh.shape["hour"]
        channels = traces.shape[0] // chan
        fits = (
            chan == 8
            and hour == TILES
            and channels % (16 * chan) == 0
            and traces.shape[1] == hour * FR
            and taps.shape[1] == SPLIT * LANES // 2
            and owners.shape[0] == chan * hour
        )
        return jax.shard_map(
            split_body if fits else body,
            mesh=mesh,
            in_specs=placed,
            out_specs=P(("chan", "hour"), None),
            check_vma=False,
        )(traces, taps, bin_ids, owners)

    return whole
```

```python
import functools
import math

import jax
import jax.numpy as jnp
import numpy as np
from jax import lax
from jax.experimental import pallas as pl
from jax.experimental.pallas import tpu as pltpu
from jax.sharding import PartitionSpec as P

FR = 4096
ROUNDS = 4
MESH = pl.DeviceIdType.MESH


exact = lax.Precision.HIGHEST

def passed_along(shard, axis, by):
    devices = lax.axis_size(axis)
    pairs = [(i, i + by) for i in range(devices) if 0 <= i + by < devices]
    return lax.ppermute(shard, axis, pairs)


def transform(real_part, imag_part, count):
    span = real_part.shape[-1]
    inner = 2 * span // 128
    lead = real_part.shape[:-1]
    first = jnp.arange(64, dtype=jnp.float32)[:, None]
    middle = jnp.arange(128, dtype=jnp.float32)[None, :]
    angle_one = 2.0 * math.pi / 128.0 * jnp.mod(first * middle, 128.0)
    cos_one = jnp.cos(angle_one)
    sin_one = -jnp.sin(angle_one)
    second = jnp.arange(inner, dtype=jnp.float32)[:, None]
    angle_turn = 2.0 * math.pi / (128.0 * inner) * jnp.mod(second * middle, 128.0 * inner)
    cos_turn = jnp.cos(angle_turn)
    sin_turn = -jnp.sin(angle_turn)
    outer = jnp.arange(count // 128, dtype=jnp.float32)[None, :]
    angle_two = 2.0 * math.pi / inner * jnp.mod(second * outer, float(inner))
    cos_two = jnp.cos(angle_two)
    sin_two = -jnp.sin(angle_two)
    grid = real_part.reshape(lead + (64, inner))
    section_re = jnp.einsum("...an,ak->...nk", grid, cos_one, precision=exact)
    section_im = jnp.einsum("...an,ak->...nk", grid, sin_one, precision=exact)
    if imag_part is not None:
        grid_im = imag_part.reshape(lead + (64, inner))
        section_re = section_re - jnp.einsum("...an,ak->...nk", grid_im, sin_one, precision=exact)
        section_im = section_im + jnp.einsum("...an,ak->...nk", grid_im, cos_one, precision=exact)
    turned_re = section_re * cos_turn - section_im * sin_turn
    turned_im = section_re * sin_turn + section_im * cos_turn
    out_re = jnp.einsum("...nk,nm->...mk", turned_re, cos_two, precision=exact) - jnp.einsum(
        "...nk,nm->...mk", turned_im, sin_two, precision=exact
    )
    out_im = jnp.einsum("...nk,nm->...mk", turned_re, sin_two, precision=exact) + jnp.einsum(
        "...nk,nm->...mk", turned_im, cos_two, precision=exact
    )
    return (out_re.reshape(lead + (count,)), out_im.reshape(lead + (count,)))


def filtered(samples, filters):
    channels = samples.shape[0]
    frames = samples.shape[1] // FR
    signal = samples.astype(jnp.float32).reshape(channels, frames, FR)
    freq_re, freq_im = transform(signal, None, FR)
    padded_taps = jnp.pad(filters.astype(jnp.float32), ((0, 0), (0, FR - filters.shape[1])))
    resp_re, resp_im = transform(padded_taps, None, FR)
    resp_re = resp_re[:, None, :]
    resp_im = resp_im[:, None, :]
    spec_re = (freq_re * resp_re - freq_im * resp_im).astype(jnp.bfloat16)
    spec_im = (freq_re * resp_im + freq_im * resp_re).astype(jnp.bfloat16)
    return (spec_re, spec_im)


def body(traces, taps, bin_ids, owners):
    channels = traces.shape[0]
    frames = traces.shape[1] // FR
    spec_re, spec_im = filtered(traces, taps)
    mine = lax.axis_index("chan")
    near_re = spec_re.astype(jnp.float32)
    near_im = spec_im.astype(jnp.float32)
    results = []
    for offset in range(ROUNDS):
        far_re, far_im = passed_along((spec_re, spec_im), "chan", offset + 1)
        far_re = far_re.astype(jnp.float32)
        far_im = far_im.astype(jnp.float32)
        cross_re = jnp.sum(far_re * near_re + far_im * near_im, axis=(0, 1))
        cross_im = jnp.sum(far_im * near_re - far_re * near_im, axis=(0, 1))
        results.append(jnp.stack([cross_re, cross_im]))
    contrib = jnp.stack(results)
    nbins = owners.shape[0]
    own_bins = bin_ids[:, 0]
    labels = jnp.arange(nbins, dtype=jnp.int32)
    places = jnp.sum(jnp.where(own_bins[:, None] == labels[None, :], owners[None, :], 0), axis=1)
    valid = jnp.arange(ROUNDS, dtype=jnp.int32) < mine
    places = jnp.where(valid, places, -1)
    width = contrib.shape[2]
    flat = contrib.reshape(ROUNDS, 2 * width)
    per_device = nbins // lax.axis_size("chan")
    rows = jnp.arange(lax.axis_size("chan") * per_device, dtype=jnp.int32)
    onehot = (places[None, :] == rows[:, None]).astype(jnp.float32)
    stacked = lax.psum_scatter(
        jnp.dot(onehot, flat, precision=exact, preferred_element_type=jnp.float32),
        "chan",
        scatter_dimension=0,
        tiled=True,
    )
    stacked = stacked.reshape(per_device, 2, width)
    final = lax.psum_scatter(stacked, "hour", scatter_dimension=0, tiled=True)
    weights = jnp.where(jnp.arange(FR) == 0, 1.0, 2.0).astype(jnp.float32)
    wave_re, wave_im = transform(final[:, 0] * weights, -final[:, 1] * weights, 2 * FR)
    norm = 1.0 / (FR * math.sqrt(FR * lax.axis_size("hour") * frames * channels))
    return wave_re * norm

SPLIT = 8
SUB = FR // SPLIT
LANES = 128
TILES = SUB // LANES


def sub_tables():
    a = np.arange(SUB)[:, None]
    k1 = np.arange(SUB)[None, :]
    turn = 2.0 * np.pi * ((a * k1) % (2 * SUB)) / (2 * SUB)
    cos, sin = np.cos(turn), -np.sin(turn)
    sin[:, 0] = 1.0 - 2.0 * (np.arange(SUB) % 2)
    table = np.stack([cos.reshape(SUB, TILES, LANES), sin.reshape(SUB, TILES, LANES)], axis=2)
    return table.reshape(SUB, 2 * SUB)


def two_parts(table):
    high = table.astype(jnp.bfloat16)
    low = (table - high.astype(np.float64)).astype(jnp.bfloat16)
    return high, low


PIECE = 512
SHARE = PIECE // SPLIT


def pick_tables():
    table = np.zeros((PIECE, SPLIT, 2, SHARE), np.float32)
    for n in range(SPLIT):
        for b in range(SHARE):
            table[SPLIT * b + n, n, :, b] = 1.0
    twice = table.reshape(PIECE, 2 * PIECE).astype(jnp.bfloat16)
    return np.ascontiguousarray(table[:, :, 0].reshape(PIECE, PIECE)).astype(jnp.bfloat16), twice


def turn_table():
    n = np.arange(SPLIT)[:, None]
    k1 = np.arange(SUB)[None, :]
    turn = 2.0 * np.pi * n * k1 / (2 * FR)
    table = np.stack([np.cos(turn), -np.sin(turn)], axis=1).reshape(SPLIT, 2, TILES, 1, LANES)
    table = np.broadcast_to(table.transpose(2, 0, 1, 3, 4), (TILES, SPLIT, 2, 8, LANES))
    return np.ascontiguousarray(table).astype(np.float32)


def times(value, angle):
    re, im = value
    c, s = math.cos(angle), math.sin(angle)
    if abs(s) < 1e-12:
        return (re, im) if c > 0 else (-re, -im)
    if abs(c) < 1e-12:
        return (-im, re) if s > 0 else (im, -re)
    if abs(abs(c) - abs(s)) < 1e-12:
        root = abs(c)
        p, q = math.copysign(1.0, c), math.copysign(1.0, s)
        first = (re if p > 0 else -re) + (-im if q > 0 else im)
        second = (re if q > 0 else -re) + (im if p > 0 else -im)
        return first * root, second * root
    return re * c - im * s, re * s + im * c


def small_dft(values, sign, half=False):
    size = len(values)
    if size == 1:
        return values
    even = small_dft(values[0::2], sign)
    odd = small_dft(values[1::2], sign)
    low, high = [], []
    for k in range(size // 2):
        turned = times(odd[k], sign * 2.0 * math.pi * k / size)
        low.append((even[k][0] + turned[0], even[k][1] + turned[1]))
        if not half:
            high.append((even[k][0] - turned[0], even[k][1] - turned[1]))
    return low + high


LATE = 8
SLOTS = 32


def slot_of(step, before, chan):
    if isinstance(step, int) and step == chan - 1:
        return before
    return LATE + step * (step - 1) // 2 + before


def rows_of_pairs(ids, owners):
    depth = ids.shape[1]
    nbins = owners.shape[1]
    bins = lax.broadcasted_iota(jnp.int32, (nbins, depth), 0) + 1
    picked = (bins == ids[0:1, :]).astype(jnp.float32).astype(jnp.bfloat16)
    row = lax.broadcasted_iota(jnp.int32, (nbins, nbins), 0)
    moved = (row == owners[...]).astype(jnp.float32).astype(jnp.bfloat16)
    return jnp.dot(moved, picked, preferred_element_type=jnp.float32).astype(jnp.bfloat16)


def fold(values):
    sublane = lax.broadcasted_iota(jnp.int32, values[0].shape, 0)
    shift = 1
    while len(values) > 1:
        first = lax.rem(lax.div(sublane, shift), 2) == 0
        values = [
            jnp.where(first, a, b) + pltpu.roll(jnp.where(first, b, a), SPLIT - shift, 0)
            for a, b in zip(values[0::2], values[1::2])
        ]
        shift *= 2
    return values[0]


OUT_ROWS = 2 * FR // LANES
TERMS = 2 * SPLIT * (TILES + 1)


def column_table():
    v = np.arange(LANES)[:, None]
    t, k2 = np.arange(TILES)[None, :, None], np.arange(SPLIT)[None, None, :]
    main = 2.0 * np.pi * ((v[:, :, None] * (SPLIT * k2 + t)) % OUT_ROWS) / OUT_ROWS
    extra = 2.0 * np.pi * ((v * (SPLIT // 2 + SPLIT * (np.arange(SPLIT)[None, :] - SPLIT // 2))) % OUT_ROWS) / OUT_ROWS
    phase = np.concatenate([main, extra[:, None, :]], axis=1)
    top = np.stack([np.cos(phase), -np.sin(phase)], axis=2).reshape(LANES, TERMS)
    under = np.stack([np.sin(phase), np.cos(phase)], axis=2).reshape(LANES, TERMS)
    high, low = two_parts(np.concatenate([top, under], axis=0))
    rest = np.zeros((2 * LANES, 2 * LANES - 3 * TERMS), jnp.bfloat16)
    return np.concatenate([high, high, low, rest], axis=1)


def twist_table():
    turn = 2.0 * np.pi * np.arange(LANES)[:, None] * np.arange(LANES)[None, :] / (2 * FR)
    return np.stack([np.cos(turn), np.sin(turn)]).astype(np.float32)


def row_table():
    turn = 2.0 * np.pi * ((np.arange(OUT_ROWS)[:, None] * np.arange(LANES)[None, :]) % OUT_ROWS) / OUT_ROWS
    high, low = two_parts(np.concatenate([np.cos(turn), -np.sin(turn)], axis=1))
    return np.concatenate([high, high, low], axis=1)


def halves(value):
    top = value.astype(jnp.bfloat16)
    return top, (value - top.astype(jnp.float32)).astype(jnp.bfloat16)


def over_lanes(a, b):
    return lax.dot_general(a, b, (((1,), (1,)), ((), ())), preferred_element_type=jnp.float32)


def inverse(rows, column, twist, across):
    lane = lax.broadcasted_iota(jnp.int32, rows.shape, 1)
    slot = lax.broadcasted_iota(jnp.int32, rows.shape, 0)
    rows = rows * jnp.where((lane == 0) & (slot == 0), 1.0, 2.0)
    apart = (lane == 0) & (slot < 2 * SPLIT) & (lax.rem(slot, SPLIT) >= SPLIT // 2)
    every = jnp.concatenate(
        [jnp.where(apart, 0.0, rows), jnp.where(apart, rows, 0.0)[: 2 * SPLIT]], axis=0
    )
    top, rest = halves(every)
    nothing = jnp.zeros((2 * LANES - 3 * TERMS, LANES), jnp.bfloat16)
    z = jnp.dot(
        column[...], jnp.concatenate([top, rest, top, nothing], axis=0), preferred_element_type=jnp.float32
    )
    z_re, z_im = z[:LANES], z[LANES:]
    c, s = twist[0], twist[1]
    y = jnp.concatenate([z_re * c - z_im * s, z_re * s + z_im * c], axis=1)
    top, rest = halves(y)
    return over_lanes(across[...], jnp.concatenate([top, rest, top], axis=1))


def kernel(chan, hour, x, taps, bin_ids, owners, *refs):
    tables, out = refs[:7], refs[7]
    held = refs[8:15]
    pick, high, turns, column, twist = held[:5]
    across, twice = held[5:]
    xin, tin, ids, ids_in, xd, td, fx, fh, spec, kron, part, first, early, outbox, inbox = refs[15:30]
    table_sem, own_sem, ids_send, ids_recv, t_send, t_recv, x_send, x_recv = refs[30:38]
    f_send, f_recv, send, recv, send2, recv2 = refs[38:]
    me, my_hour = lax.axis_index("chan"), lax.axis_index("hour")
    per = xin.shape[1]
    share = pl.ds(pl.multiple_of(my_hour * (tin.shape[2] // hour), LANES), tin.shape[2] // hour)

    def flipped(at, o, size):
        to, bit = at, 1
        while bit < size:
            to = to + lax.rem(lax.div(o, bit), 2) * bit * (1 - 2 * lax.rem(lax.div(at, bit), 2))
            bit *= 2
        return to

    def partner(o):
        return flipped(me, o, chan)

    def beside(o):
        return flipped(my_hour, o, hour)

    def sent(src, dst, sends, recvs, **device):
        return pltpu.make_async_remote_copy(
            src_ref=src, dst_ref=dst, send_sem=sends, recv_sem=recvs, device_id=device, device_id_type=MESH
        )

    loads = [pltpu.make_async_copy(src, dst, table_sem.at[z]) for z, (src, dst) in enumerate(zip(tables, held))]
    own = [
        pltpu.make_async_copy(x.at[me], xin.at[me], own_sem.at[0]),
        pltpu.make_async_copy(taps.at[me, :, share], tin.at[me, :, share], own_sem.at[1]),
    ]
    barrier = pltpu.get_barrier_semaphore()
    for o in reversed(range(1, chan)):
        pl.semaphore_signal(barrier, inc=1, device_id={"chan": partner(o)}, device_id_type=MESH)
    for o in range(1, hour):
        pl.semaphore_signal(
            barrier, inc=1, device_id={"hour": lax.rem(my_hour + o, hour)}, device_id_type=MESH
        )
    for copy in own + loads:
        copy.start()
    place = lax.broadcasted_iota(jnp.int32, ids.shape, 1)
    labels = jnp.zeros(ids.shape, jnp.int32)
    for r in range(ROUNDS):
        live = (place == me * ROUNDS + r) & (me >= r + 1)
        labels = jnp.where(live, bin_ids[:, r : r + 1] + 1, labels)
    ids[...] = labels
    pl.semaphore_wait(barrier, chan + hour - 2)

    def x_copy(o):
        to = partner(o)
        return sent(x.at[to], xin.at[me], x_send.at[o], x_recv.at[o], chan=to)

    far_first = sorted(range(1, chan), key=lambda o: -(o.bit_length()))
    tap_copies, id_copies = [], []
    for o in far_first:
        to = partner(o)
        tap_copies.append(
            sent(taps.at[to, :, share], tin.at[me, :, share], t_send.at[o], t_recv.at[o], chan=to)
        )
        tap_copies[-1].start()
    for o in far_first:
        id_copies.append(
            sent(ids.at[0:1], ids_in.at[o, 0:1], ids_send.at[o], ids_recv.at[o], chan=partner(o))
        )
        id_copies[-1].start()
    for o in range(1, chan):
        x_copy(o).start()
    lane0 = lax.broadcasted_iota(jnp.int32, (8, LANES), 1) == 0

    def bins_of(f, rows, t, edge):
        values, extra = [], []
        for n in range(SPLIT):
            re = f[n, rows, pl.ds(pl.multiple_of(2 * t * LANES, LANES), LANES)]
            im = f[n, rows, pl.ds(pl.multiple_of((2 * t + 1) * LANES, LANES), LANES)]
            if edge:
                angle = -math.pi * n / SPLIT
                extra.append((im * math.cos(angle), im * math.sin(angle)))
                im = jnp.where(lane0, 0.0, im)
            if n == 0:
                values.append((re, im))
            else:
                c, s = turns[t, n, 0], turns[t, n, 1]
                values.append((re * c - im * s, re * s + im * c))
        found = small_dft(values, -1)
        if edge:
            more = small_dft(extra, -1, half=True)
            for k2 in range(SPLIT // 2):
                old = found[SPLIT // 2 + k2]
                found[SPLIT // 2 + k2] = tuple(jnp.where(lane0, more[k2][z], old[z]) for z in range(2))
        return found

    def responses(t, edge):
        @pl.loop(0, chan * per // 8)
        def _(g):
            here = pl.ds(pl.multiple_of(8 * g, 8), 8)
            for k2, (hr, hi) in enumerate(bins_of(fh, here, t, edge)):
                spec[t, k2, 0, here, :] = hr
                spec[t, k2, 1, here, :] = hi

    def spectra(block, t, edge):
        for g in range(per // 8):
            here = pl.ds(pl.multiple_of(block * per + 8 * g, 8), 8)
            for k2, (xr, xi) in enumerate(bins_of(fx, slice(8 * g, 8 * g + 8), t, edge)):
                hr, hi = spec[t, k2, 0, here, :], spec[t, k2, 1, here, :]
                spec[t, k2, 0, here, :] = (xr * hr - xi * hi).astype(jnp.bfloat16).astype(jnp.float32)
                spec[t, k2, 1, here, :] = (xr * hi + xi * hr).astype(jnp.bfloat16).astype(jnp.float32)

    half = lax.broadcasted_iota(jnp.int32, (per, LANES), 1) < SHARE

    def transform_of(block):
        flat = jnp.concatenate([xin[block, :, q * PIECE : (q + 1) * PIECE] for q in range(FR // PIECE)], axis=0)
        got = jnp.dot(flat, pick[...], preferred_element_type=jnp.float32)
        for g in range(TILES):
            for n in range(SPLIT):
                a, b = (
                    got[q * per : (q + 1) * per, n // 2 * LANES : (n // 2 + 1) * LANES] for q in (2 * g, 2 * g + 1)
                )
                if n % 2:
                    a = pltpu.roll(a, SHARE, 1)
                else:
                    b = pltpu.roll(b, SHARE, 1)
                xd[n * per : (n + 1) * per, g * LANES : (g + 1) * LANES] = jnp.where(half, a, b).astype(jnp.bfloat16)
        found = jnp.dot(jnp.concatenate([xd[...], xd[...]], axis=1), high[...], preferred_element_type=jnp.float32)
        for n in range(SPLIT):
            fx[n] = found[n * per : (n + 1) * per]

    def spectra_of(block):
        spectra(block, 0, True)

        @pl.loop(1, TILES)
        def _(t):
            spectra(block, t, False)

    def take(block):
        transform_of(block)
        spectra_of(block)

    for copy in loads + own[:1]:
        copy.wait()
    transform_of(me)
    own[1].wait()
    for copy in tap_copies:
        copy.wait_recv()
    forwards = []
    for o in range(1, hour):
        to = lax.rem(my_hour + o, hour)
        forwards.append(sent(tin.at[:, :, share], tin.at[:, :, share], f_send.at[o], f_recv.at[o], hour=to))
        forwards[-1].start()
    for copy in id_copies:
        copy.wait_recv()
    labels = ids[0:1, :]
    for o in range(1, chan):
        labels = labels + ids_in[o, 0:1, :]
    by_pair = rows_of_pairs(labels, owners)
    nbins = chan * hour
    pair = lax.broadcasted_iota(jnp.int32, (ids.shape[1], SLOTS), 0)
    column_of = lax.broadcasted_iota(jnp.int32, (ids.shape[1], SLOTS), 1)
    places = jnp.zeros(pair.shape, jnp.float32)
    for s in range(1, chan):
        for j in range(s):
            near, far = jnp.maximum(partner(s), partner(j)), jnp.minimum(partner(s), partner(j))
            held_by = jnp.where(near - far <= ROUNDS, near * ROUNDS + near - far - 1, -1)
            hit = (column_of == slot_of(s, j, chan)) & (pair == held_by)
            places = jnp.where(hit, 1.0, places)
    by_slot = jnp.dot(by_pair, places.astype(jnp.bfloat16), preferred_element_type=jnp.float32).astype(jnp.bfloat16)
    deep = 2 * SPLIT
    spread = (
        lax.div(lax.broadcasted_iota(jnp.int32, (nbins * deep, nbins), 0), deep)
        == lax.broadcasted_iota(jnp.int32, (nbins * deep, nbins), 1)
    ).astype(jnp.float32).astype(jnp.bfloat16)
    widen = (
        lax.div(lax.broadcasted_iota(jnp.int32, (SLOTS, SLOTS * deep), 1), deep)
        == lax.broadcasted_iota(jnp.int32, (SLOTS, SLOTS * deep), 0)
    ).astype(jnp.float32).astype(jnp.bfloat16)
    tall = jnp.dot(spread, by_slot, preferred_element_type=jnp.float32).astype(jnp.bfloat16)
    both = jnp.dot(tall, widen, preferred_element_type=jnp.float32)
    same = lax.rem(lax.broadcasted_iota(jnp.int32, both.shape, 0), deep) == lax.rem(
        lax.broadcasted_iota(jnp.int32, both.shape, 1), deep
    )
    kron[...] = jnp.where(same, both, 0.0).astype(jnp.bfloat16)

    def cross(t, near, far, slot):
        res, ims = [], []
        for k2 in range(SPLIT):
            re = im = None
            for c in range(per // 8):
                at = pl.ds(pl.multiple_of(near * per + 8 * c, 8), 8)
                of = pl.ds(pl.multiple_of(far * per + 8 * c, 8), 8)
                nr, ni = spec[t, k2, 0, at, :], spec[t, k2, 1, at, :]
                fr, fi = spec[t, k2, 0, of, :], spec[t, k2, 1, of, :]
                one, two = fr * nr + fi * ni, fi * nr - fr * ni
                re, im = (one, two) if re is None else (re + one, im + two)
            res.append(re)
            ims.append(im)
        part[t, slot] = jnp.concatenate([fold(res), fold(ims)], axis=0).astype(jnp.bfloat16)

    def crosses(s, begin):
        @pl.loop(0, s)
        def _(j):
            a, b = partner(s), partner(j)
            for t in range(TILES):
                cross(t, jnp.maximum(a, b), jnp.minimum(a, b), begin + j)

    def part_copy(z, o, begin, count):
        where = pl.ds(begin, count)
        return sent(part.at[beside(o), where], first.at[o, where], send.at[z, o], recv.at[z, o], hour=beside(o))

    groups = [(LATE, 6), (LATE + 6, 4), (LATE + 10, 5), (LATE + 15, 6), (0, 7)]
    order = [2, 3, 1, 0]
    for copy in forwards:
        copy.wait_recv()
    count = tin.shape[2]
    got = jnp.dot(tin[...].reshape(chan * per, count), twice[...], preferred_element_type=jnp.float32)
    for n in range(SPLIT):
        td[n] = got[:, n * LANES : (n + 1) * LANES].astype(jnp.bfloat16)
    found = jnp.dot(
        td[...].reshape(SPLIT * chan * per, LANES),
        jnp.concatenate([high[:SHARE, :], high[SUB : SUB + SHARE, :]], axis=0),
        preferred_element_type=jnp.float32,
    )
    for n in range(SPLIT):
        fh[n] = found[n * chan * per : (n + 1) * chan * per]
    responses(0, True)

    @pl.loop(1, TILES)
    def _(t):
        responses(t, False)

    spectra_of(me)

    @pl.loop(1, chan // 2)
    def _(s):
        x_copy(s).wait_recv()
        take(partner(s))
        crosses(s, LATE + lax.div(s * (s - 1), 2))

    for o in order[:3]:
        part_copy(0, o, *groups[0]).start()

    @pl.loop(chan // 2, chan - 1)
    def _(s):
        x_copy(s).wait_recv()
        take(partner(s))
        crosses(s, LATE + lax.div(s * (s - 1), 2))

        for z in range(1, len(groups) - 1):

            @pl.when(s == z + 3)
            def _():
                for o in order[:3]:
                    part_copy(z, o, *groups[z]).start()

    x_copy(chan - 1).wait_recv()
    block = partner(chan - 1)
    transform_of(block)

    @pl.loop(0, TILES)
    def _(z):
        late = lax.div(z, 2)
        o = (1 - late) * (2 + z) + late * (3 - z)
        t = beside(o)

        @pl.when(t == 0)
        def _():
            spectra(block, 0, True)

        @pl.when(t > 0)
        def _():
            spectra(block, t, False)

        for j in range(chan - 1):
            cross(t, jnp.maximum(block, partner(j)), jnp.minimum(block, partner(j)), j)

        @pl.when(o > 0)
        def _():
            part_copy(4, o, *groups[4]).start()

    def summed(begin, count, room):
        where = slice(begin, begin + count)
        total = part[my_hour, where].astype(jnp.float32)
        for o in range(1, hour):
            total = total + first[o, where].astype(jnp.float32)
        total = total.reshape(count * deep, LANES)
        if room > count:
            total = jnp.concatenate([total, jnp.zeros(((room - count) * deep, LANES), jnp.float32)], axis=0)
        return jnp.concatenate(halves(total), axis=1)

    def mixed(rows, begin, room, values):
        got = jnp.dot(
            kron[rows, begin * deep : (begin + room) * deep], values, preferred_element_type=jnp.float32
        )
        return got[:, :LANES] + got[:, LANES:]

    for z in range(len(groups) - 1):
        for o in range(1, hour):
            part_copy(z, o, *groups[z]).wait_recv()
    early[...] = mixed(slice(None), LATE, SLOTS - LATE, summed(LATE, 21, SLOTS - LATE))
    for o in range(1, hour):
        part_copy(4, o, *groups[4]).wait_recv()
    late = summed(0, 7, LATE)
    side = nbins // 2
    for z in range(2):
        half_of = 1 - lax.div(me, chan // 2) if z == 0 else lax.div(me, chan // 2)
        deep_rows = pl.ds(pl.multiple_of(half_of * side * deep, side * deep), side * deep)
        outbox[pl.ds(half_of * side, side)] = (
            (mixed(deep_rows, 0, LATE, late) + early[deep_rows, :]).astype(jnp.bfloat16).reshape(side, deep, LANES)
        )
        for oc in (5, 4, 7, 6) if z == 0 else (3, 2, 1, 0):
            for o in (0, 1, 2, 3):
                if oc or o:
                    to, at = partner(oc), beside(o)
                    sent(
                        outbox.at[to * hour + at],
                        inbox.at[oc * hour + my_hour],
                        send2.at[0],
                        recv2.at[0],
                        chan=to,
                        hour=at,
                    ).start()
    inbox[my_hour] = outbox[me * hour + my_hour]
    for copy in tap_copies + id_copies + forwards:
        copy.wait_send()
    for o in range(1, chan):
        x_copy(o).wait_send()
    for z in range(len(groups)):
        for o in range(1, hour):
            part_copy(z, o, *groups[z]).wait_send()

    others = pl.ds(0, chan * hour - 1)
    all_rows = sent(outbox.at[others], inbox.at[others], send2.at[0], recv2.at[0], chan=partner(1))
    all_rows.wait_recv()
    rows = inbox[0:hour].astype(jnp.float32)
    for oc in range(1, chan):
        rows = rows + inbox[oc * hour : (oc + 1) * hour].astype(jnp.float32)
    wave = inverse(rows.reshape(TILES * deep, LANES), column, twist, across)
    out[...] = wave
    all_rows.wait_send()


def split_body(traces, taps, bin_ids, owners):
    chan, hour = lax.axis_size("chan"), lax.axis_size("hour")
    channels, count = taps.shape
    per = channels // chan
    norm = 1.0 / (FR * math.sqrt(FR * hour * channels))
    high, low = two_parts(sub_tables())
    pick, twice = pick_tables()
    tables = [pick, np.concatenate([high, low], axis=0), turn_table(), column_table(), twist_table(), row_table(), twice]
    depth = LANES
    part = (hour, SLOTS, 2 * SPLIT, LANES)
    rows = (chan * hour, 2 * SPLIT, LANES)
    vmem, hbm = pl.BlockSpec(memory_space=pltpu.VMEM), pl.BlockSpec(memory_space=pl.ANY)
    sems = pltpu.SemaphoreType.DMA
    wave = pl.pallas_call(
        functools.partial(kernel, chan, hour),
        out_shape=pltpu.VMEM((OUT_ROWS, LANES), jnp.float32),
        in_specs=[hbm, hbm, vmem, vmem] + [hbm] * len(tables),
        out_specs=vmem,
        scratch_shapes=[pltpu.VMEM(table.shape, table.dtype) for table in tables]
        + [
            pltpu.VMEM((chan, per, FR), jnp.bfloat16),
            pltpu.VMEM((chan, per, count), jnp.bfloat16),
            pltpu.VMEM((8, depth), jnp.int32),
            pltpu.VMEM((chan, 8, depth), jnp.int32),
            pltpu.VMEM((SPLIT * per, SUB), jnp.bfloat16),
            pltpu.VMEM((SPLIT, channels, LANES), jnp.bfloat16),
            pltpu.VMEM((SPLIT, per, 2 * SUB), jnp.float32),
            pltpu.VMEM((SPLIT, channels, 2 * SUB), jnp.float32),
            pltpu.VMEM((TILES, SPLIT, 2, channels, LANES), jnp.float32),
            pltpu.VMEM((rows[0] * rows[1], SLOTS * rows[1]), jnp.bfloat16),
            pltpu.VMEM(part, jnp.bfloat16),
            pltpu.VMEM(part, jnp.bfloat16),
            pltpu.VMEM((rows[0] * rows[1], LANES), jnp.float32),
            pltpu.VMEM(rows, jnp.bfloat16),
            pltpu.VMEM(rows, jnp.bfloat16),
            sems((len(tables),)),
            sems((2,)),
        ]
        + [sems((chan,))] * 6
        + [sems((hour,))] * 2
        + [sems((5, hour))] * 2
        + [sems((1,))] * 2,
        compiler_params=pltpu.CompilerParams(
            collective_id=0, has_side_effects=True, vmem_limit_bytes=56 * 2**20
        ),
    )(
        traces.reshape(chan, per, FR),
        taps.reshape(chan, per, count),
        bin_ids.T,
        owners.reshape(1, -1),
        *[jnp.asarray(table) for table in tables],
    )
    return (wave * norm).reshape(1, 2 * FR)


def solution(mesh):
    placed = (P("chan", "hour"), P("chan", None), P(None, "chan"), P())

    def whole(traces, taps, bin_ids, owners):
        chan, hour = mesh.shape["chan"], mesh.shape["hour"]
        channels = traces.shape[0] // chan
        fits = (
            chan == 8
            and hour == TILES
            and channels % (16 * chan) == 0
            and traces.shape[1] == hour * FR
            and taps.shape[1] == SPLIT * LANES // 2
            and owners.shape[0] == chan * hour
        )
        return jax.shard_map(
            split_body if fits else body,
            mesh=mesh,
            in_specs=placed,
            out_specs=P(("chan", "hour"), None),
            check_vma=False,
        )(traces, taps, bin_ids, owners)

    return whole
```
